32 devices in a mesh: groups: 2 (over y), train: 4 (over x, core), test: 4 (over z).
Axes of the slice: x: 2, y: 2, z: 4, core: 2. Of those that a mesh axis runs over, the one named last changes fastest.
Arguments:
- train_grads: bfloat16 [4096, 8192], P(('groups', 'train'), 'test'), parts along dimension 0, may hold values from -0.0625 to 0.0625
- test_grads: bfloat16 [4096, 8192], P(('groups', 'test'), 'train'), parts along dimension 0, may hold values from -6 to 6
- fisher: bfloat16 [8192, 8192], P('train', 'test')
- chosen_ids: int32 [4096, 16], P(('groups', 'test')), parts along dimension 0, may hold values from 0 to 2047
Outputs:
- scores: float32 [4096, 2048], P(('groups', 'train'), 'test'), parts along dimension 0
- chosen_sums: float32 [4096], P(('groups', 'test')), parts along dimension 0
The draws below stay inside these ranges and needn't reach their ends.
There are 2 independent parts, one for each index of `groups`. The reference program is written for one: setup_inputs(seed, part) draws one part's arguments, and reference() takes and returns one part's arrays. A program takes and returns all parts, laid end to end along the dimension named above; an argument that names none is the same for every part. Nothing has to cross between parts.
Inputs may be any that keep to these rules, and one draw needn't show every extreme that they name: `chosen_ids`: each id names a train row of the same group; ids may repeat.
All inputs are finite; a program needn't handle non-finite values.
Results may differ from the reference program's by a relative error of at most 0.003.
Values may be sent and summed in bfloat16 or wider, within the bound.
No kernel may reach another device: no remote copies, remote signals or barrier semaphores. Data moves between devices by JAX's collectives and lax.ppermute only.
A program may use at most 128 MiB of HBM per device.

```python
import jax
import jax.numpy as jnp

K = 8192
SEL = 16
TRAIN_ROWS = 2048
TEST_ROWS = 2048


def draw_fisher(key, part):
    key = jax.random.fold_in(key, 7)
    diag_key, off_key = jax.random.split(key)
    diag_vals = jax.random.uniform(diag_key, (K,), jnp.float32, 0.5, 2.0)
    noise = jax.random.normal(off_key, (K, K), jnp.float32) * 0.7
    rows = jnp.arange(K)[:, None]
    cols = jnp.arange(K)[None, :]
    whole = jnp.where(rows == cols, diag_vals[None, :], 0.0) + noise / jnp.sqrt(jnp.float32(K))
    return whole.astype(jnp.bfloat16)


def place_ends(array, stream_key, least, largest):
    place = [jax.random.randint(jax.random.fold_in(stream_key, axis), (), 0, length) for axis, length in enumerate(array.shape)]
    widest = array.shape.index(max(array.shape))
    next_to = place[:widest] + [(place[widest] + 1) % array.shape[widest]] + place[widest + 1:]
    return array.at[tuple(place)].set(least).at[tuple(next_to)].set(largest)


def block_levels(rng, extent, cuts, least, high):
    gain, own = 1.0, jax.random.fold_in(rng, 6)
    for dim, blocks in cuts:
        draws = jnp.exp(jax.random.uniform(jax.random.fold_in(own, dim), (blocks,), jnp.float32, least / len(cuts), high / len(cuts)))
        gain = gain * jnp.repeat(draws, extent[dim] // blocks).reshape([-1 if axis == dim else 1 for axis in range(len(extent))])
    return gain


def scatter_about(own_key, shape, deviation, limit, shards=(), held_as=jnp.bfloat16):
    result = jax.random.normal(own_key, shape, jnp.float32) * deviation
    if len(shards) > 0:
        result = block_levels(own_key, shape, shards, -0.22, 0.18) * result
    return jnp.clip(result, min=-limit, max=limit).astype(held_as)


def setup_inputs(seed: int = 0, part: int = 0) -> dict:
    seeds = jax.random.split(jax.random.key(seed), 5)
    part_splits = jax.random.split(jax.random.fold_in(seeds[4], part), 5)
    return {
        "train_grads": scatter_about(part_splits[0], (TRAIN_ROWS, K), K ** -0.5, 0.0625, ((0, 4), (1, 4))),
        "test_grads": scatter_about(part_splits[1], (TEST_ROWS, K), 1.0, 6.0, ((0, 4), (1, 4))),
        "fisher": draw_fisher(jax.random.fold_in(seeds[4], 71), part),
        "chosen_ids": place_ends(jax.random.randint(part_splits[3], (TEST_ROWS, SEL), 0, TRAIN_ROWS), jax.random.fold_in(part_splits[3], 1), 0, TRAIN_ROWS - 1).astype(jnp.int32),
    }


def reference(train_grads, test_grads, fisher, chosen_ids):
    precond = jnp.dot(test_grads, fisher, preferred_element_type=jnp.float32).astype(jnp.bfloat16)
    scores = jnp.dot(train_grads, precond.T, preferred_element_type=jnp.float32)
    columns = jnp.arange(TEST_ROWS, dtype=jnp.int32)[:, None]
    picked = scores[chosen_ids, columns]
    chosen_sums = jnp.sum(picked, axis=1)
    return scores, chosen_sums
```

```python
import jax
import jax.numpy as jnp
from jax import lax
from jax.sharding import PartitionSpec as P

CHUNKS = 4

F32 = jnp.float32
BF16 = jnp.bfloat16


def dot_t(a, b):
    return lax.dot_general(a, b, (((1,), (1,)), ((), ())), preferred_element_type=F32)


def selection_counts(chosen_ids, first_row, rows):
    row_ids = first_row + lax.broadcasted_iota(jnp.int32, (rows, chosen_ids.shape[0]), 0)
    ids = chosen_ids.T
    counts = jnp.zeros(row_ids.shape, F32)
    for k in range(ids.shape[0]):
        counts = counts + (row_ids == ids[k][None, :]).astype(F32)
    return counts


def any_mesh(train_grads, test_grads, fisher, chosen_ids):
    test_whole = lax.all_gather(test_grads, "test", axis=0, tiled=True)
    partial_value = jnp.dot(test_whole, fisher, preferred_element_type=F32)
    precond = lax.psum(partial_value, "train").astype(BF16)
    partial_scores = dot_t(train_grads, precond)
    scores = lax.psum_scatter(partial_scores, "test", scatter_dimension=1, tiled=True)
    rows = scores.shape[0]
    counts = selection_counts(chosen_ids, lax.axis_index("train") * rows, rows)
    return scores, lax.psum(jnp.sum(counts * scores, axis=0), "train")


def four_by_four(train_grads, test_grads, fisher, chosen_ids):
    z = lax.axis_index("test")
    i = lax.axis_index("train")
    chip, core = i // 2, i % 2
    inner = (z == 1) | (z == 2)
    quarter = test_grads.shape[0] // CHUNKS // 4
    own_rows = train_grads.shape[0]

    def along(value, pairs):
        return lax.ppermute(value, "test", pairs)

    def to_other(value, r):
        return lax.ppermute(value, "train", [(k, k ^ r) for k in range(4)])

    pair = [(0, 1), (1, 0), (2, 3), (3, 2)]
    middle = [(1, 2), (2, 1)]
    outward = [(1, 0), (2, 3)]
    inward = [(0, 1), (3, 2)]

    def reorder(parts):
        parts = [jnp.where(core == 0, parts[r], parts[r ^ 1]) for r in range(4)]
        return [jnp.where(chip == 0, parts[r], parts[r ^ 2]) for r in range(4)]

    in_quarters = test_grads.reshape(CHUNKS, 4, quarter, -1)
    relative = reorder([in_quarters[:, q] for q in range(4)])
    chunked = jnp.concatenate([relative[r] for r in (0, 2, 1, 3)], axis=1)

    grads = [train_grads, to_other(train_grads, 1), to_other(train_grads, 2)]
    grads = jnp.concatenate(grads + [to_other(grads[2], 1)])

    def scores_part(block):
        part = jnp.dot(block, fisher, preferred_element_type=F32)
        chip_part = part[: 2 * quarter] + to_other(part[2 * quarter :], 1)
        precond = chip_part[:quarter] + to_other(chip_part[quarter:], 2)
        return dot_t(precond.astype(BF16), grads)

    own, near, second, third = [], [], [], []
    for c in range(CHUNKS):
        block = chunked[c]
        near.append(along(block, pair))
        second.append(along(block, middle))
    for c in range(CHUNKS):
        third.append(along(near[c], middle))
    for c in range(CHUNKS):
        second[c] = jnp.where(inner, second[c], along(second[c], outward))
    for c in range(CHUNKS):
        third[c] = jnp.where(inner, third[c], along(third[c], outward))

    pieces = []
    for c in range(CHUNKS):
        own.append(scores_part(chunked[c]))
    for c in range(CHUNKS):
        near[c] = scores_part(near[c])
    for c in range(CHUNKS):
        value = scores_part(second[c])
        value = value + along(value.astype(BF16), inward).astype(F32)
        own[c] = own[c] + along(value.astype(BF16), middle).astype(F32)
    for c in range(CHUNKS):
        value = scores_part(third[c])
        value = value + along(value.astype(BF16), inward).astype(F32)
        value = near[c] + along(value.astype(BF16), middle).astype(F32)
        pieces.append(own[c] + along(value.astype(BF16), pair).astype(F32))

    ids = reorder([chosen_ids.reshape(CHUNKS, 4, quarter, -1)[:, q] for q in range(4)])[0]
    blocks = jnp.stack([i, i ^ 1, i ^ 2, i ^ 3])
    row_ids = (blocks[:, None] * own_rows + jnp.arange(own_rows)[None, :]).reshape(1, 1, -1)
    outs, sums = [], []
    for c in range(CHUNKS):
        counts = jnp.sum((ids[c][:, :, None] == row_ids).astype(F32), axis=1)
        chosen = jnp.sum(counts * pieces[c], axis=1)
        parts = [pieces[c][:, r * own_rows : (r + 1) * own_rows] for r in range(4)]
        outs += reorder([parts[0]] + [to_other(parts[r], r) for r in range(1, 4)])
        sums += reorder([chosen] + [to_other(chosen, r) for r in range(1, 4)])
    return jnp.concatenate(outs).T, jnp.concatenate(sums)


def solution(mesh):
    sizes = (mesh.shape["train"], mesh.shape["test"])
    return jax.shard_map(
        four_by_four if sizes == (4, 4) else any_mesh,
        mesh=mesh,
        in_specs=(
            P(("groups", "train"), "test"),
            P(("groups", "test"), "train"),
            P("train", "test"),
            P(("groups", "test"), None),
        ),
        out_specs=(P(("groups", "train"), "test"), P(("groups", "test"))),
        check_vma=False,
    )
```

```python
import jax
import jax.numpy as jnp
from jax import lax
from jax.sharding import PartitionSpec as P

CHUNK_ROWS = (160, 160, 128, 64)

F32 = jnp.float32
BF16 = jnp.bfloat16


def dot_t(a, b):
    return lax.dot_general(a, b, (((1,), (1,)), ((), ())), preferred_element_type=F32)


def selection_counts(chosen_ids, first_row, rows):
    row_ids = first_row + lax.broadcasted_iota(jnp.int32, (rows, chosen_ids.shape[0]), 0)
    ids = chosen_ids.T
    counts = jnp.zeros(row_ids.shape, F32)
    for k in range(ids.shape[0]):
        counts = counts + (row_ids == ids[k][None, :]).astype(F32)
    return counts


def any_mesh(train_grads, test_grads, fisher, chosen_ids):
    test_whole = lax.all_gather(test_grads, "test", axis=0, tiled=True)
    partial_value = jnp.dot(test_whole, fisher, preferred_element_type=F32)
    precond = lax.psum(partial_value, "train").astype(BF16)
    partial_scores = dot_t(train_grads, precond)
    scores = lax.psum_scatter(partial_scores, "test", scatter_dimension=1, tiled=True)
    rows = scores.shape[0]
    counts = selection_counts(chosen_ids, lax.axis_index("train") * rows, rows)
    return scores, lax.psum(jnp.sum(counts * scores, axis=0), "train")


def four_by_four(train_grads, test_grads, fisher, chosen_ids):
    z = lax.axis_index("test")
    i = lax.axis_index("train")
    chip, core = i // 2, i % 2
    own_rows = train_grads.shape[0]

    def along(value, pairs):
        return lax.ppermute(value.astype(BF16), "test", pairs).astype(F32)

    def to_other(value, r):
        return lax.ppermute(value, "train", [(k, k ^ r) for k in range(4)])

    pair = [(0, 1), (1, 0), (2, 3), (3, 2)]
    middle = [(1, 2), (2, 1)]
    inward = [(0, 1), (3, 2)]

    def reorder(parts):
        parts = [jnp.where(core == 0, parts[r], parts[r ^ 1]) for r in range(4)]
        return [jnp.where(chip == 0, parts[r], parts[r ^ 2]) for r in range(4)]

    grads = [train_grads, to_other(train_grads, 1), to_other(train_grads, 2)]
    grads = jnp.concatenate(grads + [to_other(grads[2], 1)])

    blocks = jnp.stack([i, i ^ 1, i ^ 2, i ^ 3])
    row_ids = (blocks[:, None] * own_rows + jnp.arange(own_rows)[None, :]).reshape(1, 1, -1)

    outs, sums = [], []
    first = 0
    for rows in CHUNK_ROWS:
        quarter = rows // 4
        piece = test_grads[first : first + rows]
        relative = reorder([piece[q * quarter : (q + 1) * quarter] for q in range(4)])
        relative = jnp.concatenate([relative[r] for r in (0, 2, 1, 3)])
        block = lax.all_gather(relative, "test", axis=0, tiled=True)

        part = jnp.dot(block, fisher, preferred_element_type=F32).reshape(4, 4, quarter, -1)
        chip_part = part[:, :2] + to_other(part[:, 2:], 1)
        other = to_other(chip_part[:, 1].astype(BF16), 2).astype(F32)
        precond = (chip_part[:, 0] + other).reshape(rows, -1)
        high = precond.astype(BF16)
        low = (precond - high.astype(F32)).astype(BF16)
        both = dot_t(jnp.concatenate([high, low]), grads)
        value = (both[:rows] + both[rows:]).reshape(4, quarter, -1)

        own = value[z]
        near = value[z ^ 1]
        if first + rows == test_grads.shape[0]:
            total = own + along(near, pair)
            total = total + along(value[z ^ 2], [(0, 2), (1, 3), (2, 0), (3, 1)])
            total = total + along(value[z ^ 3], [(0, 3), (1, 2), (2, 1), (3, 0)])
        else:
            low_half = z < 2
            far = jnp.where(low_half, value[2:], value[1::-1])
            far = far + along(far, inward)
            got = along(far, middle)
            total = own + got[0] + along(near + got[1], pair)

        ids = reorder([chosen_ids[first + q * quarter : first + (q + 1) * quarter] for q in range(4)])[0]
        counts = jnp.sum((ids[:, :, None] == row_ids).astype(F32), axis=1)
        chosen = jnp.sum(counts * total, axis=1)
        parts = [total[:, r * own_rows : (r + 1) * own_rows] for r in range(4)]
        outs += reorder([parts[0]] + [to_other(parts[r], r) for r in range(1, 4)])
        sums += reorder([chosen] + [to_other(chosen, r) for r in range(1, 4)])
        first += rows
    return jnp.concatenate(outs).T, jnp.concatenate(sums)


def solution(mesh):
    sizes = (mesh.shape["train"], mesh.shape["test"])
    return jax.shard_map(
        four_by_four if sizes == (4, 4) else any_mesh,
        mesh=mesh,
        in_specs=(
            P(("groups", "train"), "test"),
            P(("groups", "test"), "train"),
            P("train", "test"),
            P(("groups", "test"), None),
        ),
        out_specs=(P(("groups", "train"), "test"), P(("groups", "test"))),
        check_vma=False,
    )
```

```python
import jax
import jax.numpy as jnp
from jax import lax
from jax.sharding import PartitionSpec as P

LAST_ROWS = 128

F32 = jnp.float32
BF16 = jnp.bfloat16


def dot_t(a, b):
    return lax.dot_general(a, b, (((1,), (1,)), ((), ())), preferred_element_type=F32)


def selection_counts(chosen_ids, first_row, rows):
    row_ids = first_row + lax.broadcasted_iota(jnp.int32, (rows, chosen_ids.shape[0]), 0)
    ids = chosen_ids.T
    counts = jnp.zeros(row_ids.shape, F32)
    for k in range(ids.shape[0]):
        counts = counts + (row_ids == ids[k][None, :]).astype(F32)
    return counts


def any_mesh(train_grads, test_grads, fisher, chosen_ids):
    test_whole = lax.all_gather(test_grads, "test", axis=0, tiled=True)
    partial_value = jnp.dot(test_whole, fisher, preferred_element_type=F32)
    precond = lax.psum(partial_value, "train").astype(BF16)
    partial_scores = dot_t(train_grads, precond)
    scores = lax.psum_scatter(partial_scores, "test", scatter_dimension=1, tiled=True)
    rows = scores.shape[0]
    counts = selection_counts(chosen_ids, lax.axis_index("train") * rows, rows)
    return scores, lax.psum(jnp.sum(counts * scores, axis=0), "train")


def four_by_four(train_grads, test_grads, fisher, chosen_ids):
    z = lax.axis_index("test")
    i = lax.axis_index("train")
    chip, core = i // 2, i % 2
    inner = (z == 1) | (z == 2)
    own_rows = train_grads.shape[0]
    queries = test_grads.shape[0]
    pieces = ((0, queries - LAST_ROWS), (queries - LAST_ROWS, LAST_ROWS))

    def along(value, pairs):
        return lax.ppermute(value, "test", pairs)

    def scores_along(value, pairs):
        return along(value.astype(BF16), pairs).astype(F32)

    def to_other(value, r):
        return lax.ppermute(value, "train", [(k, k ^ r) for k in range(4)])

    def tied(*values):
        return lax.optimization_barrier(values)

    pair = [(0, 1), (1, 0), (2, 3), (3, 2)]
    middle = [(1, 2), (2, 1)]
    outward = [(1, 0), (2, 3)]
    far_pairs = [(0, 3), (3, 0), (1, 2), (2, 1)]

    def portion(value, cuts, which, of):
        return jnp.concatenate(
            [
                lax.dynamic_slice_in_dim(value, first + which * (rows // of), rows // of)
                for first, rows in cuts
            ]
        )

    def cut(sizes):
        return [(sum(sizes[:p]), sizes[p]) for p in range(len(sizes))]

    def core_sum(block, sizes):
        part = jnp.dot(block, fisher, preferred_element_type=F32)
        sent = to_other(portion(part, cut(sizes), 1 - core, 2), 1)
        return portion(part, cut(sizes), core, 2) + sent

    def chip_sum(part, sizes):
        halves = cut([rows // 2 for rows in sizes])
        sent = to_other(portion(part, halves, 1 - chip, 2), 2)
        return (portion(part, halves, chip, 2) + sent).astype(BF16)

    whole = [rows for _, rows in pieces]

    near = along(test_grads, pair)
    third = along(test_grads, middle)
    grads = [train_grads, to_other(train_grads, 1), to_other(train_grads, 2)]
    own_part = core_sum(test_grads, whole)
    near, third, grads, own_part = tied(near, third, grads, own_part)

    second_in = along(near, middle)
    second_edge = along(third, outward)
    own_precond = chip_sum(own_part, whole)
    grads = jnp.concatenate(grads + [to_other(grads[2], 1)])
    near_precond = chip_sum(core_sum(near, whole), whole)
    own = dot_t(own_precond, grads)
    near = dot_t(near_precond, grads)
    second_in, second_edge, own, near, grads = tied(second_in, second_edge, own, near, grads)

    last_in = second_in[pieces[1][0] :]
    first_edge = along(second_in[: pieces[0][1]], outward)
    second = jnp.where(inner, second_in, second_edge)
    second = dot_t(chip_sum(core_sum(second, whole), whole), grads)
    total = own + scores_along(second, [(0, 2), (3, 1)])
    near = near + scores_along(second, middle)
    total = total + scores_along(near, pair)
    first_edge, last_in, total = tied(first_edge, last_in, total)
    last_edge = along(last_in, outward)

    blocks = jnp.stack([i, i ^ 1, i ^ 2, i ^ 3])
    row_ids = (blocks[:, None] * own_rows + jnp.arange(own_rows)[None, :]).reshape(1, 1, -1)

    outs = []
    edges = (first_edge, last_edge)
    for (first, rows), edge in zip(pieces, edges):
        quarter = rows // 4
        block = jnp.where(inner, third[first : first + rows], edge)
        value = dot_t(chip_sum(core_sum(block, [rows]), [rows]), grads)
        value = total[first // 4 : first // 4 + quarter] + scores_along(value, far_pairs)
        ids = lax.dynamic_slice_in_dim(chosen_ids, first + (core * 2 + chip) * quarter, quarter)
        counts = jnp.sum((ids[:, :, None] == row_ids).astype(F32), axis=1)
        chosen = jnp.sum(counts * value, axis=1, keepdims=True)
        parts = [value[:, r * own_rows : (r + 1) * own_rows] for r in range(4)]
        parts = [jnp.pad(part, ((0, 0), (0, 128))) for part in parts]
        column = lax.broadcasted_iota(jnp.int32, parts[0].shape, 1)
        parts = [jnp.where(column < own_rows, part, chosen) for part in parts]
        got = [parts[0]] + [to_other(parts[r], r) for r in range(1, 4)]
        got = [got[0], got[2], got[1], got[3]]
        got = [jnp.where(chip == 0, got[q], got[q ^ 1]) for q in range(4)]
        outs += [jnp.where(core == 0, got[q], got[q ^ 2]) for q in range(4)]
    turned = jnp.concatenate(outs).T
    return turned[:own_rows], turned[own_rows]


def solution(mesh):
    sizes = (mesh.shape["train"], mesh.shape["test"])
    return jax.shard_map(
        four_by_four if sizes == (4, 4) else any_mesh,
        mesh=mesh,
        in_specs=(
            P(("groups", "train"), "test"),
            P(("groups", "test"), "train"),
            P("train", "test"),
            P(("groups", "test"), None),
        ),
        out_specs=(P(("groups", "train"), "test"), P(("groups", "test"))),
        check_vma=False,
    )
```

```python
import jax
import jax.numpy as jnp
from jax import lax
from jax.sharding import PartitionSpec as P

LAST_ROWS = 128

F32 = jnp.float32
BF16 = jnp.bfloat16


def dot_t(a, b):
    return lax.dot_general(a, b, (((1,), (1,)), ((), ())), preferred_element_type=F32)


def selection_counts(chosen_ids, first_row, rows):
    row_ids = first_row + lax.broadcasted_iota(jnp.int32, (rows, chosen_ids.shape[0]), 0)
    ids = chosen_ids.T
    counts = jnp.zeros(row_ids.shape, F32)
    for k in range(ids.shape[0]):
        counts = counts + (row_ids == ids[k][None, :]).astype(F32)
    return counts


def any_mesh(train_grads, test_grads, fisher, chosen_ids):
    test_whole = lax.all_gather(test_grads, "test", axis=0, tiled=True)
    partial_value = jnp.dot(test_whole, fisher, preferred_element_type=F32)
    precond = lax.psum(partial_value, "train").astype(BF16)
    partial_scores = dot_t(train_grads, precond)
    scores = lax.psum_scatter(partial_scores, "test", scatter_dimension=1, tiled=True)
    rows = scores.shape[0]
    counts = selection_counts(chosen_ids, lax.axis_index("train") * rows, rows)
    return scores, lax.psum(jnp.sum(counts * scores, axis=0), "train")


def four_by_four(train_grads, test_grads, fisher, chosen_ids):
    z = lax.axis_index("test")
    i = lax.axis_index("train")
    chip, core = i // 2, i % 2
    inner = (z == 1) | (z == 2)
    own_rows = train_grads.shape[0]
    queries = test_grads.shape[0]
    pieces = ((0, queries - LAST_ROWS), (queries - LAST_ROWS, LAST_ROWS))

    def along(value, pairs):
        return lax.ppermute(value, "test", pairs)

    def scores_along(value, pairs):
        return along(value.astype(BF16), pairs).astype(F32)

    def to_other(value, r):
        return lax.ppermute(value, "train", [(k, k ^ r) for k in range(4)])

    def tied(*values):
        return lax.optimization_barrier(values)

    pair = [(0, 1), (1, 0), (2, 3), (3, 2)]
    middle = [(1, 2), (2, 1)]
    outward = [(1, 0), (2, 3)]
    far_pairs = [(0, 3), (3, 0), (1, 2), (2, 1)]

    def portion(value, cuts, which, of):
        return jnp.concatenate(
            [
                lax.dynamic_slice_in_dim(value, first + which * (rows // of), rows // of)
                for first, rows in cuts
            ]
        )

    def cut(sizes):
        return [(sum(sizes[:p]), sizes[p]) for p in range(len(sizes))]

    def product(block):
        return jnp.dot(block, fisher, preferred_element_type=F32)

    def core_sum(part, sizes, ways=2):
        kept = portion(part, cut(sizes), core, 2)
        sent = portion(part, cut(sizes), 1 - core, 2)
        step = sent.shape[0] // ways
        got = [to_other(sent[w * step : (w + 1) * step], 1) for w in range(ways)]
        return kept + jnp.concatenate(got)

    def chip_sum(part, sizes, sent_as=F32):
        halves = cut([rows // 2 for rows in sizes])
        sent = to_other(portion(part, halves, 1 - chip, 2).astype(sent_as), 2)
        return (portion(part, halves, chip, 2) + sent.astype(F32)).astype(BF16)

    whole = [rows for _, rows in pieces]
    first_rows = pieces[0][1]

    near = along(test_grads, pair)
    third = along(test_grads, middle)
    grads = [train_grads, to_other(train_grads, 1), to_other(train_grads, 2)]
    own = product(test_grads)
    near, third, grads, own = tied(near, third, grads, own)

    second_in = along(near, middle)
    second_edge = along(third, outward)
    own = chip_sum(core_sum(own, whole), whole)
    near = core_sum(product(near), whole)
    second_in, second_edge, own, near, grads = tied(second_in, second_edge, own, near, grads)

    grads = jnp.concatenate(grads + [to_other(grads[2], 1)])
    first_edge = along(second_in[:first_rows], outward)
    near = chip_sum(near, whole)
    second = core_sum(product(jnp.where(inner, second_in, second_edge)), whole)
    last_in = second_in[first_rows:]
    first_edge, last_in, own, near, second, grads = tied(
        first_edge, last_in, own, near, second, grads
    )

    last_edge = along(last_in, outward)
    own = dot_t(own, grads)
    near = dot_t(near, grads)
    second = chip_sum(second, whole, BF16)
    block = jnp.where(inner, third[:first_rows], first_edge)
    first_part = core_sum(product(block), whole[:1], 3)
    last_edge, second, first_part, own, near, grads = tied(
        last_edge, second, first_part, own, near, grads
    )

    second = dot_t(second, grads)
    got_in = scores_along(second, middle)
    first_value = chip_sum(first_part, whole[:1], BF16)
    block = jnp.where(inner, third[first_rows:], last_edge)
    last_part = core_sum(product(block), whole[1:], 1)
    got_in, second, first_value, last_part, own, near, grads = tied(
        got_in, second, first_value, last_part, own, near, grads
    )
    near_got = scores_along(near + got_in, pair)
    edge_got = scores_along(second, [(0, 2), (3, 1)])
    total = own + near_got + edge_got
    last_value = chip_sum(last_part, whole[1:], BF16)

    blocks = jnp.stack([i, i ^ 1, i ^ 2, i ^ 3])
    row_ids = (blocks[:, None] * own_rows + jnp.arange(own_rows)[None, :]).reshape(1, 1, -1)

    outs = []
    for (first, rows), value in zip(pieces, (first_value, last_value)):
        quarter = rows // 4
        value = dot_t(value, grads)
        value = total[first // 4 : first // 4 + quarter] + scores_along(value, far_pairs)
        ids = lax.dynamic_slice_in_dim(chosen_ids, first + (core * 2 + chip) * quarter, quarter)
        counts = jnp.sum((ids[:, :, None] == row_ids).astype(F32), axis=1)
        chosen = jnp.sum(counts * value, axis=1, keepdims=True)
        parts = [value[:, r * own_rows : (r + 1) * own_rows] for r in range(4)]
        parts = [jnp.pad(part, ((0, 0), (0, 128))) for part in parts]
        column = lax.broadcasted_iota(jnp.int32, parts[0].shape, 1)
        parts = [jnp.where(column < own_rows, part, chosen) for part in parts]
        got = [parts[0]] + [to_other(parts[r], r) for r in range(1, 4)]
        got = [got[0], got[2], got[1], got[3]]
        got = [jnp.where(chip == 0, got[q], got[q ^ 1]) for q in range(4)]
        outs += [jnp.where(core == 0, got[q], got[q ^ 2]) for q in range(4)]
    turned = jnp.concatenate(outs).T
    return turned[:own_rows], turned[own_rows]


def solution(mesh):
    sizes = (mesh.shape["train"], mesh.shape["test"])
    return jax.shard_map(
        four_by_four if sizes == (4, 4) else any_mesh,
        mesh=mesh,
        in_specs=(
            P(("groups", "train"), "test"),
            P(("groups", "test"), "train"),
            P("train", "test"),
            P(("groups", "test"), None),
        ),
        out_specs=(P(("groups", "train"), "test"), P(("groups", "test"))),
        check_vma=False,
    )
```

```python
import jax
import jax.numpy as jnp
from jax import lax
from jax.sharding import PartitionSpec as P

LAST_ROWS = 128

F32 = jnp.float32
BF16 = jnp.bfloat16


def dot_t(a, b):
    return lax.dot_general(a, b, (((1,), (1,)), ((), ())), preferred_element_type=F32)


def selection_counts(chosen_ids, first_row, rows):
    row_ids = first_row + lax.broadcasted_iota(jnp.int32, (rows, chosen_ids.shape[0]), 0)
    ids = chosen_ids.T
    counts = jnp.zeros(row_ids.shape, F32)
    for k in range(ids.shape[0]):
        counts = counts + (row_ids == ids[k][None, :]).astype(F32)
    return counts


def any_mesh(train_grads, test_grads, fisher, chosen_ids):
    test_whole = lax.all_gather(test_grads, "test", axis=0, tiled=True)
    partial_value = jnp.dot(test_whole, fisher, preferred_element_type=F32)
    precond = lax.psum(partial_value, "train").astype(BF16)
    partial_scores = dot_t(train_grads, precond)
    scores = lax.psum_scatter(partial_scores, "test", scatter_dimension=1, tiled=True)
    rows = scores.shape[0]
    counts = selection_counts(chosen_ids, lax.axis_index("train") * rows, rows)
    return scores, lax.psum(jnp.sum(counts * scores, axis=0), "train")


def four_by_four(train_grads, test_grads, fisher, chosen_ids):
    z = lax.axis_index("test")
    i = lax.axis_index("train")
    chip, core = i // 2, i % 2
    inner = (z == 1) | (z == 2)
    own_rows = train_grads.shape[0]
    queries = test_grads.shape[0]
    pieces = ((0, queries - LAST_ROWS), (queries - LAST_ROWS, LAST_ROWS))

    def along(value, pairs):
        return lax.ppermute(value, "test", pairs)

    def to_other(value, r):
        return lax.ppermute(value, "train", [(k, k ^ r) for k in range(4)])

    def tied(*values):
        return lax.optimization_barrier(values)

    pair = [(0, 1), (1, 0), (2, 3), (3, 2)]
    middle = [(1, 2), (2, 1)]
    outward = [(1, 0), (2, 3)]
    inward = [(0, 1), (3, 2)]

    def portion(value, cuts, which, of):
        return jnp.concatenate(
            [
                lax.dynamic_slice_in_dim(value, first + which * (rows // of), rows // of)
                for first, rows in cuts
            ]
        )

    def cut(sizes):
        return [(sum(sizes[:p]), sizes[p]) for p in range(len(sizes))]

    def product(block):
        return jnp.dot(block, fisher, preferred_element_type=F32)

    def core_sum(part, sizes, ways=2):
        kept = portion(part, cut(sizes), core, 2)
        sent = portion(part, cut(sizes), 1 - core, 2)
        step = sent.shape[0] // ways
        got = [to_other(sent[w * step : (w + 1) * step], 1) for w in range(ways)]
        return kept + jnp.concatenate(got)

    def chip_sum(part, sizes, sent_as=F32):
        halves = cut([rows // 2 for rows in sizes])
        sent = to_other(portion(part, halves, 1 - chip, 2).astype(sent_as), 2)
        return (portion(part, halves, chip, 2) + sent.astype(F32)).astype(BF16)

    whole = [rows for _, rows in pieces]
    first_rows = pieces[0][1]

    blocks = jnp.stack([i, i ^ 1, i ^ 2, i ^ 3])
    row_ids = (blocks[:, None] * own_rows + jnp.arange(own_rows)[None, :]).reshape(1, 1, -1)
    ids = portion(chosen_ids, cut(whole), core * 2 + chip, 4)
    counts = jnp.sum((ids[:, :, None] == row_ids).astype(F32), axis=1)

    def scores_of(precond):
        return [dot_t(precond, block) for block in grads]

    def send_scores(values, *pairs):
        packed = jnp.concatenate([value.astype(BF16) for value in values], axis=1)
        return [along(packed, each) for each in pairs]

    pair_in = along(test_grads, pair)
    middle_in = along(test_grads, middle)
    grads = [train_grads, to_other(train_grads, 1), to_other(train_grads, 2)]
    own = product(test_grads)
    pair_in, middle_in, grads, own, counts = tied(pair_in, middle_in, grads, own, counts)

    far_in = along(pair_in, middle)
    second_edge = along(middle_in, outward)
    own = core_sum(own, whole)
    near, own = tied(jnp.where(inner, middle_in, pair_in), own)
    near = product(near)
    own = chip_sum(own, whole)
    grads = grads + [to_other(grads[2], 1)]
    far_in, second_edge, pair_in, own, near, grads = tied(
        far_in, second_edge, pair_in, own, near, grads
    )

    first_edge = along(far_in[:first_rows], outward)
    near = core_sum(near, whole)
    second, near, own = tied(jnp.where(inner, pair_in, second_edge), near, own)
    second = core_sum(product(second), whole)
    near = scores_of(chip_sum(near, whole, BF16))
    own = scores_of(own)
    last_in = far_in[first_rows:]
    first_edge, last_in, far_in, own, near, second, grads = tied(
        first_edge, last_in, far_in, own, near, second, grads
    )

    last_edge = along(last_in, outward)
    second = chip_sum(second, whole, BF16)
    first_part = product(jnp.where(inner, far_in[:first_rows], first_edge))
    near = send_scores(near, inward, middle)
    last_edge, last_in, second, first_part, own, near, grads = tied(
        last_edge, last_in, second, first_part, own, near, grads
    )

    first_part = core_sum(first_part, whole[:1])
    second = send_scores(scores_of(second), [(1, 0), (2, 3), (0, 2), (3, 1)])
    last_part = core_sum(product(jnp.where(inner, last_in, last_edge)), whole[1:], 1)
    first_value = chip_sum(first_part, whole[:1], BF16)
    last_value = chip_sum(last_part, whole[1:], BF16)
    total = [
        sum([got[:, r * own_rows : (r + 1) * own_rows].astype(F32) for got in near + second], own[r])
        for r in range(4)
    ]

    outs = []
    for (first, rows), precond in zip(pieces, (first_value, last_value)):
        quarter = rows // 4
        sent = send_scores(scores_of(precond), [(0, 3), (3, 0)], [(1, 3), (2, 0)])
        parts = [
            sum(
                [got[:, r * own_rows : (r + 1) * own_rows].astype(F32) for got in sent],
                total[r][first // 4 : first // 4 + quarter],
            )
            for r in range(4)
        ]
        times = counts[first // 4 : first // 4 + quarter]
        times = [times[:, r * own_rows : (r + 1) * own_rows] for r in range(4)]
        chosen = sum(jnp.sum(times[r] * parts[r], axis=1, keepdims=True) for r in range(4))
        parts = [jnp.pad(part, ((0, 0), (0, 128))) for part in parts]
        column = lax.broadcasted_iota(jnp.int32, parts[0].shape, 1)
        parts = [jnp.where(column < own_rows, part, chosen) for part in parts]
        got = [parts[0]] + [to_other(parts[r], r) for r in range(1, 4)]
        got = [got[0], got[2], got[1], got[3]]
        got = [jnp.where(chip == 0, got[q], got[q ^ 1]) for q in range(4)]
        outs += [jnp.where(core == 0, got[q], got[q ^ 2]) for q in range(4)]
    turned = jnp.concatenate(outs).T
    return turned[:own_rows], turned[own_rows]


def solution(mesh):
    sizes = (mesh.shape["train"], mesh.shape["test"])
    return jax.shard_map(
        four_by_four if sizes == (4, 4) else any_mesh,
        mesh=mesh,
        in_specs=(
            P(("groups", "train"), "test"),
            P(("groups", "test"), "train"),
            P("train", "test"),
            P(("groups", "test"), None),
        ),
        out_specs=(P(("groups", "train"), "test"), P(("groups", "test"))),
        check_vma=False,
    )
```

```python
import jax
import jax.numpy as jnp
from jax import lax
from jax.experimental import pallas as pl
from jax.experimental.pallas import tpu as pltpu
from jax.sharding import PartitionSpec as P

COLUMNS = 512

F32 = jnp.float32
BF16 = jnp.bfloat16


def dot_t(a, b):
    return lax.dot_general(a, b, (((1,), (1,)), ((), ())), preferred_element_type=F32)


def selection_counts(chosen_ids, first_row, rows):
    row_ids = first_row + lax.broadcasted_iota(jnp.int32, (rows, chosen_ids.shape[0]), 0)
    ids = chosen_ids.T
    counts = jnp.zeros(row_ids.shape, F32)
    for k in range(ids.shape[0]):
        counts = counts + (row_ids == ids[k][None, :]).astype(F32)
    return counts


def any_mesh(train_grads, test_grads, fisher, chosen_ids):
    test_whole = lax.all_gather(test_grads, "test", axis=0, tiled=True)
    partial_value = jnp.dot(test_whole, fisher, preferred_element_type=F32)
    precond = lax.psum(partial_value, "train").astype(BF16)
    partial_scores = dot_t(train_grads, precond)
    scores = lax.psum_scatter(partial_scores, "test", scatter_dimension=1, tiled=True)
    rows = scores.shape[0]
    counts = selection_counts(chosen_ids, lax.axis_index("train") * rows, rows)
    return scores, lax.psum(jnp.sum(counts * scores, axis=0), "train")


SMALL = pl.CostEstimate(flops=1, bytes_accessed=1, transcendentals=0)
PARAMS = pltpu.CompilerParams(vmem_limit_bytes=60 * 2**20)


def product_body(choices, parts, flags, *refs):
    count = sum(len(choice) for choice in choices)
    blocks, fisher, outs, (held, sems) = refs[:count], refs[count], refs[count + 1 : -2], refs[-2:]
    block_rows = blocks[0].shape[0]

    @pl.when(pl.program_id(0) == 0)
    def _():
        places = [held.at[pl.ds(u * block_rows, block_rows)] for u in range(len(choices))]
        first = 0
        for u, choice in enumerate(choices):
            if len(choice) == 1:
                pltpu.make_async_copy(blocks[first], places[u], sems.at[u]).start()
            else:

                @pl.when(flags[2] == 1)
                def _():
                    pltpu.make_async_copy(blocks[first], places[u], sems.at[u]).start()

                @pl.when(flags[2] == 0)
                def _():
                    pltpu.make_async_copy(blocks[first + 1], places[u], sems.at[u]).start()

            first += len(choice)
        for u in range(len(choices)):
            pltpu.make_async_copy(blocks[0], places[u], sems.at[u]).wait()

    quarter = block_rows // 4
    rows = quarter // parts
    first = flags[0] == 0
    for u in range(len(choices)):
        block = held[u * block_rows : (u + 1) * block_rows]
        value = jnp.dot(block, fisher[...], preferred_element_type=F32)
        for p in range(parts):
            kept, sent = outs[2 * (u * parts + p) :][:2]
            for chip in range(2):
                low, high = (
                    value[(2 * core + chip) * quarter + p * rows :][:rows] for core in range(2)
                )
                kept[chip * rows : (chip + 1) * rows] = jnp.where(first, low, high)
                sent[chip * rows : (chip + 1) * rows] = jnp.where(first, high, low).astype(BF16)


def product(flags, choices, fisher, parts=1):
    rows, depth = choices[0][0].shape
    columns = fisher.shape[1]
    half = rows // 2 // parts
    blocks = [block for choice in choices for block in choice]
    outs = len(choices) * parts
    return pl.pallas_call(
        lambda *refs: product_body(choices, parts, *refs),
        grid=(columns // COLUMNS,),
        in_specs=[pl.BlockSpec(memory_space=pltpu.SMEM)]
        + [pl.BlockSpec(memory_space=pl.ANY)] * len(blocks)
        + [pl.BlockSpec((depth, COLUMNS), lambda n: (0, n))],
        out_specs=[pl.BlockSpec((half, COLUMNS), lambda n: (0, n))] * (2 * outs),
        out_shape=[
            jax.ShapeDtypeStruct((half, columns), F32),
            jax.ShapeDtypeStruct((half, columns), BF16),
        ]
        * outs,
        scratch_shapes=[
            pltpu.VMEM((len(choices) * rows, depth), BF16),
            pltpu.SemaphoreType.DMA((len(choices),)),
        ],
        compiler_params=PARAMS,
        cost_estimate=SMALL,
        name="product",
    )(flags, *blocks, fisher)


def fold_body(flags, kept, got, kept_out, sent_out):
    value = kept[...] + got[...].astype(F32)
    half = value.shape[0] // 2
    first = flags[1] == 0
    low, high = value[:half], value[half:]
    kept_out[...] = jnp.where(first, low, high)
    sent_out[...] = jnp.where(first, high, low).astype(sent_out.dtype)


def fold(flags, kept, got, sent_as):
    rows, columns = kept.shape
    tile = COLUMNS
    before = pl.BlockSpec((rows, tile), lambda n: (0, n))
    after = pl.BlockSpec((rows // 2, tile), lambda n: (0, n))
    return pl.pallas_call(
        fold_body,
        grid=(columns // tile,),
        in_specs=[pl.BlockSpec(memory_space=pltpu.SMEM), before, before],
        out_specs=[after, after],
        out_shape=[
            jax.ShapeDtypeStruct((rows // 2, columns), F32),
            jax.ShapeDtypeStruct((rows // 2, columns), sent_as),
        ],
        compiler_params=PARAMS,
        cost_estimate=SMALL,
        name="fold",
    )(flags, kept, got)


def scores_body(units, *refs):
    sums, grads, outs, (held, sems) = refs[: 2 * units], refs[2 * units :][:4], refs[-2 - units : -2], refs[-2:]
    copies = [pltpu.make_async_copy(grads[r], held.at[r], sems.at[r]) for r in range(4)]
    for copy in copies:
        copy.start()
    values = [sums[2 * u][...] + sums[2 * u + 1][...].astype(F32) for u in range(units)]
    values = [(value.astype(BF16), value) for value in values]
    values = [(high, (value - high.astype(F32)).astype(BF16)) for high, value in values]
    precond = jnp.concatenate([part for value in values for part in value])
    rows = sums[0].shape[0]
    for r in range(4):
        copies[r].wait()
        both = dot_t(precond, held[r])
        for u in range(units):
            value = both[2 * u * rows :][:rows] + both[(2 * u + 1) * rows :][:rows]
            outs[u][r] = value.astype(outs[u].dtype)


def partial_scores(units, grads, out_as):
    rows = units[0][0].shape[0]
    train_rows, depth = grads[0].shape
    return pl.pallas_call(
        lambda *refs: scores_body(len(units), *refs),
        in_specs=[pl.BlockSpec(memory_space=pltpu.VMEM)] * (2 * len(units))
        + [pl.BlockSpec(memory_space=pl.ANY)] * 4,
        out_specs=[pl.BlockSpec(memory_space=pltpu.VMEM)] * len(units),
        out_shape=[jax.ShapeDtypeStruct((4, rows, train_rows), kind) for kind in out_as],
        scratch_shapes=[
            pltpu.VMEM((4, train_rows, depth), BF16),
            pltpu.SemaphoreType.DMA((4,)),
        ],
        compiler_params=PARAMS,
        cost_estimate=SMALL,
        name="scores",
    )(*[value for unit in units for value in unit], *grads)


def four_by_four(train_grads, test_grads, fisher, chosen_ids):
    z = lax.axis_index("test")
    i = lax.axis_index("train")
    chip, core = i // 2, i % 2
    inner = (z == 1) | (z == 2)
    flags = jnp.stack([core, chip, inner.astype(jnp.int32)])
    own_rows = train_grads.shape[0]
    queries, depth = test_grads.shape
    quarter = queries // 4
    split = quarter // 2

    def along(value, pairs):
        return lax.ppermute(value, "test", pairs)

    def to_other(value, r):
        return lax.ppermute(value, "train", [(k, k ^ r) for k in range(4)])

    def tied(*values):
        return lax.optimization_barrier(values)

    pair = [(0, 1), (1, 0), (2, 3), (3, 2)]
    middle = [(1, 2), (2, 1)]
    outward = [(1, 0), (2, 3)]
    inward = [(0, 1), (3, 2)]

    def core_sum(kept, sent, sent_as=BF16):
        return fold(flags, kept, to_other(sent, 1), sent_as)

    def scores_of(*units, out_as=(BF16, BF16)):
        return partial_scores(units, grads, out_as[: len(units)])

    blocks = jnp.stack([i, i ^ 1, i ^ 2, i ^ 3])
    row_ids = blocks[:, None, None, None] * own_rows + jnp.arange(own_rows)
    ids = lax.dynamic_slice_in_dim(chosen_ids, (core * 2 + chip) * quarter, quarter)
    counts = jnp.sum((ids[None, :, :, None] == row_ids).astype(F32), axis=2)

    pair_in = along(test_grads, pair)
    middle_in = along(test_grads, middle)
    grads = [train_grads, to_other(train_grads, 1), to_other(train_grads, 2)]
    own, own_sent = core_sum(*product(flags, [[test_grads]], fisher), F32)
    pair_in, middle_in, own, own_sent, counts, grads[1] = tied(
        pair_in, middle_in, own, own_sent, counts, grads[1]
    )

    far_in = along(pair_in, middle)
    second_edge = along(middle_in, outward)
    own_got = to_other(own_sent, 2)
    near, near_sent = core_sum(*product(flags, [[middle_in, pair_in]], fisher))
    near_got = to_other(near_sent, 2)
    grads = grads + [to_other(grads[2], 1)]
    far_in, second_edge, pair_in, own, own_got, near, near_got, grads = tied(
        far_in, second_edge, pair_in, own, own_got, near, near_got, grads
    )

    first_edge = along(far_in, outward)
    second, second_sent, third, third_sent = product(
        flags, [[far_in, second_edge], [pair_in]], fisher
    )
    second, second_sent = core_sum(second, second_sent)
    third, third_sent = core_sum(third, third_sent)
    second_sent, third_sent, near, own = tied(second_sent, third_sent, near, own)
    near, total = scores_of((near, near_got), (own, own_got), out_as=(BF16, F32))
    second, third = scores_of(
        (second, to_other(second_sent, 2)), (third, to_other(third_sent, 2))
    )
    total = total + along(near, inward).astype(F32) + along(near, middle).astype(F32)
    first_edge, total, second, third, grads = tied(first_edge, total, second, third, grads)

    second = along(second, [(0, 2), (3, 1), (1, 3), (2, 0)])
    third = along(third, outward)
    total = total + second.astype(F32) + third.astype(F32)
    last = product(flags, [[first_edge]], fisher, 2)

    outs = []
    for p, first in enumerate((0, split)):
        part, part_sent = core_sum(*last[2 * p : 2 * p + 2])
        (value,) = scores_of((part, to_other(part_sent, 2)))
        value = along(value, [(0, 3), (3, 0)]).astype(F32) + total[:, first : first + split]
        rows = split
        chosen = jnp.sum(value * counts[:, first : first + rows], axis=(0, 2))[:, None]
        parts = [jnp.pad(value[r], ((0, 0), (0, 128))) for r in range(4)]
        column = lax.broadcasted_iota(jnp.int32, parts[0].shape, 1)
        parts = [jnp.where(column < own_rows, part, chosen) for part in parts]
        got = [parts[0]] + [to_other(parts[r], r) for r in range(1, 4)]
        got = [got[0], got[2], got[1], got[3]]
        got = [jnp.where(chip == 0, got[q], got[q ^ 1]) for q in range(4)]
        outs.append([jnp.where(core == 0, got[q], got[q ^ 2]) for q in range(4)])
    turned = jnp.concatenate([piece[q] for q in range(4) for piece in outs]).T
    return turned[:own_rows], turned[own_rows]


def solution(mesh):
    sizes = (mesh.shape["train"], mesh.shape["test"])
    return jax.shard_map(
        four_by_four if sizes == (4, 4) else any_mesh,
        mesh=mesh,
        in_specs=(
            P(("groups", "train"), "test"),
            P(("groups", "test"), "train"),
            P("train", "test"),
            P(("groups", "test"), None),
        ),
        out_specs=(P(("groups", "train"), "test"), P(("groups", "test"))),
        check_vma=False,
    )
```

```python
import jax
import jax.numpy as jnp
from jax import lax
from jax.experimental import pallas as pl
from jax.experimental.pallas import tpu as pltpu
from jax.sharding import PartitionSpec as P

COLUMNS = 512

F32 = jnp.float32
BF16 = jnp.bfloat16


def dot_t(a, b):
    return lax.dot_general(a, b, (((1,), (1,)), ((), ())), preferred_element_type=F32)


def selection_counts(chosen_ids, first_row, rows):
    row_ids = first_row + lax.broadcasted_iota(jnp.int32, (rows, chosen_ids.shape[0]), 0)
    ids = chosen_ids.T
    counts = jnp.zeros(row_ids.shape, F32)
    for k in range(ids.shape[0]):
        counts = counts + (row_ids == ids[k][None, :]).astype(F32)
    return counts


def any_mesh(train_grads, test_grads, fisher, chosen_ids):
    test_whole = lax.all_gather(test_grads, "test", axis=0, tiled=True)
    partial_value = jnp.dot(test_whole, fisher, preferred_element_type=F32)
    precond = lax.psum(partial_value, "train").astype(BF16)
    partial_scores = dot_t(train_grads, precond)
    scores = lax.psum_scatter(partial_scores, "test", scatter_dimension=1, tiled=True)
    rows = scores.shape[0]
    counts = selection_counts(chosen_ids, lax.axis_index("train") * rows, rows)
    return scores, lax.psum(jnp.sum(counts * scores, axis=0), "train")


SMALL = pl.CostEstimate(flops=1, bytes_accessed=1, transcendentals=0)
PARAMS = pltpu.CompilerParams(vmem_limit_bytes=16 * 2**20)


VMEM = pl.BlockSpec(memory_space=pltpu.VMEM)


def product_body(choices, parts, flags, *refs):
    count = sum(len(choice) for choice in choices)
    blocks, fisher, outs = refs[:count], refs[count], refs[count + 1 :]
    quarter = blocks[0].shape[0] // 4
    rows = quarter // parts
    mine = flags[0] == 0

    def multiply(block, outs):
        @pl.loop(0, fisher.shape[1] // COLUMNS)
        def _(n):
            columns = pl.ds(pl.multiple_of(n * COLUMNS, COLUMNS), COLUMNS)
            value = jnp.dot(block[...], fisher[:, columns], preferred_element_type=F32)
            for p in range(parts):
                kept, sent = outs[2 * p : 2 * p + 2]
                for chip in range(2):
                    low, high = (
                        value[(2 * core + chip) * quarter + p * rows :][:rows] for core in range(2)
                    )
                    place = pl.ds(chip * rows, rows)
                    kept[place, columns] = jnp.where(mine, low, high)
                    sent[place, columns] = jnp.where(mine, high, low).astype(BF16)

    first = 0
    for u, choice in enumerate(choices):
        these = outs[2 * parts * u : 2 * parts * (u + 1)]
        if len(choice) == 1:
            multiply(blocks[first], these)
        else:
            pl.when(flags[2] == 1)(lambda: multiply(blocks[first], these))
            pl.when(flags[2] == 0)(lambda: multiply(blocks[first + 1], these))
        first += len(choice)


def product(flags, choices, fisher, parts=1):
    half = choices[0][0].shape[0] // 2 // parts
    columns = fisher.shape[1]
    blocks = [block for choice in choices for block in choice]
    outs = len(choices) * parts
    return pl.pallas_call(
        lambda *refs: product_body(choices, parts, *refs),
        in_specs=[pl.BlockSpec(memory_space=pltpu.SMEM)] + [VMEM] * (len(blocks) + 1),
        out_specs=[VMEM] * (2 * outs),
        out_shape=[
            jax.ShapeDtypeStruct((half, columns), F32),
            jax.ShapeDtypeStruct((half, columns), BF16),
        ]
        * outs,
        compiler_params=PARAMS,
        cost_estimate=SMALL,
        name="product",
    )(flags, *blocks, fisher)


def fold_body(flags, kept, got, kept_out, sent_out):
    half = kept.shape[0] // 2
    first = flags[1] == 0

    @pl.loop(0, kept.shape[1] // COLUMNS)
    def _(n):
        columns = pl.ds(pl.multiple_of(n * COLUMNS, COLUMNS), COLUMNS)
        value = kept[:, columns] + got[:, columns].astype(F32)
        low, high = value[:half], value[half:]
        kept_out[:, columns] = jnp.where(first, low, high)
        sent_out[:, columns] = jnp.where(first, high, low).astype(sent_out.dtype)


def fold(flags, kept, got, sent_as):
    rows, columns = kept.shape
    return pl.pallas_call(
        fold_body,
        in_specs=[pl.BlockSpec(memory_space=pltpu.SMEM), VMEM, VMEM],
        out_specs=[VMEM, VMEM],
        out_shape=[
            jax.ShapeDtypeStruct((rows // 2, columns), F32),
            jax.ShapeDtypeStruct((rows // 2, columns), sent_as),
        ],
        compiler_params=PARAMS,
        cost_estimate=SMALL,
        name="fold",
    )(flags, kept, got)


def scores_body(units, *refs):
    sums, grads, outs = refs[: 2 * units], refs[2 * units :][:4], refs[2 * units + 4 :]
    values = [sums[2 * u][...] + sums[2 * u + 1][...].astype(F32) for u in range(units)]
    values = [(value.astype(BF16), value) for value in values]
    values = [(high, (value - high.astype(F32)).astype(BF16)) for high, value in values]
    precond = jnp.concatenate([part for value in values for part in value])
    rows = sums[0].shape[0]
    for r in range(4):
        both = dot_t(precond, grads[r][...])
        for u in range(units):
            value = both[2 * u * rows :][:rows] + both[(2 * u + 1) * rows :][:rows]
            outs[u][r] = value.astype(outs[u].dtype)


def partial_scores(units, grads, out_as):
    rows = units[0][0].shape[0]
    train_rows = grads[0].shape[0]
    return pl.pallas_call(
        lambda *refs: scores_body(len(units), *refs),
        in_specs=[VMEM] * (2 * len(units) + 4),
        out_specs=[VMEM] * len(units),
        out_shape=[jax.ShapeDtypeStruct((4, rows, train_rows), kind) for kind in out_as],
        compiler_params=PARAMS,
        cost_estimate=SMALL,
        name="scores",
    )(*[value for unit in units for value in unit], *grads)


def four_by_four(train_grads, test_grads, fisher, chosen_ids):
    z = lax.axis_index("test")
    i = lax.axis_index("train")
    chip, core = i // 2, i % 2
    inner = (z == 1) | (z == 2)
    flags = jnp.stack([core, chip, inner.astype(jnp.int32)])
    own_rows = train_grads.shape[0]
    queries, depth = test_grads.shape
    quarter = queries // 4
    split = quarter // 2

    def along(value, pairs):
        return lax.ppermute(value, "test", pairs)

    def to_other(value, r):
        return lax.ppermute(value, "train", [(k, k ^ r) for k in range(4)])

    def tied(*values):
        return lax.optimization_barrier(values)

    pair = [(0, 1), (1, 0), (2, 3), (3, 2)]
    middle = [(1, 2), (2, 1)]
    outward = [(1, 0), (2, 3)]
    inward = [(0, 1), (3, 2)]

    def core_sum(kept, sent, sent_as=BF16):
        return fold(flags, kept, to_other(sent, 1), sent_as)

    def scores_of(*units, out_as=(BF16, BF16)):
        return partial_scores(units, grads, out_as[: len(units)])

    blocks = jnp.stack([i, i ^ 1, i ^ 2, i ^ 3])
    row_ids = blocks[:, None, None, None] * own_rows + jnp.arange(own_rows)
    ids = lax.dynamic_slice_in_dim(chosen_ids, (core * 2 + chip) * quarter, quarter)
    counts = jnp.sum((ids[None, :, :, None] == row_ids).astype(F32), axis=2)

    pair_in = along(test_grads, pair)
    middle_in = along(test_grads, middle)
    grads = [train_grads, to_other(train_grads, 1), to_other(train_grads, 2)]
    own, own_sent = core_sum(*product(flags, [[test_grads]], fisher), F32)
    pair_in, middle_in, own, own_sent, counts, grads[1] = tied(
        pair_in, middle_in, own, own_sent, counts, grads[1]
    )

    far_in = along(pair_in, middle)
    second_edge = along(middle_in, outward)
    own_got = to_other(own_sent, 2)
    near, near_sent = core_sum(*product(flags, [[middle_in, pair_in]], fisher))
    near_got = to_other(near_sent, 2)
    grads = grads + [to_other(grads[2], 1)]
    far_in, second_edge, pair_in, own, own_got, near, near_got, grads = tied(
        far_in, second_edge, pair_in, own, own_got, near, near_got, grads
    )

    first_edge = along(far_in, outward)
    second, second_sent, third, third_sent = product(
        flags, [[far_in, second_edge], [pair_in]], fisher
    )
    second, second_sent = core_sum(second, second_sent)
    third, third_sent = core_sum(third, third_sent)
    second_sent, third_sent, near, own = tied(second_sent, third_sent, near, own)
    near, total = scores_of((near, near_got), (own, own_got), out_as=(BF16, F32))
    second, third = scores_of(
        (second, to_other(second_sent, 2)), (third, to_other(third_sent, 2))
    )
    total = total + along(near, inward).astype(F32) + along(near, middle).astype(F32)
    first_edge, total, second, third, grads = tied(first_edge, total, second, third, grads)

    second = along(second, [(0, 2), (3, 1), (1, 3), (2, 0)])
    third = along(third, outward)
    total = total + second.astype(F32) + third.astype(F32)
    last = product(flags, [[first_edge]], fisher, 2)

    outs = []
    for p, first in enumerate((0, split)):
        part, part_sent = core_sum(*last[2 * p : 2 * p + 2])
        (value,) = scores_of((part, to_other(part_sent, 2)))
        value = along(value, [(0, 3), (3, 0)]).astype(F32) + total[:, first : first + split]
        rows = split
        chosen = jnp.sum(value * counts[:, first : first + rows], axis=(0, 2))[:, None]
        parts = [jnp.pad(value[r], ((0, 0), (0, 128))) for r in range(4)]
        column = lax.broadcasted_iota(jnp.int32, parts[0].shape, 1)
        parts = [jnp.where(column < own_rows, part, chosen) for part in parts]
        got = [parts[0]] + [to_other(parts[r], r) for r in range(1, 4)]
        got = [got[0], got[2], got[1], got[3]]
        got = [jnp.where(chip == 0, got[q], got[q ^ 1]) for q in range(4)]
        outs.append([jnp.where(core == 0, got[q], got[q ^ 2]) for q in range(4)])
    turned = jnp.concatenate([piece[q] for q in range(4) for piece in outs]).T
    return turned[:own_rows], turned[own_rows]


def solution(mesh):
    sizes = (mesh.shape["train"], mesh.shape["test"])
    return jax.shard_map(
        four_by_four if sizes == (4, 4) else any_mesh,
        mesh=mesh,
        in_specs=(
            P(("groups", "train"), "test"),
            P(("groups", "test"), "train"),
            P("train", "test"),
            P(("groups", "test"), None),
        ),
        out_specs=(P(("groups", "train"), "test"), P(("groups", "test"))),
        check_vma=False,
    )
```

```python
import jax
import jax.numpy as jnp
from jax import lax
from jax.experimental import pallas as pl
from jax.experimental.pallas import tpu as pltpu
from jax.sharding import PartitionSpec as P

COLUMNS = 512

F32 = jnp.float32
BF16 = jnp.bfloat16


def dot_t(a, b):
    return lax.dot_general(a, b, (((1,), (1,)), ((), ())), preferred_element_type=F32)


def selection_counts(chosen_ids, first_row, rows):
    row_ids = first_row + lax.broadcasted_iota(jnp.int32, (rows, chosen_ids.shape[0]), 0)
    ids = chosen_ids.T
    counts = jnp.zeros(row_ids.shape, F32)
    for k in range(ids.shape[0]):
        counts = counts + (row_ids == ids[k][None, :]).astype(F32)
    return counts


def any_mesh(train_grads, test_grads, fisher, chosen_ids):
    test_whole = lax.all_gather(test_grads, "test", axis=0, tiled=True)
    partial_value = jnp.dot(test_whole, fisher, preferred_element_type=F32)
    precond = lax.psum(partial_value, "train").astype(BF16)
    partial_scores = dot_t(train_grads, precond)
    scores = lax.psum_scatter(partial_scores, "test", scatter_dimension=1, tiled=True)
    rows = scores.shape[0]
    counts = selection_counts(chosen_ids, lax.axis_index("train") * rows, rows)
    return scores, lax.psum(jnp.sum(counts * scores, axis=0), "train")


SMALL = pl.CostEstimate(flops=1, bytes_accessed=1, transcendentals=0)
PARAMS = pltpu.CompilerParams(vmem_limit_bytes=16 * 2**20)


VMEM = pl.BlockSpec(memory_space=pltpu.VMEM)


def product_body(choices, flags, *refs):
    count = sum(len(choice) for choice in choices)
    blocks, fisher, outs = refs[:count], refs[count], refs[count + 1 :]
    quarter = blocks[0].shape[0] // 4
    mine = flags[0] == 0

    def multiply(block, kept, *sent):
        @pl.loop(0, fisher.shape[1] // COLUMNS)
        def _(n):
            columns = pl.ds(pl.multiple_of(n * COLUMNS, COLUMNS), COLUMNS)
            value = jnp.dot(block[...], fisher[:, columns], preferred_element_type=F32)
            for chip in range(2):
                low, high = (value[(2 * core + chip) * quarter :][:quarter] for core in range(2))
                kept[pl.ds(chip * quarter, quarter), columns] = jnp.where(mine, low, high)
                sent[chip][:, columns] = jnp.where(mine, high, low).astype(BF16)

    first = 0
    for u, choice in enumerate(choices):
        these = outs[3 * u : 3 * (u + 1)]
        if len(choice) == 1:
            multiply(blocks[first], *these)
        else:
            pl.when(flags[2] == 1)(lambda: multiply(blocks[first], *these))
            pl.when(flags[2] == 0)(lambda: multiply(blocks[first + 1], *these))
        first += len(choice)


def product(flags, choices, fisher):
    quarter = choices[0][0].shape[0] // 4
    columns = fisher.shape[1]
    blocks = [block for choice in choices for block in choice]
    return pl.pallas_call(
        lambda *refs: product_body(choices, *refs),
        in_specs=[pl.BlockSpec(memory_space=pltpu.SMEM)] + [VMEM] * (len(blocks) + 1),
        out_specs=[VMEM] * (3 * len(choices)),
        out_shape=[
            jax.ShapeDtypeStruct((2 * quarter, columns), F32),
            jax.ShapeDtypeStruct((quarter, columns), BF16),
            jax.ShapeDtypeStruct((quarter, columns), BF16),
        ]
        * len(choices),
        compiler_params=PARAMS,
        cost_estimate=SMALL,
        name="product",
    )(flags, *blocks, fisher)


def fold_body(flags, kept, got_low, got_high, kept_out, sent_out):
    half = got_low.shape[0]
    first = flags[1] == 0

    @pl.loop(0, kept.shape[1] // COLUMNS)
    def _(n):
        columns = pl.ds(pl.multiple_of(n * COLUMNS, COLUMNS), COLUMNS)
        low = kept[:half, columns] + got_low[:, columns].astype(F32)
        high = kept[half:, columns] + got_high[:, columns].astype(F32)
        kept_out[:, columns] = jnp.where(first, low, high)
        sent_out[:, columns] = jnp.where(first, high, low).astype(sent_out.dtype)


def fold(flags, kept, got_low, got_high, sent_as):
    return pl.pallas_call(
        fold_body,
        in_specs=[pl.BlockSpec(memory_space=pltpu.SMEM)] + [VMEM] * 3,
        out_specs=[VMEM, VMEM],
        out_shape=[
            jax.ShapeDtypeStruct(got_low.shape, F32),
            jax.ShapeDtypeStruct(got_low.shape, sent_as),
        ],
        compiler_params=PARAMS,
        cost_estimate=SMALL,
        name="fold",
    )(flags, kept, got_low, got_high)


def split_sum(kept, got):
    value = kept[...] + got[...].astype(F32)
    high = value.astype(BF16)
    return high, (value - high.astype(F32)).astype(BF16)


def scores_body(units, *refs):
    sums, grads, outs = refs[: 2 * units], refs[2 * units :][:4], refs[2 * units + 4 :]
    rows = sums[0].shape[0]
    precond = jnp.concatenate(
        [part for u in range(units) for part in split_sum(sums[2 * u], sums[2 * u + 1])]
    )
    for r in range(4):
        both = dot_t(precond, grads[r][...])
        for u in range(units):
            value = both[2 * u * rows :][:rows] + both[(2 * u + 1) * rows :][:rows]
            outs[u][r] = value.astype(outs[u].dtype)


def partial_scores(units, grads, out_as):
    rows = units[0][0].shape[0]
    train_rows = grads[0].shape[0]
    return pl.pallas_call(
        lambda *refs: scores_body(len(units), *refs),
        in_specs=[VMEM] * (2 * len(units) + 4),
        out_specs=[VMEM] * len(units),
        out_shape=[jax.ShapeDtypeStruct((4, rows, train_rows), kind) for kind in out_as],
        compiler_params=PARAMS,
        cost_estimate=SMALL,
        name="scores",
    )(*[value for unit in units for value in unit], *grads)


def last_scores_body(kept, got, counts, *refs):
    grads, out = refs[:4], refs[4]
    rows = kept.shape[0]
    train_rows = grads[0].shape[0]
    precond = jnp.concatenate(split_sum(kept, got))
    chosen = jnp.zeros((rows, 1), F32)
    for r in range(4):
        both = dot_t(precond, grads[r][...])
        value = both[:rows] + both[rows:]
        out[r, :, :train_rows] = value.astype(out.dtype)
        chosen = chosen + jnp.sum(value * counts[r], axis=1, keepdims=True)
    for r in range(4):
        out[r, :, train_rows:] = jnp.broadcast_to(chosen, (rows, 128)).astype(out.dtype)


def last_scores(kept, got, counts, grads):
    rows = kept.shape[0]
    return pl.pallas_call(
        last_scores_body,
        in_specs=[VMEM] * 7,
        out_specs=VMEM,
        out_shape=jax.ShapeDtypeStruct((4, rows, grads[0].shape[0] + 128), BF16),
        compiler_params=PARAMS,
        cost_estimate=SMALL,
        name="last_scores",
    )(kept, got, counts, *grads)


def four_by_four(train_grads, test_grads, fisher, chosen_ids):
    z = lax.axis_index("test")
    i = lax.axis_index("train")
    chip, core = i // 2, i % 2
    inner = (z == 1) | (z == 2)
    flags = jnp.stack([core, chip, inner.astype(jnp.int32)])
    own_rows = train_grads.shape[0]
    quarter = test_grads.shape[0] // 4

    def along(value, pairs):
        return lax.ppermute(value, "test", pairs)

    def to_other(value, r):
        return lax.ppermute(value, "train", [(k, k ^ r) for k in range(4)])

    def tied(*values):
        return lax.optimization_barrier(values)

    pair = [(0, 1), (1, 0), (2, 3), (3, 2)]
    middle = [(1, 2), (2, 1)]
    outward = [(1, 0), (2, 3)]
    inward = [(0, 1), (3, 2)]

    def core_sum(kept, *sent, sent_as=BF16):
        return fold(flags, kept, *(to_other(part, 1) for part in sent), sent_as)

    def scores_of(*units, out_as=(BF16, BF16)):
        return partial_scores(units, grads, out_as[: len(units)])

    def straight(value, r):
        pairs = [(0, 3), (3, 0)]
        pairs = [(k * 4 + a, (k ^ r) * 4 + b) for k in range(4) for a, b in pairs]
        return lax.ppermute(value, ("train", "test"), pairs)

    def in_order(parts):
        parts = [parts[0], parts[2], parts[1], parts[3]]
        parts = [jnp.where(chip == 0, parts[q], parts[q ^ 1]) for q in range(4)]
        return jnp.concatenate([jnp.where(core == 0, parts[q], parts[q ^ 2]) for q in range(4)])

    row_ids = jnp.stack([i, i ^ 1, i ^ 2, i ^ 3])[:, None, None, None] * own_rows
    row_ids = row_ids + jnp.arange(own_rows)

    def selected(ids):
        ids = lax.dynamic_slice_in_dim(ids, (core * 2 + chip) * quarter, quarter)
        return jnp.sum((ids[None, :, :, None] == row_ids).astype(F32), axis=2)

    pair_in = along(test_grads, pair)
    middle_in = along(test_grads, middle)
    grads = [train_grads, to_other(train_grads, 1), to_other(train_grads, 2)]
    own, own_sent = core_sum(*product(flags, [[test_grads]], fisher), sent_as=F32)
    counts = selected(chosen_ids)
    far_ids = along(chosen_ids, [(0, 3), (3, 0)])
    pair_in, middle_in, own, own_sent, counts, far_ids, grads[1] = tied(
        pair_in, middle_in, own, own_sent, counts, far_ids, grads[1]
    )

    second_edge = along(middle_in, outward)
    far_in = along(pair_in, middle)
    own_got = to_other(own_sent, 2)
    near, near_sent = core_sum(*product(flags, [[middle_in, pair_in]], fisher))
    near_got = to_other(near_sent, 2)
    far_counts = selected(far_ids)
    grads = grads + [to_other(grads[2], 1)]
    far_in, second_edge, pair_in, own, own_got, near, near_got, far_counts, grads = tied(
        far_in, second_edge, pair_in, own, own_got, near, near_got, far_counts, grads
    )

    first_edge = along(far_in, outward)
    second, second_sent = core_sum(*product(flags, [[far_in, second_edge]], fisher))
    second_sent, pair_in, near, own = tied(second_sent, pair_in, near, own)
    third, third_sent = core_sum(*product(flags, [[pair_in]], fisher))
    near, total = scores_of((near, near_got), (own, own_got), out_as=(BF16, F32))
    total = total + along(near, inward).astype(F32) + along(near, middle).astype(F32)
    (second,) = scores_of((second, to_other(second_sent, 2)))
    total = total + along(second, [(0, 2), (3, 1)]).astype(F32)
    second = along(second, middle)
    third_got = to_other(third_sent, 2)
    first_edge, total, second, third, third_got, grads, far_counts = tied(
        first_edge, total, second, third, third_got, grads, far_counts
    )

    (third,) = scores_of((third, third_got), out_as=(F32,))
    third = along((third + second.astype(F32)).astype(BF16), outward)
    last, last_sent = core_sum(*product(flags, [[first_edge]], fisher))
    last = last_scores(last, to_other(last_sent, 2), far_counts, grads)
    last = in_order([straight(last[r], r) for r in range(4)])

    total = total + third.astype(F32)
    chosen = jnp.sum(total * counts, axis=(0, 2))[:, None]
    total = jnp.pad(total, ((0, 0), (0, 0), (0, 128)))
    column = lax.broadcasted_iota(jnp.int32, total.shape, 2)
    total = jnp.where(column < own_rows, total, chosen)
    total = in_order([total[0]] + [to_other(total[r], r) for r in range(1, 4)])

    turned = (total + last.astype(F32)).T
    return turned[:own_rows], turned[own_rows]


def solution(mesh):
    sizes = (mesh.shape["train"], mesh.shape["test"])
    return jax.shard_map(
        four_by_four if sizes == (4, 4) else any_mesh,
        mesh=mesh,
        in_specs=(
            P(("groups", "train"), "test"),
            P(("groups", "test"), "train"),
            P("train", "test"),
            P(("groups", "test"), None),
        ),
        out_specs=(P(("groups", "train"), "test"), P(("groups", "test"))),
        check_vma=False,
    )
```

```python
import functools

import jax
import jax.numpy as jnp
from jax import lax
from jax.experimental import pallas as pl
from jax.experimental.pallas import tpu as pltpu
from jax.sharding import PartitionSpec as P

COLUMNS = 512
EXTRA = 16

F32 = jnp.float32
BF16 = jnp.bfloat16


def dot_t(a, b):
    return lax.dot_general(a, b, (((1,), (1,)), ((), ())), preferred_element_type=F32)


def selection_counts(chosen_ids, first_row, rows):
    row_ids = first_row + lax.broadcasted_iota(jnp.int32, (rows, chosen_ids.shape[0]), 0)
    ids = chosen_ids.T
    counts = jnp.zeros(row_ids.shape, F32)
    for k in range(ids.shape[0]):
        counts = counts + (row_ids == ids[k][None, :]).astype(F32)
    return counts


def any_mesh(train_grads, test_grads, fisher, chosen_ids):
    test_whole = lax.all_gather(test_grads, "test", axis=0, tiled=True)
    partial_value = jnp.dot(test_whole, fisher, preferred_element_type=F32)
    precond = lax.psum(partial_value, "train").astype(BF16)
    partial_scores = dot_t(train_grads, precond)
    scores = lax.psum_scatter(partial_scores, "test", scatter_dimension=1, tiled=True)
    rows = scores.shape[0]
    counts = selection_counts(chosen_ids, lax.axis_index("train") * rows, rows)
    return scores, lax.psum(jnp.sum(counts * scores, axis=0), "train")


SMALL = pl.CostEstimate(flops=1, bytes_accessed=1, transcendentals=0)
PARAMS = pltpu.CompilerParams(vmem_limit_bytes=16 * 2**20)


VMEM = pl.BlockSpec(memory_space=pltpu.VMEM)


def product_body(count, flags, *refs):
    blocks, fisher, outs = refs[:count], refs[count], refs[count + 1 :]
    quarter = blocks[0].shape[0] // 4
    mine = flags[0] == 0

    def multiply(block, kept, *sent):
        @pl.loop(0, fisher.shape[1] // COLUMNS)
        def _(n):
            columns = pl.ds(pl.multiple_of(n * COLUMNS, COLUMNS), COLUMNS)
            value = jnp.dot(block[...], fisher[:, columns], preferred_element_type=F32)
            for chip in range(2):
                low, high = (value[(2 * core + chip) * quarter :][:quarter] for core in range(2))
                kept[pl.ds(chip * quarter, quarter), columns] = jnp.where(mine, low, high)
                other = jnp.where(mine, high, low).astype(BF16)
                if len(sent) == 2:
                    sent[chip][:, columns] = other
                else:
                    sent[0][pl.ds(chip * quarter, quarter), columns] = other

    if len(blocks) == 1:
        multiply(blocks[0], *outs)
    else:
        pl.when(flags[2] == 1)(lambda: multiply(blocks[0], *outs))
        pl.when(flags[2] == 0)(lambda: multiply(blocks[1], *outs))


def product(flags, blocks, fisher, ways=2):
    half = blocks[0].shape[0] // 2
    columns = fisher.shape[1]
    sent = jax.ShapeDtypeStruct((half // ways, columns), BF16)
    return pl.pallas_call(
        functools.partial(product_body, len(blocks)),
        in_specs=[pl.BlockSpec(memory_space=pltpu.SMEM)] + [VMEM] * (len(blocks) + 1),
        out_specs=[VMEM] * (1 + ways),
        out_shape=[jax.ShapeDtypeStruct((half, columns), F32)] + [sent] * ways,
        compiler_params=PARAMS,
        cost_estimate=SMALL,
        name="product",
    )(flags, *blocks, fisher)


def fold_body(flags, kept, *refs):
    got, kept_out, sent_out = refs[:-2], refs[-2], refs[-1]
    half = kept_out.shape[0]
    first = flags[1] == 0

    @pl.loop(0, kept.shape[1] // COLUMNS)
    def _(n):
        columns = pl.ds(pl.multiple_of(n * COLUMNS, COLUMNS), COLUMNS)
        if len(got) == 2:
            low, high = got[0][:, columns], got[1][:, columns]
        else:
            low, high = got[0][:half, columns], got[0][half:, columns]
        low = kept[:half, columns] + low.astype(F32)
        high = kept[half:, columns] + high.astype(F32)
        kept_out[:, columns] = jnp.where(first, low, high)
        sent_out[:, columns] = jnp.where(first, high, low).astype(sent_out.dtype)


def fold(flags, kept, got, sent_as):
    shape = (kept.shape[0] // 2, kept.shape[1])
    return pl.pallas_call(
        fold_body,
        in_specs=[pl.BlockSpec(memory_space=pltpu.SMEM)] + [VMEM] * (1 + len(got)),
        out_specs=[VMEM, VMEM],
        out_shape=[jax.ShapeDtypeStruct(shape, F32), jax.ShapeDtypeStruct(shape, sent_as)],
        compiler_params=PARAMS,
        cost_estimate=SMALL,
        name="fold",
    )(flags, kept, *got)


def split_sum(kept, got):
    value = kept[...] + got[...].astype(F32)
    high = value.astype(BF16)
    return high, (value - high.astype(F32)).astype(BF16)


def scores_body(units, *refs):
    sums, grads, outs = refs[: 2 * units], refs[2 * units :][:4], refs[2 * units + 4 :]
    rows = sums[0].shape[0]
    precond = jnp.concatenate(
        [part for u in range(units) for part in split_sum(sums[2 * u], sums[2 * u + 1])]
    )
    for r in range(4):
        both = dot_t(grads[r][...], precond)
        for u in range(units):
            value = both[:, 2 * u * rows :][:, :rows] + both[:, (2 * u + 1) * rows :][:, :rows]
            outs[u][r] = value.astype(outs[u].dtype)


def partial_scores(units, grads, out_as):
    rows = units[0][0].shape[0]
    train_rows = grads[0].shape[0]
    return pl.pallas_call(
        lambda *refs: scores_body(len(units), *refs),
        in_specs=[VMEM] * (2 * len(units) + 4),
        out_specs=[VMEM] * len(units),
        out_shape=[jax.ShapeDtypeStruct((4, train_rows, rows), kind) for kind in out_as],
        compiler_params=PARAMS,
        cost_estimate=SMALL,
        name="scores",
    )(*[value for unit in units for value in unit], *grads)


def last_scores_body(kept, got, counts, *refs):
    grads, out = refs[:4], refs[4]
    rows = kept.shape[0]
    train_rows = grads[0].shape[0]
    precond = jnp.concatenate(split_sum(kept, got))
    chosen = jnp.zeros((1, rows), F32)
    for r in range(4):
        both = dot_t(grads[r][...], precond)
        value = both[:, :rows] + both[:, rows:]
        out[r, :train_rows] = value.astype(out.dtype)
        chosen = chosen + jnp.sum(value * counts[r], axis=0, keepdims=True)
    for r in range(4):
        out[r, train_rows:] = jnp.broadcast_to(chosen, (EXTRA, rows)).astype(out.dtype)


def last_scores(kept, got, counts, grads):
    rows = kept.shape[0]
    return pl.pallas_call(
        last_scores_body,
        in_specs=[VMEM] * 7,
        out_specs=VMEM,
        out_shape=jax.ShapeDtypeStruct((4, grads[0].shape[0] + EXTRA, rows), BF16),
        compiler_params=PARAMS,
        cost_estimate=SMALL,
        name="last_scores",
    )(kept, got, counts, *grads)


def four_by_four(train_grads, test_grads, fisher, chosen_ids):
    z = lax.axis_index("test")
    i = lax.axis_index("train")
    chip, core = i // 2, i % 2
    inner = (z == 1) | (z == 2)
    flags = jnp.stack([core, chip, inner.astype(jnp.int32)])
    own_rows = train_grads.shape[0]
    quarter = test_grads.shape[0] // 4

    def along(value, pairs):
        return lax.ppermute(value, "test", pairs)

    def to_other(value, r):
        return lax.ppermute(value, "train", [(k, k ^ r) for k in range(4)])

    def tied(*values):
        return lax.optimization_barrier(values)

    pair = [(0, 1), (1, 0), (2, 3), (3, 2)]
    middle = [(1, 2), (2, 1)]
    outward = [(1, 0), (2, 3)]
    inward = [(0, 1), (3, 2)]

    def core_sum(kept, *sent, sent_as=BF16):
        return fold(flags, kept, [to_other(part, 1) for part in sent], sent_as)

    def scores_of(*units, out_as=(BF16, BF16)):
        return partial_scores(units, grads, out_as[: len(units)])

    def straight(value, r):
        pairs = [(0, 3), (3, 0)]
        pairs = [(k * 4 + a, (k ^ r) * 4 + b) for k in range(4) for a, b in pairs]
        return lax.ppermute(value, ("train", "test"), pairs)

    def in_order(parts):
        parts = [parts[0], parts[2], parts[1], parts[3]]
        parts = [jnp.where(chip == 0, parts[q], parts[q ^ 1]) for q in range(4)]
        parts = [jnp.where(core == 0, parts[q], parts[q ^ 2]) for q in range(4)]
        return jnp.concatenate(parts, axis=1)

    row_ids = jnp.stack([i, i ^ 1, i ^ 2, i ^ 3])[:, None] * own_rows + jnp.arange(own_rows)

    def selected(ids):
        ids = lax.dynamic_slice_in_dim(ids, (core * 2 + chip) * quarter, quarter).T
        return sum((ids[k] == row_ids[:, :, None]).astype(F32) for k in range(ids.shape[0]))

    pair_in = along(test_grads, pair)
    middle_in = along(test_grads, middle)
    grads = [train_grads, to_other(train_grads, 1), to_other(train_grads, 2)]
    own, own_sent = core_sum(*product(flags, [test_grads], fisher), sent_as=F32)
    counts = selected(chosen_ids)
    far_ids = along(chosen_ids, [(0, 3), (3, 0)])
    pair_in, middle_in, own, own_sent, counts, far_ids, grads[1] = tied(
        pair_in, middle_in, own, own_sent, counts, far_ids, grads[1]
    )

    second_edge = along(middle_in, outward)
    far_in = along(pair_in, middle)
    own_got = to_other(own_sent, 2)
    near, near_sent = core_sum(*product(flags, [middle_in, pair_in], fisher))
    near_got = to_other(near_sent, 2)
    far_counts = selected(far_ids)
    grads = grads + [to_other(grads[2], 1)]
    far_in, second_edge, pair_in, own, own_got, near, near_got, far_counts, grads = tied(
        far_in, second_edge, pair_in, own, own_got, near, near_got, far_counts, grads
    )

    first_edge = along(far_in, outward)
    near, total = scores_of((near, near_got), (own, own_got), out_as=(BF16, F32))
    near_in, near_across = along(near, inward), along(near, middle)
    far_in, pair_in, near = tied(far_in, pair_in, near)
    second, second_sent = core_sum(*product(flags, [far_in, second_edge], fisher))
    third, third_sent = core_sum(*product(flags, [pair_in], fisher, 1))
    second, near_in, near_across = tied(second, near_in, near_across)
    (second,) = scores_of((second, to_other(second_sent, 2)))
    across = along(second, middle)
    (third,) = scores_of((third, to_other(third_sent, 2)), out_as=(F32,))
    first_edge, total, near_in, near_across, second, across, third, grads, far_counts = tied(
        first_edge, total, near_in, near_across, second, across, third, grads, far_counts
    )

    third = along((third + across.astype(F32)).astype(BF16), outward)
    second = along(second, [(0, 2), (3, 1)])
    last, last_sent = core_sum(*product(flags, [first_edge], fisher))
    last = last_scores(last, to_other(last_sent, 2), far_counts, grads)
    last, second, third = tied(last, second, third)
    last = in_order([straight(last[r], r) for r in range(4)])

    total = total + sum(value.astype(F32) for value in (near_in, near_across, second, third))
    chosen = jnp.sum(total * counts, axis=(0, 1))
    total = [jnp.concatenate([part, jnp.broadcast_to(chosen, (8, quarter))]) for part in total]
    total = in_order([total[0]] + [to_other(total[r], r) for r in range(1, 4)])

    scores = total[:own_rows] + last[:own_rows].astype(F32)
    return scores, total[own_rows] + last[own_rows].astype(F32)


def solution(mesh):
    sizes = (mesh.shape["train"], mesh.shape["test"])
    return jax.shard_map(
        four_by_four if sizes == (4, 4) else any_mesh,
        mesh=mesh,
        in_specs=(
            P(("groups", "train"), "test"),
            P(("groups", "test"), "train"),
            P("train", "test"),
            P(("groups", "test"), None),
        ),
        out_specs=(P(("groups", "train"), "test"), P(("groups", "test"))),
        check_vma=False,
    )
```

```python
import functools

import jax
import jax.numpy as jnp
from jax import lax
from jax.experimental import pallas as pl
from jax.experimental.pallas import tpu as pltpu
from jax.sharding import PartitionSpec as P

COLUMNS = 512
EXTRA = 16

F32 = jnp.float32
BF16 = jnp.bfloat16


def dot_t(a, b):
    return lax.dot_general(a, b, (((1,), (1,)), ((), ())), preferred_element_type=F32)


def selection_counts(chosen_ids, first_row, rows):
    row_ids = first_row + lax.broadcasted_iota(jnp.int32, (rows, chosen_ids.shape[0]), 0)
    ids = chosen_ids.T
    counts = jnp.zeros(row_ids.shape, F32)
    for k in range(ids.shape[0]):
        counts = counts + (row_ids == ids[k][None, :]).astype(F32)
    return counts


def any_mesh(train_grads, test_grads, fisher, chosen_ids):
    test_whole = lax.all_gather(test_grads, "test", axis=0, tiled=True)
    partial_value = jnp.dot(test_whole, fisher, preferred_element_type=F32)
    precond = lax.psum(partial_value, "train").astype(BF16)
    partial_scores = dot_t(train_grads, precond)
    scores = lax.psum_scatter(partial_scores, "test", scatter_dimension=1, tiled=True)
    rows = scores.shape[0]
    counts = selection_counts(chosen_ids, lax.axis_index("train") * rows, rows)
    return scores, lax.psum(jnp.sum(counts * scores, axis=0), "train")


SMALL = pl.CostEstimate(flops=1, bytes_accessed=1, transcendentals=0)
PARAMS = pltpu.CompilerParams(vmem_limit_bytes=12 * 2**20)


VMEM = pl.BlockSpec(memory_space=pltpu.VMEM)


def product_body(count, flags, *refs):
    blocks, fisher, outs = refs[:count], refs[count], refs[count + 1 :]
    quarter = blocks[0].shape[0] // 4
    mine = flags[0] == 0

    def multiply(block, kept, *sent):
        @pl.loop(0, fisher.shape[1] // COLUMNS)
        def _(n):
            columns = pl.ds(pl.multiple_of(n * COLUMNS, COLUMNS), COLUMNS)
            value = jnp.dot(block[...], fisher[:, columns], preferred_element_type=F32)
            for chip in range(2):
                low, high = (value[(2 * core + chip) * quarter :][:quarter] for core in range(2))
                kept[pl.ds(chip * quarter, quarter), columns] = jnp.where(mine, low, high)
                other = jnp.where(mine, high, low).astype(BF16)
                if len(sent) == 2:
                    sent[chip][:, columns] = other
                else:
                    sent[0][pl.ds(chip * quarter, quarter), columns] = other

    if len(blocks) == 1:
        multiply(blocks[0], *outs)
    else:
        pl.when(flags[2] == 1)(lambda: multiply(blocks[0], *outs))
        pl.when(flags[2] == 0)(lambda: multiply(blocks[1], *outs))


def product(flags, blocks, fisher, ways=2):
    half = blocks[0].shape[0] // 2
    columns = fisher.shape[1]
    sent = jax.ShapeDtypeStruct((half // ways, columns), BF16)
    return pl.pallas_call(
        functools.partial(product_body, len(blocks)),
        in_specs=[pl.BlockSpec(memory_space=pltpu.SMEM)] + [VMEM] * (len(blocks) + 1),
        out_specs=[VMEM] * (1 + ways),
        out_shape=[jax.ShapeDtypeStruct((half, columns), F32)] + [sent] * ways,
        compiler_params=PARAMS,
        cost_estimate=SMALL,
        name="product",
    )(flags, *blocks, fisher)


def fold_body(flags, kept, *refs):
    got, kept_out, sent_out = refs[:-2], refs[-2], refs[-1]
    half = kept_out.shape[0]
    first = flags[1] == 0

    @pl.loop(0, kept.shape[1] // COLUMNS)
    def _(n):
        columns = pl.ds(pl.multiple_of(n * COLUMNS, COLUMNS), COLUMNS)
        if len(got) == 2:
            low, high = got[0][:, columns], got[1][:, columns]
        else:
            low, high = got[0][:half, columns], got[0][half:, columns]
        low = kept[:half, columns] + low.astype(F32)
        high = kept[half:, columns] + high.astype(F32)
        kept_out[:, columns] = jnp.where(first, low, high)
        sent_out[:, columns] = jnp.where(first, high, low).astype(sent_out.dtype)


def fold(flags, kept, got, sent_as):
    shape = (kept.shape[0] // 2, kept.shape[1])
    return pl.pallas_call(
        fold_body,
        in_specs=[pl.BlockSpec(memory_space=pltpu.SMEM)] + [VMEM] * (1 + len(got)),
        out_specs=[VMEM, VMEM],
        out_shape=[jax.ShapeDtypeStruct(shape, F32), jax.ShapeDtypeStruct(shape, sent_as)],
        compiler_params=PARAMS,
        cost_estimate=SMALL,
        name="fold",
    )(flags, kept, *got)


def split_sum(kept, got):
    value = kept[...] + got[...].astype(F32)
    high = value.astype(BF16)
    return high, (value - high.astype(F32)).astype(BF16)


def scores_body(units, *refs):
    sums, grads, outs = refs[: 2 * units], refs[2 * units :][:4], refs[2 * units + 4 :]
    rows = sums[0].shape[0]
    precond = jnp.concatenate(
        [part for u in range(units) for part in split_sum(sums[2 * u], sums[2 * u + 1])]
    )
    for r in range(4):
        both = dot_t(grads[r][...], precond)
        for u in range(units):
            value = both[:, 2 * u * rows :][:, :rows] + both[:, (2 * u + 1) * rows :][:, :rows]
            outs[u][r] = value.astype(outs[u].dtype)


def partial_scores(units, grads, out_as):
    rows = units[0][0].shape[0]
    train_rows = grads[0].shape[0]
    return pl.pallas_call(
        lambda *refs: scores_body(len(units), *refs),
        in_specs=[VMEM] * (2 * len(units) + 4),
        out_specs=[VMEM] * len(units),
        out_shape=[jax.ShapeDtypeStruct((4, train_rows, rows), kind) for kind in out_as],
        compiler_params=PARAMS,
        cost_estimate=SMALL,
        name="scores",
    )(*[value for unit in units for value in unit], *grads)


def last_scores_body(which, kept, got, counts, before, *refs):
    grads, out, chosen_out = refs[: len(which)], refs[-2], refs[-1]
    rows = kept.shape[0]
    train_rows = grads[0].shape[0]
    precond = jnp.concatenate(split_sum(kept, got))
    chosen = before[:1]
    for n, r in enumerate(which):
        both = dot_t(grads[n][...], precond)
        value = both[:, :rows] + both[:, rows:]
        out[n, :train_rows] = value.astype(BF16)
        chosen = chosen + jnp.sum(value * counts[r], axis=0, keepdims=True)
    chosen_out[...] = jnp.broadcast_to(chosen, chosen_out.shape)
    for n in range(len(which)):
        if out.shape[1] > train_rows:
            out[n, train_rows:] = jnp.broadcast_to(chosen, (EXTRA, rows)).astype(BF16)


def last_scores(kept, got, counts, before, grads, which, extra):
    rows = kept.shape[0]
    train_rows = grads[0].shape[0]
    return pl.pallas_call(
        functools.partial(last_scores_body, which),
        in_specs=[VMEM] * (4 + len(which)),
        out_specs=[VMEM, VMEM],
        out_shape=[
            jax.ShapeDtypeStruct((len(which), train_rows + extra, rows), BF16),
            jax.ShapeDtypeStruct((8, rows), F32),
        ],
        compiler_params=PARAMS,
        cost_estimate=SMALL,
        name="last_scores",
    )(kept, got, counts, before, *[grads[r] for r in which])


def four_by_four(train_grads, test_grads, fisher, chosen_ids):
    z = lax.axis_index("test")
    i = lax.axis_index("train")
    chip, core = i // 2, i % 2
    inner = (z == 1) | (z == 2)
    flags = jnp.stack([core, chip, inner.astype(jnp.int32)])
    own_rows = train_grads.shape[0]
    quarter = test_grads.shape[0] // 4

    def along(value, pairs):
        return lax.ppermute(value, "test", pairs)

    def to_other(value, r):
        return lax.ppermute(value, "train", [(k, k ^ r) for k in range(4)])

    def tied(*values):
        return lax.optimization_barrier(values)

    pair = [(0, 1), (1, 0), (2, 3), (3, 2)]
    middle = [(1, 2), (2, 1)]
    outward = [(1, 0), (2, 3)]
    inward = [(0, 1), (3, 2)]

    def core_sum(kept, *sent, sent_as=BF16):
        return fold(flags, kept, [to_other(part, 1) for part in sent], sent_as)

    def scores_of(*units, out_as=(BF16, BF16)):
        return partial_scores(units, grads, out_as[: len(units)])

    def in_order(parts):
        parts = [parts[0], parts[2], parts[1], parts[3]]
        parts = [jnp.where(chip == 0, parts[q], parts[q ^ 1]) for q in range(4)]
        parts = [jnp.where(core == 0, parts[q], parts[q ^ 2]) for q in range(4)]
        return jnp.concatenate(parts, axis=1)

    row_ids = jnp.stack([i, i ^ 1, i ^ 2, i ^ 3])[:, None] * own_rows + jnp.arange(own_rows)

    def selected(ids):
        ids = lax.dynamic_slice_in_dim(ids, (core * 2 + chip) * quarter, quarter).T
        return sum((ids[k] == row_ids[:, :, None]).astype(F32) for k in range(ids.shape[0]))

    pair_in = along(test_grads, pair)
    middle_in = along(test_grads, middle)
    grads = [train_grads, to_other(train_grads, 1), to_other(train_grads, 2)]
    own, own_sent = core_sum(*product(flags, [test_grads], fisher), sent_as=F32)
    counts = selected(chosen_ids)
    far_ids = along(chosen_ids, [(0, 3), (3, 0)])
    pair_in, middle_in, own, own_sent, counts, far_ids, grads[1] = tied(
        pair_in, middle_in, own, own_sent, counts, far_ids, grads[1]
    )

    second_edge = along(middle_in, outward)
    far_in = along(pair_in, middle)
    near, near_sent = core_sum(*product(flags, [middle_in, pair_in], fisher))
    near_sent, own_sent = tied(near_sent, own_sent)
    near_got = to_other(near_sent, 2)
    own_got = to_other(own_sent, 2)
    far_counts = selected(far_ids)
    grads = grads + [to_other(grads[2], 1)]
    (near,) = scores_of((near, near_got))
    far_in, second_edge, pair_in, own, own_got, near, far_counts, grads = tied(
        far_in, second_edge, pair_in, own, own_got, near, far_counts, grads
    )

    first_edge = along(far_in, outward)
    near_in, near_across = along(near, inward), along(near, middle)
    second, second_sent = core_sum(*product(flags, [far_in, second_edge], fisher))
    second_sent, pair_in = tied(second_sent, pair_in)
    third, third_sent = core_sum(*product(flags, [pair_in], fisher))
    second, near_in, near_across = tied(second, near_in, near_across)
    (second,) = scores_of((second, to_other(second_sent, 2)))
    across = along(second, middle)
    third, total = scores_of(
        (third, to_other(third_sent, 2)), (own, own_got), out_as=(F32, F32)
    )
    first_edge, total, near_in, near_across, second, across, third, grads, far_counts = tied(
        first_edge, total, near_in, near_across, second, across, third, grads, far_counts
    )

    third = along((third + across.astype(F32)).astype(BF16), outward)
    second = along(second, [(0, 2), (3, 1)])
    last, last_sent = core_sum(*product(flags, [first_edge], fisher))
    last_got = to_other(last_sent, 2)
    ends = [(0, 3), (3, 0)]
    none = jnp.zeros((8, quarter), F32)
    away, chosen = last_scores(last, last_got, far_counts, none, grads, (2, 3), 0)
    away = along(away, ends)
    away = [to_other(away[0], 2), to_other(away[1], 3)]
    here, _ = last_scores(last, last_got, far_counts, chosen, grads, (0, 1), EXTRA)
    here, second, third = tied(here, second, third)
    here = along(here, ends)
    here = [here[0], to_other(here[1], 1)]
    chosen = [part[own_rows:] for part in here]
    chosen += [to_other(chosen[0], 2), to_other(chosen[0], 3)]
    last = in_order([part[:own_rows] for part in here] + away)
    last_chosen = in_order(chosen)[0]

    total = total + sum(value.astype(F32) for value in (near_in, near_across, second, third))
    chosen = jnp.sum(total * counts, axis=(0, 1))
    total = [jnp.concatenate([part, jnp.broadcast_to(chosen, (8, quarter))]) for part in total]
    total = in_order([total[0]] + [to_other(total[r], r) for r in range(1, 4)])

    scores = total[:own_rows] + last.astype(F32)
    return scores, total[own_rows] + last_chosen.astype(F32)


def solution(mesh):
    sizes = (mesh.shape["train"], mesh.shape["test"])
    return jax.shard_map(
        four_by_four if sizes == (4, 4) else any_mesh,
        mesh=mesh,
        in_specs=(
            P(("groups", "train"), "test"),
            P(("groups", "test"), "train"),
            P("train", "test"),
            P(("groups", "test"), None),
        ),
        out_specs=(P(("groups", "train"), "test"), P(("groups", "test"))),
        check_vma=False,
    )
```

```python
import functools

import jax
import jax.numpy as jnp
from jax import lax
from jax.experimental import pallas as pl
from jax.experimental.pallas import tpu as pltpu
from jax.sharding import PartitionSpec as P

COLUMNS = 512
EXTRA = 16

F32 = jnp.float32
BF16 = jnp.bfloat16


def dot_t(a, b):
    return lax.dot_general(a, b, (((1,), (1,)), ((), ())), preferred_element_type=F32)


def selection_counts(chosen_ids, first_row, rows):
    row_ids = first_row + lax.broadcasted_iota(jnp.int32, (rows, chosen_ids.shape[0]), 0)
    ids = chosen_ids.T
    counts = jnp.zeros(row_ids.shape, F32)
    for k in range(ids.shape[0]):
        counts = counts + (row_ids == ids[k][None, :]).astype(F32)
    return counts


def any_mesh(train_grads, test_grads, fisher, chosen_ids):
    test_whole = lax.all_gather(test_grads, "test", axis=0, tiled=True)
    partial_value = jnp.dot(test_whole, fisher, preferred_element_type=F32)
    precond = lax.psum(partial_value, "train").astype(BF16)
    partial_scores = dot_t(train_grads, precond)
    scores = lax.psum_scatter(partial_scores, "test", scatter_dimension=1, tiled=True)
    rows = scores.shape[0]
    counts = selection_counts(chosen_ids, lax.axis_index("train") * rows, rows)
    return scores, lax.psum(jnp.sum(counts * scores, axis=0), "train")


SMALL = pl.CostEstimate(flops=1, bytes_accessed=1, transcendentals=0)
SOME = pl.CostEstimate(flops=2 * 10**9, bytes_accessed=2**20, transcendentals=0)
PARAMS = pltpu.CompilerParams(vmem_limit_bytes=12 * 2**20)


VMEM = pl.BlockSpec(memory_space=pltpu.VMEM)


def product_body(count, flags, *refs):
    blocks, fisher, outs = refs[:count], refs[count], refs[count + 1 :]
    quarter = blocks[0].shape[0] // 4
    mine = flags[0] == 0

    def multiply(block, kept, *sent):
        @pl.loop(0, fisher.shape[1] // COLUMNS)
        def _(n):
            columns = pl.ds(pl.multiple_of(n * COLUMNS, COLUMNS), COLUMNS)
            value = jnp.dot(block[...], fisher[:, columns], preferred_element_type=F32)
            for chip in range(2):
                low, high = (value[(2 * core + chip) * quarter :][:quarter] for core in range(2))
                kept[pl.ds(chip * quarter, quarter), columns] = jnp.where(mine, low, high)
                other = jnp.where(mine, high, low).astype(BF16)
                if len(sent) == 2:
                    sent[chip][:, columns] = other
                else:
                    sent[0][pl.ds(chip * quarter, quarter), columns] = other

    if len(blocks) == 1:
        multiply(blocks[0], *outs)
    else:
        pl.when(flags[2] == 1)(lambda: multiply(blocks[0], *outs))
        pl.when(flags[2] == 0)(lambda: multiply(blocks[1], *outs))


def product(flags, blocks, fisher, ways=2):
    half = blocks[0].shape[0] // 2
    columns = fisher.shape[1]
    sent = jax.ShapeDtypeStruct((half // ways, columns), BF16)
    return pl.pallas_call(
        functools.partial(product_body, len(blocks)),
        in_specs=[pl.BlockSpec(memory_space=pltpu.SMEM)] + [VMEM] * (len(blocks) + 1),
        out_specs=[VMEM] * (1 + ways),
        out_shape=[jax.ShapeDtypeStruct((half, columns), F32)] + [sent] * ways,
        compiler_params=PARAMS,
        cost_estimate=SMALL,
        name="product",
    )(flags, *blocks, fisher)


def fold_body(flags, kept, *refs):
    got, kept_out, sent_out = refs[:-2], refs[-2], refs[-1]
    half = kept_out.shape[0]
    first = flags[1] == 0

    @pl.loop(0, kept.shape[1] // COLUMNS)
    def _(n):
        columns = pl.ds(pl.multiple_of(n * COLUMNS, COLUMNS), COLUMNS)
        if len(got) == 2:
            low, high = got[0][:, columns], got[1][:, columns]
        else:
            low, high = got[0][:half, columns], got[0][half:, columns]
        low = kept[:half, columns] + low.astype(F32)
        high = kept[half:, columns] + high.astype(F32)
        kept_out[:, columns] = jnp.where(first, low, high)
        sent_out[:, columns] = jnp.where(first, high, low).astype(sent_out.dtype)


def fold(flags, kept, got, sent_as):
    shape = (kept.shape[0] // 2, kept.shape[1])
    return pl.pallas_call(
        fold_body,
        in_specs=[pl.BlockSpec(memory_space=pltpu.SMEM)] + [VMEM] * (1 + len(got)),
        out_specs=[VMEM, VMEM],
        out_shape=[jax.ShapeDtypeStruct(shape, F32), jax.ShapeDtypeStruct(shape, sent_as)],
        compiler_params=PARAMS,
        cost_estimate=SMALL,
        name="fold",
    )(flags, kept, *got)


def split_sum(kept, got):
    value = kept[...] + got[...].astype(F32)
    high = value.astype(BF16)
    return high, (value - high.astype(F32)).astype(BF16)


def scores_body(units, *refs):
    sums, grads, outs = refs[: 2 * units], refs[2 * units :][:4], refs[2 * units + 4 :]
    rows = sums[0].shape[0]
    precond = jnp.concatenate(
        [part for u in range(units) for part in split_sum(sums[2 * u], sums[2 * u + 1])]
    )
    for r in range(4):
        both = dot_t(grads[r][...], precond)
        for u in range(units):
            value = both[:, 2 * u * rows :][:, :rows] + both[:, (2 * u + 1) * rows :][:, :rows]
            outs[u][r] = value.astype(outs[u].dtype)


def partial_scores(units, grads, out_as, cost):
    rows = units[0][0].shape[0]
    train_rows = grads[0].shape[0]
    return pl.pallas_call(
        lambda *refs: scores_body(len(units), *refs),
        in_specs=[VMEM] * (2 * len(units) + 4),
        out_specs=[VMEM] * len(units),
        out_shape=[jax.ShapeDtypeStruct((4, train_rows, rows), kind) for kind in out_as],
        compiler_params=PARAMS,
        cost_estimate=cost,
        name="scores",
    )(*[value for unit in units for value in unit], *grads)


def last_scores_body(which, kept, got, counts, before, *refs):
    grads, out, chosen_out = refs[: len(which)], refs[-2], refs[-1]
    rows = kept.shape[0]
    train_rows = grads[0].shape[0]
    precond = jnp.concatenate(split_sum(kept, got))
    chosen = before[:1]
    for n, r in enumerate(which):
        both = dot_t(grads[n][...], precond)
        value = both[:, :rows] + both[:, rows:]
        out[n, :train_rows] = value.astype(BF16)
        chosen = chosen + jnp.sum(value * counts[r], axis=0, keepdims=True)
    chosen_out[...] = jnp.broadcast_to(chosen, chosen_out.shape)
    for n in range(len(which)):
        if out.shape[1] > train_rows:
            out[n, train_rows:] = jnp.broadcast_to(chosen, (EXTRA, rows)).astype(BF16)


def last_scores(kept, got, counts, before, grads, which, extra):
    rows = kept.shape[0]
    train_rows = grads[0].shape[0]
    return pl.pallas_call(
        functools.partial(last_scores_body, which),
        in_specs=[VMEM] * (4 + len(which)),
        out_specs=[VMEM, VMEM],
        out_shape=[
            jax.ShapeDtypeStruct((len(which), train_rows + extra, rows), BF16),
            jax.ShapeDtypeStruct((8, rows), F32),
        ],
        compiler_params=PARAMS,
        cost_estimate=SMALL,
        name="last_scores",
    )(kept, got, counts, before, *[grads[r] for r in which])


def four_by_four(train_grads, test_grads, fisher, chosen_ids):
    z = lax.axis_index("test")
    i = lax.axis_index("train")
    chip, core = i // 2, i % 2
    inner = (z == 1) | (z == 2)
    flags = jnp.stack([core, chip, inner.astype(jnp.int32)])
    own_rows = train_grads.shape[0]
    quarter = test_grads.shape[0] // 4

    def along(value, pairs):
        return lax.ppermute(value, "test", pairs)

    def to_other(value, r):
        return lax.ppermute(value, "train", [(k, k ^ r) for k in range(4)])

    def tied(*values):
        return lax.optimization_barrier(values)

    pair = [(0, 1), (1, 0), (2, 3), (3, 2)]
    middle = [(1, 2), (2, 1)]
    outward = [(1, 0), (2, 3)]
    inward = [(0, 1), (3, 2)]

    def core_sum(kept, *sent, sent_as=BF16):
        return fold(flags, kept, [to_other(part, 1) for part in sent], sent_as)

    def scores_of(*units, out_as=(BF16, BF16), cost=SMALL):
        return partial_scores(units, grads, out_as[: len(units)], cost)

    def in_order(parts):
        parts = [parts[0], parts[2], parts[1], parts[3]]
        parts = [jnp.where(chip == 0, parts[q], parts[q ^ 1]) for q in range(4)]
        parts = [jnp.where(core == 0, parts[q], parts[q ^ 2]) for q in range(4)]
        return jnp.concatenate(parts, axis=1)

    row_ids = jnp.stack([i, i ^ 1, i ^ 2, i ^ 3])[:, None] * own_rows + jnp.arange(own_rows)

    def selected(ids):
        ids = lax.dynamic_slice_in_dim(ids, (core * 2 + chip) * quarter, quarter).T
        return sum((ids[k] == row_ids[:, :, None]).astype(F32) for k in range(ids.shape[0]))

    pair_in = along(test_grads, pair)
    middle_in = along(test_grads, middle)
    grads = [train_grads, to_other(train_grads, 1), to_other(train_grads, 2)]
    own, own_sent = core_sum(*product(flags, [test_grads], fisher), sent_as=F32)
    counts = selected(chosen_ids)
    pair_in, middle_in, own, own_sent, counts, chosen_ids, grads[1] = tied(
        pair_in, middle_in, own, own_sent, counts, chosen_ids, grads[1]
    )

    second_edge = along(middle_in, outward)
    far_in = along(pair_in, middle)
    grads = grads + [to_other(grads[2], 1)]
    near, near_sent = core_sum(*product(flags, [middle_in, pair_in], fisher))
    own_got = to_other(own_sent, 2)
    near_sent, own_got, pair_in, grads[3] = tied(near_sent, own_got, pair_in, grads[3])
    near_got = to_other(near_sent, 2)
    third, third_sent = core_sum(*product(flags, [pair_in], fisher))
    (near,) = scores_of((near, near_got), cost=SOME)
    far_ids = along(chosen_ids, [(0, 3), (3, 0)])
    far_in, second_edge, third, third_sent, own, own_got, near, far_ids, grads = tied(
        far_in, second_edge, third, third_sent, own, own_got, near, far_ids, grads
    )

    first_edge = along(far_in, outward)
    second, second_sent = core_sum(*product(flags, [far_in, second_edge], fisher))
    second, second_sent, near = tied(second, second_sent, near)
    second_got = to_other(second_sent, 2)
    near_in, near_across = along(near, inward), along(near, middle)
    second_got, near_in, near_across = tied(second_got, near_in, near_across)
    (second,) = scores_of((second, second_got))
    across = along(second, middle)
    third, total = scores_of(
        (third, to_other(third_sent, 2)), (own, own_got), out_as=(F32, F32)
    )
    far_counts = selected(far_ids)
    first_edge, total, near_in, near_across, second, across, third, grads, far_counts = tied(
        first_edge, total, near_in, near_across, second, across, third, grads, far_counts
    )

    third = along((third + across.astype(F32)).astype(BF16), outward)
    second = along(second, [(0, 2), (3, 1)])
    last, last_sent = core_sum(*product(flags, [first_edge], fisher))
    last_got = to_other(last_sent, 2)
    ends = [(0, 3), (3, 0)]
    none = jnp.zeros((8, quarter), F32)
    away, chosen = last_scores(last, last_got, far_counts, none, grads, (2, 3), 0)
    away = along(away, ends)
    away = [to_other(away[0], 2), to_other(away[1], 3)]
    here, _ = last_scores(last, last_got, far_counts, chosen, grads, (0, 1), EXTRA)
    here, second, third = tied(here, second, third)
    here = along(here, ends)
    here = [here[0], to_other(here[1], 1)]
    chosen = [part[own_rows:] for part in here]
    chosen += [to_other(chosen[0], 2), to_other(chosen[0], 3)]
    last = in_order([part[:own_rows] for part in here] + away)
    last_chosen = in_order(chosen)[0]

    total = total + sum(value.astype(F32) for value in (near_in, near_across, second, third))
    chosen = jnp.sum(total * counts, axis=(0, 1))
    total = [jnp.concatenate([part, jnp.broadcast_to(chosen, (8, quarter))]) for part in total]
    total = in_order([total[0]] + [to_other(total[r], r) for r in range(1, 4)])

    scores = total[:own_rows] + last.astype(F32)
    return scores, total[own_rows] + last_chosen.astype(F32)


def solution(mesh):
    sizes = (mesh.shape["train"], mesh.shape["test"])
    return jax.shard_map(
        four_by_four if sizes == (4, 4) else any_mesh,
        mesh=mesh,
        in_specs=(
            P(("groups", "train"), "test"),
            P(("groups", "test"), "train"),
            P("train", "test"),
            P(("groups", "test"), None),
        ),
        out_specs=(P(("groups", "train"), "test"), P(("groups", "test"))),
        check_vma=False,
    )
```

```python
import functools

import jax
import jax.numpy as jnp
from jax import lax
from jax.experimental import pallas as pl
from jax.experimental.pallas import tpu as pltpu
from jax.sharding import PartitionSpec as P

COLUMNS = 512
EXTRA = 16

F32 = jnp.float32
BF16 = jnp.bfloat16


def dot_t(a, b):
    return lax.dot_general(a, b, (((1,), (1,)), ((), ())), preferred_element_type=F32)


def selection_counts(chosen_ids, first_row, rows):
    row_ids = first_row + lax.broadcasted_iota(jnp.int32, (rows, chosen_ids.shape[0]), 0)
    ids = chosen_ids.T
    counts = jnp.zeros(row_ids.shape, F32)
    for k in range(ids.shape[0]):
        counts = counts + (row_ids == ids[k][None, :]).astype(F32)
    return counts


def any_mesh(train_grads, test_grads, fisher, chosen_ids):
    test_whole = lax.all_gather(test_grads, "test", axis=0, tiled=True)
    partial_value = jnp.dot(test_whole, fisher, preferred_element_type=F32)
    precond = lax.psum(partial_value, "train").astype(BF16)
    partial_scores = dot_t(train_grads, precond)
    scores = lax.psum_scatter(partial_scores, "test", scatter_dimension=1, tiled=True)
    rows = scores.shape[0]
    counts = selection_counts(chosen_ids, lax.axis_index("train") * rows, rows)
    return scores, lax.psum(jnp.sum(counts * scores, axis=0), "train")


SMALL = pl.CostEstimate(flops=1, bytes_accessed=1, transcendentals=0)
SOME = pl.CostEstimate(flops=2 * 10**9, bytes_accessed=2**20, transcendentals=0)
MORE = pl.CostEstimate(flops=5 * 10**9, bytes_accessed=2**20, transcendentals=0)
PARAMS = pltpu.CompilerParams(vmem_limit_bytes=12 * 2**20)


VMEM = pl.BlockSpec(memory_space=pltpu.VMEM)


def product_body(count, flags, *refs):
    blocks, fisher, outs = refs[:count], refs[count], refs[count + 1 :]
    quarter = blocks[0].shape[0] // 4
    mine = flags[0] == 0

    def multiply(block, kept, *sent):
        @pl.loop(0, fisher.shape[1] // COLUMNS)
        def _(n):
            columns = pl.ds(pl.multiple_of(n * COLUMNS, COLUMNS), COLUMNS)
            value = jnp.dot(block[...], fisher[:, columns], preferred_element_type=F32)
            for chip in range(2):
                low, high = (value[(2 * core + chip) * quarter :][:quarter] for core in range(2))
                kept[pl.ds(chip * quarter, quarter), columns] = jnp.where(mine, low, high)
                other = jnp.where(mine, high, low).astype(BF16)
                if len(sent) == 2:
                    sent[chip][:, columns] = other
                else:
                    sent[0][pl.ds(chip * quarter, quarter), columns] = other

    if len(blocks) == 1:
        multiply(blocks[0], *outs)
    else:
        pl.when(flags[2] == 1)(lambda: multiply(blocks[0], *outs))
        pl.when(flags[2] == 0)(lambda: multiply(blocks[1], *outs))


def product(flags, blocks, fisher, ways=2):
    half = blocks[0].shape[0] // 2
    columns = fisher.shape[1]
    sent = jax.ShapeDtypeStruct((half // ways, columns), BF16)
    return pl.pallas_call(
        functools.partial(product_body, len(blocks)),
        in_specs=[pl.BlockSpec(memory_space=pltpu.SMEM)] + [VMEM] * (len(blocks) + 1),
        out_specs=[VMEM] * (1 + ways),
        out_shape=[jax.ShapeDtypeStruct((half, columns), F32)] + [sent] * ways,
        compiler_params=PARAMS,
        cost_estimate=SMALL,
        name="product",
    )(flags, *blocks, fisher)


def fold_body(flags, kept, *refs):
    got, kept_out, sent_out = refs[:-2], refs[-2], refs[-1]
    half = kept_out.shape[0]
    first = flags[1] == 0

    @pl.loop(0, kept.shape[1] // COLUMNS)
    def _(n):
        columns = pl.ds(pl.multiple_of(n * COLUMNS, COLUMNS), COLUMNS)
        if len(got) == 2:
            low, high = got[0][:, columns], got[1][:, columns]
        else:
            low, high = got[0][:half, columns], got[0][half:, columns]
        low = kept[:half, columns] + low.astype(F32)
        high = kept[half:, columns] + high.astype(F32)
        kept_out[:, columns] = jnp.where(first, low, high)
        sent_out[:, columns] = jnp.where(first, high, low).astype(sent_out.dtype)


def fold(flags, kept, got, sent_as, cost):
    shape = (kept.shape[0] // 2, kept.shape[1])
    return pl.pallas_call(
        fold_body,
        in_specs=[pl.BlockSpec(memory_space=pltpu.SMEM)] + [VMEM] * (1 + len(got)),
        out_specs=[VMEM, VMEM],
        out_shape=[jax.ShapeDtypeStruct(shape, F32), jax.ShapeDtypeStruct(shape, sent_as)],
        compiler_params=PARAMS,
        cost_estimate=cost,
        name="fold",
    )(flags, kept, *got)


def split_sum(kept, got):
    value = kept[...] + got[...].astype(F32)
    high = value.astype(BF16)
    return high, (value - high.astype(F32)).astype(BF16)


def scores_body(places, units, *refs):
    sums, grads, outs = refs[: 2 * units], refs[2 * units :][: len(places)], refs[-units:]
    rows = sums[0].shape[0]
    precond = jnp.concatenate(
        [part for u in range(units) for part in split_sum(sums[2 * u], sums[2 * u + 1])]
    )
    for grad, (r, first) in zip(grads, places):
        both = dot_t(grad[...], precond)
        for u in range(units):
            value = both[:, 2 * u * rows :][:, :rows] + both[:, (2 * u + 1) * rows :][:, :rows]
            outs[u][r, first : first + grad.shape[0]] = value.astype(outs[u].dtype)


def partial_scores(units, grads, out_as, cost):
    rows = units[0][0].shape[0]
    train_rows = grads[0][2].shape[0]
    return pl.pallas_call(
        functools.partial(scores_body, [piece[:2] for piece in grads], len(units)),
        in_specs=[VMEM] * (2 * len(units) + len(grads)),
        out_specs=[VMEM] * len(units),
        out_shape=[jax.ShapeDtypeStruct((4, train_rows, rows), kind) for kind in out_as],
        compiler_params=PARAMS,
        cost_estimate=cost,
        name="scores",
    )(*[value for unit in units for value in unit], *[piece[2] for piece in grads])


def last_scores_body(places, kept, got, counts, before, *refs):
    grads, out, chosen_out = refs[: len(places)], refs[-2], refs[-1]
    rows = kept.shape[0]
    low = places[0][0]
    train_rows = counts.shape[1]
    precond = jnp.concatenate(split_sum(kept, got))
    chosen = before[:1]
    for grad, (r, first) in zip(grads, places):
        both = dot_t(grad[...], precond)
        value = both[:, :rows] + both[:, rows:]
        place = pl.ds(first, grad.shape[0])
        out[r - low, place] = value.astype(BF16)
        chosen = chosen + jnp.sum(value * counts[r, place], axis=0, keepdims=True)
    chosen_out[...] = jnp.broadcast_to(chosen, chosen_out.shape)
    for n in range(2):
        if out.shape[1] > train_rows:
            out[n, train_rows:] = jnp.broadcast_to(chosen, (EXTRA, rows)).astype(BF16)


def last_scores(kept, got, counts, before, grads, extra):
    rows = kept.shape[0]
    return pl.pallas_call(
        functools.partial(last_scores_body, [piece[:2] for piece in grads]),
        in_specs=[VMEM] * (4 + len(grads)),
        out_specs=[VMEM, VMEM],
        out_shape=[
            jax.ShapeDtypeStruct((2, counts.shape[1] + extra, rows), BF16),
            jax.ShapeDtypeStruct((8, rows), F32),
        ],
        compiler_params=PARAMS,
        cost_estimate=SMALL,
        name="last_scores",
    )(kept, got, counts, before, *[piece[2] for piece in grads])


def four_by_four(train_grads, test_grads, fisher, chosen_ids):
    z = lax.axis_index("test")
    i = lax.axis_index("train")
    chip, core = i // 2, i % 2
    inner = (z == 1) | (z == 2)
    flags = jnp.stack([core, chip, inner.astype(jnp.int32)])
    own_rows = train_grads.shape[0]
    quarter = test_grads.shape[0] // 4

    def along(value, pairs):
        return lax.ppermute(value, "test", pairs)

    def to_other(value, r):
        return lax.ppermute(value, "train", [(k, k ^ r) for k in range(4)])

    def tied(*values):
        return lax.optimization_barrier(values)

    pair = [(0, 1), (1, 0), (2, 3), (3, 2)]
    middle = [(1, 2), (2, 1)]
    outward = [(1, 0), (2, 3)]
    inward = [(0, 1), (3, 2)]

    def core_sum(kept, *sent, sent_as=BF16, cost=SMALL):
        return fold(flags, kept, [to_other(part, 1) for part in sent], sent_as, cost)

    def scores_of(*units, out_as=(BF16, BF16), cost=SMALL):
        pieces = [(*place, grad) for place, grad in zip(places, grads)]
        return partial_scores(units, pieces, out_as[: len(units)], cost)

    def in_order(parts):
        parts = [parts[0], parts[2], parts[1], parts[3]]
        parts = [jnp.where(chip == 0, parts[q], parts[q ^ 1]) for q in range(4)]
        parts = [jnp.where(core == 0, parts[q], parts[q ^ 2]) for q in range(4)]
        return jnp.concatenate(parts, axis=1)

    row_ids = jnp.stack([i, i ^ 1, i ^ 2, i ^ 3])[:, None] * own_rows + jnp.arange(own_rows)

    def selected(ids):
        ids = lax.dynamic_slice_in_dim(ids, (core * 2 + chip) * quarter, quarter).T
        return sum((ids[k] == row_ids[:, :, None]).astype(F32) for k in range(ids.shape[0]))

    pair_in = along(test_grads, pair)
    middle_in = along(test_grads, middle)
    other_core, other_chip = to_other(train_grads, 1), to_other(train_grads, 2)
    own, other_core = tied(test_grads, other_core)
    own, own_sent = core_sum(*product(flags, [own], fisher), sent_as=F32, cost=MORE)
    counts = selected(chosen_ids)
    half = own_rows // 2
    other_both = [to_other(other_chip[:half], 1), to_other(other_chip[half:], 1)]
    grads = [train_grads, other_core, other_chip, *other_both]
    pair_in, middle_in, own, own_sent, counts, chosen_ids, grads = tied(
        pair_in, middle_in, own, own_sent, counts, chosen_ids, grads
    )
    places = ((0, 0), (1, 0), (2, 0), (3, 0), (3, half))

    second_edge = along(middle_in, outward)
    far_in = along(pair_in, middle)
    near, near_sent = core_sum(*product(flags, [middle_in, pair_in], fisher))
    own_got = to_other(own_sent, 2)
    near_sent, own_got, pair_in = tied(near_sent, own_got, pair_in)
    near_got = to_other(near_sent, 2)
    third, third_sent = core_sum(*product(flags, [pair_in], fisher))
    (near,) = scores_of((near, near_got), cost=SOME)
    far_ids = along(chosen_ids, [(0, 3), (3, 0)])
    far_in, second_edge, third, third_sent, own, own_got, near, far_ids, grads = tied(
        far_in, second_edge, third, third_sent, own, own_got, near, far_ids, grads
    )

    first_edge = along(far_in, outward)
    second, second_sent = core_sum(*product(flags, [far_in, second_edge], fisher))
    second, second_sent, near = tied(second, second_sent, near)
    second_got = to_other(second_sent, 2)
    near_in, near_across = along(near, inward), along(near, middle)
    second_got, near_in, near_across = tied(second_got, near_in, near_across)
    (second,) = scores_of((second, second_got))
    across = along(second, middle)
    third, total = scores_of(
        (third, to_other(third_sent, 2)), (own, own_got), out_as=(F32, F32)
    )
    far_counts = selected(far_ids)
    first_edge, total, near_in, near_across, second, across, third, grads, far_counts = tied(
        first_edge, total, near_in, near_across, second, across, third, grads, far_counts
    )

    third = along((third + across.astype(F32)).astype(BF16), outward)
    second = along(second, [(0, 2), (3, 1)])
    last, last_sent = core_sum(*product(flags, [first_edge], fisher))
    last_got = to_other(last_sent, 2)
    ends = [(0, 3), (3, 0)]
    none = jnp.zeros((8, quarter), F32)
    pieces = [(*place, grad) for place, grad in zip(places, grads)]
    away, chosen = last_scores(last, last_got, far_counts, none, pieces[2:], 0)
    away = along(away, ends)
    away = [to_other(away[0], 2), to_other(away[1], 3)]
    here, _ = last_scores(last, last_got, far_counts, chosen, pieces[:2], EXTRA)
    here, second, third = tied(here, second, third)
    here = along(here, ends)
    here = [here[0], to_other(here[1], 1)]
    chosen = [part[own_rows:] for part in here]
    chosen += [to_other(chosen[0], 2), to_other(chosen[0], 3)]
    last = in_order([part[:own_rows] for part in here] + away)
    last_chosen = in_order(chosen)[0]

    total = total + sum(value.astype(F32) for value in (near_in, near_across, second, third))
    chosen = jnp.sum(total * counts, axis=(0, 1))
    total = [jnp.concatenate([part, jnp.broadcast_to(chosen, (8, quarter))]) for part in total]
    total = in_order([total[0]] + [to_other(total[r], r) for r in range(1, 4)])

    scores = total[:own_rows] + last.astype(F32)
    return scores, total[own_rows] + last_chosen.astype(F32)


def solution(mesh):
    sizes = (mesh.shape["train"], mesh.shape["test"])
    return jax.shard_map(
        four_by_four if sizes == (4, 4) else any_mesh,
        mesh=mesh,
        in_specs=(
            P(("groups", "train"), "test"),
            P(("groups", "test"), "train"),
            P("train", "test"),
            P(("groups", "test"), None),
        ),
        out_specs=(P(("groups", "train"), "test"), P(("groups", "test"))),
        check_vma=False,
    )
```

```python
import functools

import jax
import jax.numpy as jnp
from jax import lax
from jax.experimental import pallas as pl
from jax.experimental.pallas import tpu as pltpu
from jax.sharding import PartitionSpec as P

COLUMNS = 512
EXTRA = 16

F32 = jnp.float32
BF16 = jnp.bfloat16


def dot_t(a, b):
    return lax.dot_general(a, b, (((1,), (1,)), ((), ())), preferred_element_type=F32)


def selection_counts(chosen_ids, first_row, rows):
    row_ids = first_row + lax.broadcasted_iota(jnp.int32, (rows, chosen_ids.shape[0]), 0)
    ids = chosen_ids.T
    counts = jnp.zeros(row_ids.shape, F32)
    for k in range(ids.shape[0]):
        counts = counts + (row_ids == ids[k][None, :]).astype(F32)
    return counts


def any_mesh(train_grads, test_grads, fisher, chosen_ids):
    test_whole = lax.all_gather(test_grads, "test", axis=0, tiled=True)
    partial_value = jnp.dot(test_whole, fisher, preferred_element_type=F32)
    precond = lax.psum(partial_value, "train").astype(BF16)
    partial_scores = dot_t(train_grads, precond)
    scores = lax.psum_scatter(partial_scores, "test", scatter_dimension=1, tiled=True)
    rows = scores.shape[0]
    counts = selection_counts(chosen_ids, lax.axis_index("train") * rows, rows)
    return scores, lax.psum(jnp.sum(counts * scores, axis=0), "train")


SMALL = pl.CostEstimate(flops=1, bytes_accessed=1, transcendentals=0)
SOME = pl.CostEstimate(flops=2 * 10**9, bytes_accessed=2**20, transcendentals=0)
MORE = pl.CostEstimate(flops=7 * 10**9, bytes_accessed=2**20, transcendentals=0)
PARAMS = pltpu.CompilerParams(vmem_limit_bytes=12 * 2**20)


VMEM = pl.BlockSpec(memory_space=pltpu.VMEM)


def product_body(count, flags, *refs):
    blocks, fisher, outs = refs[:count], refs[count], refs[count + 1 :]
    quarter = blocks[0].shape[0] // 4
    mine = flags[0] == 0

    def multiply(block, kept, *sent):
        @pl.loop(0, fisher.shape[1] // COLUMNS)
        def _(n):
            columns = pl.ds(pl.multiple_of(n * COLUMNS, COLUMNS), COLUMNS)
            value = jnp.dot(block[...], fisher[:, columns], preferred_element_type=F32)
            for chip in range(2):
                low, high = (value[(2 * core + chip) * quarter :][:quarter] for core in range(2))
                kept[pl.ds(chip * quarter, quarter), columns] = jnp.where(mine, low, high)
                other = jnp.where(mine, high, low).astype(BF16)
                if len(sent) == 2:
                    sent[chip][:, columns] = other
                else:
                    sent[0][pl.ds(chip * quarter, quarter), columns] = other

    if len(blocks) == 1:
        multiply(blocks[0], *outs)
    else:
        pl.when(flags[2] == 1)(lambda: multiply(blocks[0], *outs))
        pl.when(flags[2] == 0)(lambda: multiply(blocks[1], *outs))


def product(flags, blocks, fisher, ways=2):
    half = blocks[0].shape[0] // 2
    columns = fisher.shape[1]
    sent = jax.ShapeDtypeStruct((half // ways, columns), BF16)
    return pl.pallas_call(
        functools.partial(product_body, len(blocks)),
        in_specs=[pl.BlockSpec(memory_space=pltpu.SMEM)] + [VMEM] * (len(blocks) + 1),
        out_specs=[VMEM] * (1 + ways),
        out_shape=[jax.ShapeDtypeStruct((half, columns), F32)] + [sent] * ways,
        compiler_params=PARAMS,
        cost_estimate=SMALL,
        name="product",
    )(flags, *blocks, fisher)


def fold_body(flags, kept, *refs):
    got, kept_out, sent_out = refs[:-2], refs[-2], refs[-1]
    half = kept_out.shape[0]
    first = flags[1] == 0

    @pl.loop(0, kept.shape[1] // COLUMNS)
    def _(n):
        columns = pl.ds(pl.multiple_of(n * COLUMNS, COLUMNS), COLUMNS)
        if len(got) == 2:
            low, high = got[0][:, columns], got[1][:, columns]
        else:
            low, high = got[0][:half, columns], got[0][half:, columns]
        low = kept[:half, columns] + low.astype(F32)
        high = kept[half:, columns] + high.astype(F32)
        kept_out[:, columns] = jnp.where(first, low, high)
        sent_out[:, columns] = jnp.where(first, high, low).astype(sent_out.dtype)


def fold(flags, kept, got, sent_as, cost):
    shape = (kept.shape[0] // 2, kept.shape[1])
    return pl.pallas_call(
        fold_body,
        in_specs=[pl.BlockSpec(memory_space=pltpu.SMEM)] + [VMEM] * (1 + len(got)),
        out_specs=[VMEM, VMEM],
        out_shape=[jax.ShapeDtypeStruct(shape, F32), jax.ShapeDtypeStruct(shape, sent_as)],
        compiler_params=PARAMS,
        cost_estimate=cost,
        name="fold",
    )(flags, kept, *got)


def split_sum(kept, got):
    value = kept[...] + got[...].astype(F32)
    high = value.astype(BF16)
    return high, (value - high.astype(F32)).astype(BF16)


def scores_body(places, units, *refs):
    sums, grads, outs = refs[: 2 * units], refs[2 * units :][: len(places)], refs[-units:]
    rows = sums[0].shape[0]
    precond = jnp.concatenate(
        [part for u in range(units) for part in split_sum(sums[2 * u], sums[2 * u + 1])]
    )
    for grad, (r, first) in zip(grads, places):
        both = dot_t(grad[...], precond)
        for u in range(units):
            value = both[:, 2 * u * rows :][:, :rows] + both[:, (2 * u + 1) * rows :][:, :rows]
            outs[u][r, first : first + grad.shape[0]] = value.astype(outs[u].dtype)


def partial_scores(units, grads, out_as, cost):
    rows = units[0][0].shape[0]
    train_rows = grads[0][2].shape[0]
    return pl.pallas_call(
        functools.partial(scores_body, [piece[:2] for piece in grads], len(units)),
        in_specs=[VMEM] * (2 * len(units) + len(grads)),
        out_specs=[VMEM] * len(units),
        out_shape=[jax.ShapeDtypeStruct((4, train_rows, rows), kind) for kind in out_as],
        compiler_params=PARAMS,
        cost_estimate=cost,
        name="scores",
    )(*[value for unit in units for value in unit], *[piece[2] for piece in grads])


def last_scores_body(places, kept, got, counts, before, *refs):
    grads, out, chosen_out = refs[: len(places)], refs[-2], refs[-1]
    rows = kept.shape[0]
    low = places[0][0]
    train_rows = counts.shape[1]
    precond = jnp.concatenate(split_sum(kept, got))
    chosen = before[:1]
    for grad, (r, first) in zip(grads, places):
        both = dot_t(grad[...], precond)
        value = both[:, :rows] + both[:, rows:]
        place = pl.ds(first, grad.shape[0])
        out[r - low, place] = value.astype(BF16)
        chosen = chosen + jnp.sum(value * counts[r, place], axis=0, keepdims=True)
    chosen_out[...] = jnp.broadcast_to(chosen, chosen_out.shape)
    if out.shape[1] > train_rows:
        high = chosen.astype(BF16).astype(F32)
        both = jnp.concatenate(
            [jnp.broadcast_to(value, (EXTRA // 2, rows)) for value in (high, chosen - high)]
        )
        for n in range(2):
            out[n, train_rows:] = both.astype(BF16)


def last_scores(kept, got, counts, before, grads, extra):
    rows = kept.shape[0]
    return pl.pallas_call(
        functools.partial(last_scores_body, [piece[:2] for piece in grads]),
        in_specs=[VMEM] * (4 + len(grads)),
        out_specs=[VMEM, VMEM],
        out_shape=[
            jax.ShapeDtypeStruct((2, counts.shape[1] + extra, rows), BF16),
            jax.ShapeDtypeStruct((8, rows), F32),
        ],
        compiler_params=PARAMS,
        cost_estimate=SMALL,
        name="last_scores",
    )(kept, got, counts, before, *[piece[2] for piece in grads])


def four_by_four(train_grads, test_grads, fisher, chosen_ids):
    z = lax.axis_index("test")
    i = lax.axis_index("train")
    chip, core = i // 2, i % 2
    inner = (z == 1) | (z == 2)
    flags = jnp.stack([core, chip, inner.astype(jnp.int32)])
    own_rows = train_grads.shape[0]
    quarter = test_grads.shape[0] // 4

    def along(value, pairs):
        return lax.ppermute(value, "test", pairs)

    def to_other(value, r):
        return lax.ppermute(value, "train", [(k, k ^ r) for k in range(4)])

    def tied(*values):
        return lax.optimization_barrier(values)

    pair = [(0, 1), (1, 0), (2, 3), (3, 2)]
    middle = [(1, 2), (2, 1)]
    outward = [(1, 0), (2, 3)]
    inward = [(0, 1), (3, 2)]

    def core_sum(kept, *sent, sent_as=BF16, cost=SMALL):
        return fold(flags, kept, [to_other(part, 1) for part in sent], sent_as, cost)

    def scores_of(*units, out_as=(BF16, BF16), cost=SMALL):
        pieces = [(*place, grad) for place, grad in zip(places, grads)]
        return partial_scores(units, pieces, out_as[: len(units)], cost)

    def in_order(parts):
        parts = [parts[0], parts[2], parts[1], parts[3]]
        parts = [jnp.where(chip == 0, parts[q], parts[q ^ 1]) for q in range(4)]
        parts = [jnp.where(core == 0, parts[q], parts[q ^ 2]) for q in range(4)]
        return jnp.concatenate(parts, axis=1)

    row_ids = jnp.stack([i, i ^ 1, i ^ 2, i ^ 3])[:, None] * own_rows + jnp.arange(own_rows)

    def selected(ids):
        ids = lax.dynamic_slice_in_dim(ids, (core * 2 + chip) * quarter, quarter).T
        return sum((ids[k] == row_ids[:, :, None]).astype(F32) for k in range(ids.shape[0]))

    pair_in = along(test_grads, pair)
    middle_in = along(test_grads, middle)
    other_core, other_chip = to_other(train_grads, 1), to_other(train_grads, 2)
    own, other_core = tied(test_grads, other_core)
    own, own_sent = core_sum(*product(flags, [own], fisher), sent_as=F32, cost=MORE)
    half = own_rows // 2
    other_both = [to_other(other_chip[:half], 1), to_other(other_chip[half:], 1)]
    grads = [train_grads, other_core, other_chip, *other_both]
    pair_in, middle_in, own, own_sent, chosen_ids, grads = tied(
        pair_in, middle_in, own, own_sent, chosen_ids, grads
    )
    places = ((0, 0), (1, 0), (2, 0), (3, 0), (3, half))

    second_edge = along(middle_in, outward)
    far_in = along(pair_in, middle)
    near, near_sent = core_sum(*product(flags, [middle_in, pair_in], fisher))
    own_got = to_other(own_sent, 2)
    near_sent, own_got, pair_in = tied(near_sent, own_got, pair_in)
    near_got = to_other(near_sent, 2)
    third, third_sent = core_sum(*product(flags, [pair_in], fisher))
    (near,) = scores_of((near, near_got), cost=SOME)
    far_ids = along(chosen_ids, [(0, 3), (3, 0)])
    counts = selected(chosen_ids)
    far_in, second_edge, third, third_sent, own, own_got, near, far_ids, counts, grads = tied(
        far_in, second_edge, third, third_sent, own, own_got, near, far_ids, counts, grads
    )

    first_edge = along(far_in, outward)
    second, second_sent = core_sum(*product(flags, [far_in, second_edge], fisher))
    second, second_sent, near = tied(second, second_sent, near)
    second_got = to_other(second_sent, 2)
    near_in, near_across = along(near, inward), along(near, middle)
    second_got, near_in, near_across = tied(second_got, near_in, near_across)
    (second,) = scores_of((second, second_got))
    across = along(second, middle)
    (third,) = scores_of((third, to_other(third_sent, 2)), out_as=(F32,))
    (own,) = scores_of((own, own_got), out_as=(F32,))
    own = own + near_in.astype(F32) + near_across.astype(F32)
    chosen = jnp.broadcast_to(jnp.sum(own * counts, axis=(0, 1)), (8, quarter))
    early = [jnp.concatenate([part, chosen]) for part in own]
    early = [early[0]] + [to_other(early[r], r) for r in range(1, 4)]
    far_counts = selected(far_ids)
    first_edge, early, second, across, third, grads, counts, far_counts = tied(
        first_edge, early, second, across, third, grads, counts, far_counts
    )

    third = along((third + across.astype(F32)).astype(BF16), outward)
    second = along(second, [(0, 2), (3, 1)])
    last, last_sent = core_sum(*product(flags, [first_edge], fisher))
    last_got = to_other(last_sent, 2)
    ends = [(0, 3), (3, 0)]
    none = jnp.zeros((8, quarter), F32)
    pieces = [(*place, grad) for place, grad in zip(places, grads)]
    away, chosen = last_scores(last, last_got, far_counts, none, pieces[2:], 0)
    away = along(away, ends)
    away, second, third = tied(away, second, third)
    away = [to_other(away[0], 2).astype(F32), to_other(away[1], 3).astype(F32)]
    here, _ = last_scores(last, last_got, far_counts, chosen, pieces[:2], EXTRA)
    here = along(here, ends)
    here = [here[0], to_other(here[1], 1)]
    sums = [part[own_rows:] for part in here]
    sums += [to_other(sums[0], 2), to_other(sums[0], 3)]

    late = second + third
    chosen = jnp.sum(late.astype(F32) * counts, axis=(0, 1))
    high = lax.reduce_precision(chosen, 8, 7)
    chosen = [jnp.broadcast_to(value, (EXTRA // 2, quarter)) for value in (high, chosen - high)]
    chosen = jnp.concatenate(chosen).astype(BF16)
    late = [jnp.concatenate([part, chosen]) for part in late]
    late = [late[0]] + [to_other(late[r], r) for r in range(1, 4)]

    def of_sums(value):
        return value[0].astype(F32) + value[EXTRA // 2].astype(F32)

    early, late, sums = in_order(early), in_order(late), in_order(sums)
    last = in_order([part[:own_rows].astype(F32) for part in here] + away)
    scores = early[:own_rows] + late[:own_rows].astype(F32) + last
    return scores, early[own_rows] + of_sums(late[own_rows:]) + of_sums(sums)


def solution(mesh):
    sizes = (mesh.shape["train"], mesh.shape["test"])
    return jax.shard_map(
        four_by_four if sizes == (4, 4) else any_mesh,
        mesh=mesh,
        in_specs=(
            P(("groups", "train"), "test"),
            P(("groups", "test"), "train"),
            P("train", "test"),
            P(("groups", "test"), None),
        ),
        out_specs=(P(("groups", "train"), "test"), P(("groups", "test"))),
        check_vma=False,
    )
```

```python
import functools

import jax
import jax.numpy as jnp
from jax import lax
from jax.experimental import pallas as pl
from jax.experimental.pallas import tpu as pltpu
from jax.sharding import PartitionSpec as P

COLUMNS = 512
EXTRA = 16

F32 = jnp.float32
BF16 = jnp.bfloat16


def dot_t(a, b):
    return lax.dot_general(a, b, (((1,), (1,)), ((), ())), preferred_element_type=F32)


def selection_counts(chosen_ids, first_row, rows):
    row_ids = first_row + lax.broadcasted_iota(jnp.int32, (rows, chosen_ids.shape[0]), 0)
    ids = chosen_ids.T
    counts = jnp.zeros(row_ids.shape, F32)
    for k in range(ids.shape[0]):
        counts = counts + (row_ids == ids[k][None, :]).astype(F32)
    return counts


def any_mesh(train_grads, test_grads, fisher, chosen_ids):
    test_whole = lax.all_gather(test_grads, "test", axis=0, tiled=True)
    partial_value = jnp.dot(test_whole, fisher, preferred_element_type=F32)
    precond = lax.psum(partial_value, "train").astype(BF16)
    partial_scores = dot_t(train_grads, precond)
    scores = lax.psum_scatter(partial_scores, "test", scatter_dimension=1, tiled=True)
    rows = scores.shape[0]
    counts = selection_counts(chosen_ids, lax.axis_index("train") * rows, rows)
    return scores, lax.psum(jnp.sum(counts * scores, axis=0), "train")


SMALL = pl.CostEstimate(flops=1, bytes_accessed=1, transcendentals=0)
SOME = pl.CostEstimate(flops=2 * 10**9, bytes_accessed=2**20, transcendentals=0)
MORE = pl.CostEstimate(flops=7 * 10**9, bytes_accessed=2**20, transcendentals=0)
PARAMS = pltpu.CompilerParams(vmem_limit_bytes=8 * 2**20)


VMEM = pl.BlockSpec(memory_space=pltpu.VMEM)


def product_body(count, flags, *refs):
    blocks, fisher, outs = refs[:count], refs[count], refs[count + 1 :]
    quarter = blocks[0].shape[0] // 4
    mine = flags[0] == 0

    def multiply(block, kept, *sent):
        @pl.loop(0, fisher.shape[1] // COLUMNS)
        def _(n):
            columns = pl.ds(pl.multiple_of(n * COLUMNS, COLUMNS), COLUMNS)
            value = jnp.dot(block[...], fisher[:, columns], preferred_element_type=F32)
            for chip in range(2):
                low, high = (value[(2 * core + chip) * quarter :][:quarter] for core in range(2))
                kept[pl.ds(chip * quarter, quarter), columns] = jnp.where(mine, low, high)
                other = jnp.where(mine, high, low).astype(BF16)
                if len(sent) == 2:
                    sent[chip][:, columns] = other
                else:
                    sent[0][pl.ds(chip * quarter, quarter), columns] = other

    if len(blocks) == 1:
        multiply(blocks[0], *outs)
    else:
        pl.when(flags[2] == 1)(lambda: multiply(blocks[0], *outs))
        pl.when(flags[2] == 0)(lambda: multiply(blocks[1], *outs))


def product(flags, blocks, fisher, ways=2):
    half = blocks[0].shape[0] // 2
    columns = fisher.shape[1]
    sent = jax.ShapeDtypeStruct((half // ways, columns), BF16)
    return pl.pallas_call(
        functools.partial(product_body, len(blocks)),
        in_specs=[pl.BlockSpec(memory_space=pltpu.SMEM)] + [VMEM] * (len(blocks) + 1),
        out_specs=[VMEM] * (1 + ways),
        out_shape=[jax.ShapeDtypeStruct((half, columns), F32)] + [sent] * ways,
        compiler_params=PARAMS,
        cost_estimate=SMALL,
        name="product",
    )(flags, *blocks, fisher)


def fold_body(flags, kept, *refs):
    got, kept_out, sent_out = refs[:-2], refs[-2], refs[-1]
    half = kept_out.shape[0]
    first = flags[1] == 0

    @pl.loop(0, kept.shape[1] // COLUMNS)
    def _(n):
        columns = pl.ds(pl.multiple_of(n * COLUMNS, COLUMNS), COLUMNS)
        if len(got) == 2:
            low, high = got[0][:, columns], got[1][:, columns]
        else:
            low, high = got[0][:half, columns], got[0][half:, columns]
        low = kept[:half, columns] + low.astype(F32)
        high = kept[half:, columns] + high.astype(F32)
        kept_out[:, columns] = jnp.where(first, low, high)
        sent_out[:, columns] = jnp.where(first, high, low).astype(sent_out.dtype)


def fold(flags, kept, got, sent_as, cost):
    shape = (kept.shape[0] // 2, kept.shape[1])
    return pl.pallas_call(
        fold_body,
        in_specs=[pl.BlockSpec(memory_space=pltpu.SMEM)] + [VMEM] * (1 + len(got)),
        out_specs=[VMEM, VMEM],
        out_shape=[jax.ShapeDtypeStruct(shape, F32), jax.ShapeDtypeStruct(shape, sent_as)],
        compiler_params=PARAMS,
        cost_estimate=cost,
        name="fold",
    )(flags, kept, *got)


def split_sum(kept, got):
    value = kept[...] + got[...].astype(F32)
    high = value.astype(BF16)
    return high, (value - high.astype(F32)).astype(BF16)


def scores_body(places, units, *refs):
    sums, grads, outs = refs[: 2 * units], refs[2 * units :][: len(places)], refs[-units:]
    rows = sums[0].shape[0]
    precond = jnp.concatenate(
        [part for u in range(units) for part in split_sum(sums[2 * u], sums[2 * u + 1])]
    )
    for grad, (r, first) in zip(grads, places):
        both = dot_t(grad[...], precond)
        for u in range(units):
            value = both[:, 2 * u * rows :][:, :rows] + both[:, (2 * u + 1) * rows :][:, :rows]
            outs[u][r, first : first + grad.shape[0]] = value.astype(outs[u].dtype)


def partial_scores(units, grads, out_as, cost):
    rows = units[0][0].shape[0]
    train_rows = grads[0][2].shape[0]
    return pl.pallas_call(
        functools.partial(scores_body, [piece[:2] for piece in grads], len(units)),
        in_specs=[VMEM] * (2 * len(units) + len(grads)),
        out_specs=[VMEM] * len(units),
        out_shape=[jax.ShapeDtypeStruct((4, train_rows, rows), kind) for kind in out_as],
        compiler_params=PARAMS,
        cost_estimate=cost,
        name="scores",
    )(*[value for unit in units for value in unit], *[piece[2] for piece in grads])


def last_scores_body(places, kept, got, counts, before, *refs):
    grads, out, chosen_out = refs[: len(places)], refs[-2], refs[-1]
    rows = kept.shape[0]
    low = places[0][0]
    train_rows = counts.shape[1]
    precond = jnp.concatenate(split_sum(kept, got))
    chosen = before[:1]
    for grad, (r, first) in zip(grads, places):
        both = dot_t(grad[...], precond)
        value = both[:, :rows] + both[:, rows:]
        place = pl.ds(first, grad.shape[0])
        out[r - low, place] = value.astype(BF16)
        chosen = chosen + jnp.sum(value * counts[r, place], axis=0, keepdims=True)
    chosen_out[...] = jnp.broadcast_to(chosen, chosen_out.shape)
    if out.shape[1] > train_rows:
        high = chosen.astype(BF16).astype(F32)
        both = jnp.concatenate(
            [jnp.broadcast_to(value, (EXTRA // 2, rows)) for value in (high, chosen - high)]
        )
        for n in range(2):
            out[n, train_rows:] = both.astype(BF16)


def last_scores(kept, got, counts, before, grads, extra):
    rows = kept.shape[0]
    return pl.pallas_call(
        functools.partial(last_scores_body, [piece[:2] for piece in grads]),
        in_specs=[VMEM] * (4 + len(grads)),
        out_specs=[VMEM, VMEM],
        out_shape=[
            jax.ShapeDtypeStruct((2, counts.shape[1] + extra, rows), BF16),
            jax.ShapeDtypeStruct((8, rows), F32),
        ],
        compiler_params=PARAMS,
        cost_estimate=SMALL,
        name="last_scores",
    )(kept, got, counts, before, *[piece[2] for piece in grads])


def four_by_four(train_grads, test_grads, fisher, chosen_ids):
    z = lax.axis_index("test")
    i = lax.axis_index("train")
    chip, core = i // 2, i % 2
    inner = (z == 1) | (z == 2)
    flags = jnp.stack([core, chip, inner.astype(jnp.int32)])
    own_rows = train_grads.shape[0]
    quarter = test_grads.shape[0] // 4

    def along(value, pairs):
        return lax.ppermute(value, "test", pairs)

    def to_other(value, r):
        return lax.ppermute(value, "train", [(k, k ^ r) for k in range(4)])

    def tied(*values):
        return lax.optimization_barrier(values)

    pair = [(0, 1), (1, 0), (2, 3), (3, 2)]
    middle = [(1, 2), (2, 1)]
    outward = [(1, 0), (2, 3)]
    inward = [(0, 1), (3, 2)]

    def core_sum(kept, *sent, sent_as=BF16, cost=SMALL):
        return fold(flags, kept, [to_other(part, 1) for part in sent], sent_as, cost)

    def scores_of(*units, out_as=(BF16, BF16), cost=SMALL):
        pieces = [(*place, grad) for place, grad in zip(places, grads)]
        return partial_scores(units, pieces, out_as[: len(units)], cost)

    def in_order(parts):
        parts = [parts[0], parts[2], parts[1], parts[3]]
        parts = [jnp.where(chip == 0, parts[q], parts[q ^ 1]) for q in range(4)]
        parts = [jnp.where(core == 0, parts[q], parts[q ^ 2]) for q in range(4)]
        return jnp.concatenate(parts, axis=1)

    row_ids = jnp.stack([i, i ^ 1, i ^ 2, i ^ 3])[:, None] * own_rows + jnp.arange(own_rows)

    def selected(ids):
        ids = lax.dynamic_slice_in_dim(ids, (core * 2 + chip) * quarter, quarter).T
        return sum((ids[k] == row_ids[:, :, None]).astype(F32) for k in range(ids.shape[0]))

    pair_in = along(test_grads, pair)
    middle_in = along(test_grads, middle)
    other_core, other_chip = to_other(train_grads, 1), to_other(train_grads, 2)
    own, other_core = tied(test_grads, other_core)
    own, own_sent = core_sum(*product(flags, [own], fisher), sent_as=F32, cost=MORE)
    half = own_rows // 2
    other_both = [to_other(other_chip[:half], 1), to_other(other_chip[half:], 1)]
    grads = [train_grads, other_core, other_chip, *other_both]
    pair_in, middle_in, own, own_sent, chosen_ids, grads = tied(
        pair_in, middle_in, own, own_sent, chosen_ids, grads
    )
    places = ((0, 0), (1, 0), (2, 0), (3, 0), (3, half))

    second_edge = along(middle_in, outward)
    far_in = along(pair_in, middle)
    near, near_sent = core_sum(*product(flags, [middle_in, pair_in], fisher))
    own_got = to_other(own_sent, 2)
    near_sent, own_got, pair_in = tied(near_sent, own_got, pair_in)
    near_got = to_other(near_sent, 2)
    third, third_sent = core_sum(*product(flags, [pair_in], fisher))
    (near,) = scores_of((near, near_got), cost=SOME)
    far_ids = along(chosen_ids, [(0, 3), (3, 0)])
    counts = selected(chosen_ids)
    far_in, second_edge, third, third_sent, own, own_got, near, far_ids, counts, grads = tied(
        far_in, second_edge, third, third_sent, own, own_got, near, far_ids, counts, grads
    )

    first_edge = along(far_in, outward)
    second, second_sent = core_sum(*product(flags, [far_in, second_edge], fisher))
    second, second_sent, near = tied(second, second_sent, near)
    second_got = to_other(second_sent, 2)
    near_in, near_across = along(near, inward), along(near, middle)
    (second,) = scores_of((second, second_got))
    across = along(second, middle)
    (third,) = scores_of((third, to_other(third_sent, 2)), out_as=(F32,))
    (own,) = scores_of((own, own_got), out_as=(F32,))
    own = own + near_in.astype(F32) + near_across.astype(F32)
    chosen = jnp.broadcast_to(jnp.sum(own * counts, axis=(0, 1)), (8, quarter))
    early = [jnp.concatenate([part, chosen]) for part in own]
    early = [early[0]] + [to_other(early[r], r) for r in range(1, 4)]
    far_counts = selected(far_ids)
    first_edge, early, second, across, third, grads, counts, far_counts = tied(
        first_edge, early, second, across, third, grads, counts, far_counts
    )

    third = along((third + across.astype(F32)).astype(BF16), outward)
    second = along(second, [(0, 2), (3, 1)])
    last, last_sent = core_sum(*product(flags, [first_edge], fisher))
    last_got = to_other(last_sent, 2)
    ends = [(0, 3), (3, 0)]
    none = jnp.zeros((8, quarter), F32)
    pieces = [(*place, grad) for place, grad in zip(places, grads)]
    away, chosen = last_scores(last, last_got, far_counts, none, pieces[2:], 0)
    away = along(away, ends)
    away, second, third = tied(away, second, third)
    away = [to_other(away[0], 2).astype(F32), to_other(away[1], 3).astype(F32)]
    here, _ = last_scores(last, last_got, far_counts, chosen, pieces[:2], EXTRA)
    here = along(here, ends)
    here = [here[0], to_other(here[1], 1)]
    sums = [part[own_rows:] for part in here]
    sums += [to_other(sums[0], 2), to_other(sums[0], 3)]

    late = second + third
    chosen = jnp.sum(late.astype(F32) * counts, axis=(0, 1))
    high = lax.reduce_precision(chosen, 8, 7)
    chosen = [jnp.broadcast_to(value, (EXTRA // 2, quarter)) for value in (high, chosen - high)]
    chosen = jnp.concatenate(chosen).astype(BF16)
    late = [jnp.concatenate([part, chosen]) for part in late]
    late = [late[0]] + [to_other(late[r], r) for r in range(1, 4)]

    def of_sums(value):
        return value[0].astype(F32) + value[EXTRA // 2].astype(F32)

    early, late, sums = in_order(early), in_order(late), in_order(sums)
    last = in_order([part[:own_rows].astype(F32) for part in here] + away)
    scores = early[:own_rows] + late[:own_rows].astype(F32) + last
    return scores, early[own_rows] + of_sums(late[own_rows:]) + of_sums(sums)


def solution(mesh):
    sizes = (mesh.shape["train"], mesh.shape["test"])
    return jax.shard_map(
        four_by_four if sizes == (4, 4) else any_mesh,
        mesh=mesh,
        in_specs=(
            P(("groups", "train"), "test"),
            P(("groups", "test"), "train"),
            P("train", "test"),
            P(("groups", "test"), None),
        ),
        out_specs=(P(("groups", "train"), "test"), P(("groups", "test"))),
        check_vma=False,
    )
```

```python
import functools

import jax
import jax.numpy as jnp
from jax import lax
from jax.experimental import pallas as pl
from jax.experimental.pallas import tpu as pltpu
from jax.sharding import PartitionSpec as P

COLUMNS = 512
EXTRA = 16

F32 = jnp.float32
BF16 = jnp.bfloat16


def dot_t(a, b):
    return lax.dot_general(a, b, (((1,), (1,)), ((), ())), preferred_element_type=F32)


def selection_counts(chosen_ids, first_row, rows):
    row_ids = first_row + lax.broadcasted_iota(jnp.int32, (rows, chosen_ids.shape[0]), 0)
    ids = chosen_ids.T
    counts = jnp.zeros(row_ids.shape, F32)
    for k in range(ids.shape[0]):
        counts = counts + (row_ids == ids[k][None, :]).astype(F32)
    return counts


def any_mesh(train_grads, test_grads, fisher, chosen_ids):
    test_whole = lax.all_gather(test_grads, "test", axis=0, tiled=True)
    partial_value = jnp.dot(test_whole, fisher, preferred_element_type=F32)
    precond = lax.psum(partial_value, "train").astype(BF16)
    partial_scores = dot_t(train_grads, precond)
    scores = lax.psum_scatter(partial_scores, "test", scatter_dimension=1, tiled=True)
    rows = scores.shape[0]
    counts = selection_counts(chosen_ids, lax.axis_index("train") * rows, rows)
    return scores, lax.psum(jnp.sum(counts * scores, axis=0), "train")


SMALL = pl.CostEstimate(flops=1, bytes_accessed=1, transcendentals=0)
SOME = pl.CostEstimate(flops=2 * 10**9, bytes_accessed=2**20, transcendentals=0)
MORE = pl.CostEstimate(flops=7 * 10**9, bytes_accessed=2**20, transcendentals=0)
PARAMS = pltpu.CompilerParams(vmem_limit_bytes=12 * 2**20)


VMEM = pl.BlockSpec(memory_space=pltpu.VMEM)


def product_body(count, flags, *refs):
    blocks, fisher, outs = refs[:count], refs[count], refs[count + 1 :]
    quarter = blocks[0].shape[0] // 4
    mine = flags[0] == 0

    def multiply(block, kept, *sent):
        @pl.loop(0, fisher.shape[1] // COLUMNS)
        def _(n):
            columns = pl.ds(pl.multiple_of(n * COLUMNS, COLUMNS), COLUMNS)
            value = jnp.dot(block[...], fisher[:, columns], preferred_element_type=F32)
            for chip in range(2):
                low, high = (value[(2 * core + chip) * quarter :][:quarter] for core in range(2))
                kept[pl.ds(chip * quarter, quarter), columns] = jnp.where(mine, low, high)
                other = jnp.where(mine, high, low).astype(BF16)
                if len(sent) == 2:
                    sent[chip][:, columns] = other
                else:
                    sent[0][pl.ds(chip * quarter, quarter), columns] = other

    if len(blocks) == 1:
        multiply(blocks[0], *outs)
    else:
        pl.when(flags[2] == 1)(lambda: multiply(blocks[0], *outs))
        pl.when(flags[2] == 0)(lambda: multiply(blocks[1], *outs))


def product(flags, blocks, fisher, ways=2):
    half = blocks[0].shape[0] // 2
    columns = fisher.shape[1]
    sent = jax.ShapeDtypeStruct((half // ways, columns), BF16)
    return pl.pallas_call(
        functools.partial(product_body, len(blocks)),
        in_specs=[pl.BlockSpec(memory_space=pltpu.SMEM)] + [VMEM] * (len(blocks) + 1),
        out_specs=[VMEM] * (1 + ways),
        out_shape=[jax.ShapeDtypeStruct((half, columns), F32)] + [sent] * ways,
        compiler_params=PARAMS,
        cost_estimate=SMALL,
        name="product",
    )(flags, *blocks, fisher)


def fold_body(flags, kept, *refs):
    got, kept_out, sent_out = refs[:-2], refs[-2], refs[-1]
    half = kept_out.shape[0]
    first = flags[1] == 0

    @pl.loop(0, kept.shape[1] // COLUMNS)
    def _(n):
        columns = pl.ds(pl.multiple_of(n * COLUMNS, COLUMNS), COLUMNS)
        if len(got) == 2:
            low, high = got[0][:, columns], got[1][:, columns]
        else:
            low, high = got[0][:half, columns], got[0][half:, columns]
        low = kept[:half, columns] + low.astype(F32)
        high = kept[half:, columns] + high.astype(F32)
        kept_out[:, columns] = jnp.where(first, low, high)
        sent_out[:, columns] = jnp.where(first, high, low).astype(sent_out.dtype)


def fold(flags, kept, got, sent_as, cost):
    shape = (kept.shape[0] // 2, kept.shape[1])
    return pl.pallas_call(
        fold_body,
        in_specs=[pl.BlockSpec(memory_space=pltpu.SMEM)] + [VMEM] * (1 + len(got)),
        out_specs=[VMEM, VMEM],
        out_shape=[jax.ShapeDtypeStruct(shape, F32), jax.ShapeDtypeStruct(shape, sent_as)],
        compiler_params=PARAMS,
        cost_estimate=cost,
        name="fold",
    )(flags, kept, *got)


def split_sum(kept, got):
    value = kept[...] + got[...].astype(F32)
    high = value.astype(BF16)
    return high, (value - high.astype(F32)).astype(BF16)


def scores_body(places, units, *refs):
    sums, grads, outs = refs[: 2 * units], refs[2 * units :][: len(places)], refs[-units:]
    rows = sums[0].shape[0]
    precond = jnp.concatenate(
        [part for u in range(units) for part in split_sum(sums[2 * u], sums[2 * u + 1])]
    )
    for grad, (r, first) in zip(grads, places):
        both = dot_t(grad[...], precond)
        for u in range(units):
            value = both[:, 2 * u * rows :][:, :rows] + both[:, (2 * u + 1) * rows :][:, :rows]
            outs[u][r, first : first + grad.shape[0]] = value.astype(outs[u].dtype)


def partial_scores(units, grads, out_as, cost):
    rows = units[0][0].shape[0]
    train_rows = grads[0][2].shape[0]
    return pl.pallas_call(
        functools.partial(scores_body, [piece[:2] for piece in grads], len(units)),
        in_specs=[VMEM] * (2 * len(units) + len(grads)),
        out_specs=[VMEM] * len(units),
        out_shape=[jax.ShapeDtypeStruct((4, train_rows, rows), kind) for kind in out_as],
        compiler_params=PARAMS,
        cost_estimate=cost,
        name="scores",
    )(*[value for unit in units for value in unit], *[piece[2] for piece in grads])


def last_scores_body(places, kept, got, counts, before, *refs):
    grads, out, chosen_out = refs[: len(places)], refs[-2], refs[-1]
    rows = kept.shape[0]
    low = places[0][0]
    train_rows = counts.shape[1]
    precond = jnp.concatenate(split_sum(kept, got))
    chosen = before[:1]
    for grad, (r, first) in zip(grads, places):
        both = dot_t(grad[...], precond)
        value = both[:, :rows] + both[:, rows:]
        place = pl.ds(first, grad.shape[0])
        out[r - low, place] = value.astype(BF16)
        chosen = chosen + jnp.sum(value * counts[r, place], axis=0, keepdims=True)
    chosen_out[...] = jnp.broadcast_to(chosen, chosen_out.shape)
    for n in range(2):
        if out.shape[1] > train_rows:
            out[n, train_rows:] = jnp.broadcast_to(chosen, (EXTRA, rows)).astype(BF16)


def last_scores(kept, got, counts, before, grads, extra):
    rows = kept.shape[0]
    return pl.pallas_call(
        functools.partial(last_scores_body, [piece[:2] for piece in grads]),
        in_specs=[VMEM] * (4 + len(grads)),
        out_specs=[VMEM, VMEM],
        out_shape=[
            jax.ShapeDtypeStruct((2, counts.shape[1] + extra, rows), BF16),
            jax.ShapeDtypeStruct((8, rows), F32),
        ],
        compiler_params=PARAMS,
        cost_estimate=SMALL,
        name="last_scores",
    )(kept, got, counts, before, *[piece[2] for piece in grads])


def four_by_four(train_grads, test_grads, fisher, chosen_ids):
    z = lax.axis_index("test")
    i = lax.axis_index("train")
    chip, core = i // 2, i % 2
    inner = (z == 1) | (z == 2)
    flags = jnp.stack([core, chip, inner.astype(jnp.int32)])
    own_rows = train_grads.shape[0]
    quarter = test_grads.shape[0] // 4

    def along(value, pairs):
        return lax.ppermute(value, "test", pairs)

    def to_other(value, r):
        return lax.ppermute(value, "train", [(k, k ^ r) for k in range(4)])

    def tied(*values):
        return lax.optimization_barrier(values)

    pair = [(0, 1), (1, 0), (2, 3), (3, 2)]
    middle = [(1, 2), (2, 1)]
    outward = [(1, 0), (2, 3)]
    inward = [(0, 1), (3, 2)]

    def core_sum(kept, *sent, sent_as=BF16, cost=SMALL):
        return fold(flags, kept, [to_other(part, 1) for part in sent], sent_as, cost)

    def scores_of(*units, out_as=(BF16, BF16), cost=SMALL):
        pieces = [(*place, grad) for place, grad in zip(places, grads)]
        return partial_scores(units, pieces, out_as[: len(units)], cost)

    def in_order(parts):
        parts = [parts[0], parts[2], parts[1], parts[3]]
        parts = [jnp.where(chip == 0, parts[q], parts[q ^ 1]) for q in range(4)]
        parts = [jnp.where(core == 0, parts[q], parts[q ^ 2]) for q in range(4)]
        return jnp.concatenate(parts, axis=1)

    row_ids = jnp.stack([i, i ^ 1, i ^ 2, i ^ 3])[:, None] * own_rows + jnp.arange(own_rows)

    def selected(ids):
        ids = lax.dynamic_slice_in_dim(ids, (core * 2 + chip) * quarter, quarter).T
        return sum((ids[k] == row_ids[:, :, None]).astype(F32) for k in range(ids.shape[0]))

    pair_in = along(test_grads, pair)
    middle_in = along(test_grads, middle)
    other_core, other_chip = to_other(train_grads, 1), to_other(train_grads, 2)
    own, other_core = tied(test_grads, other_core)
    own, own_sent = core_sum(*product(flags, [own], fisher), sent_as=F32, cost=MORE)
    half = own_rows // 2
    other_both = [to_other(other_chip[:half], 1), to_other(other_chip[half:], 1)]
    grads = [train_grads, other_core, other_chip, *other_both]
    pair_in, middle_in, own, own_sent, chosen_ids, grads = tied(
        pair_in, middle_in, own, own_sent, chosen_ids, grads
    )
    places = ((0, 0), (1, 0), (2, 0), (3, 0), (3, half))

    second_edge = along(middle_in, outward)
    far_in = along(pair_in, middle)
    near, near_sent = core_sum(*product(flags, [middle_in, pair_in], fisher))
    own_got = to_other(own_sent, 2)
    near_sent, own_got, pair_in = tied(near_sent, own_got, pair_in)
    near_got = to_other(near_sent, 2)
    third, third_sent = core_sum(*product(flags, [pair_in], fisher))
    (near,) = scores_of((near, near_got), cost=SOME)
    far_ids = along(chosen_ids, [(0, 3), (3, 0)])
    counts = selected(chosen_ids)
    far_in, second_edge, third, third_sent, own, own_got, near, far_ids, counts, grads = tied(
        far_in, second_edge, third, third_sent, own, own_got, near, far_ids, counts, grads
    )

    first_edge = along(far_in, outward)
    second, second_sent = core_sum(*product(flags, [far_in, second_edge], fisher))
    second, second_sent, near = tied(second, second_sent, near)
    second_got = to_other(second_sent, 2)
    near_in, near_across = along(near, inward), along(near, middle)
    second_got, near_in, near_across = tied(second_got, near_in, near_across)
    (second,) = scores_of((second, second_got))
    across = along(second, middle)
    third, total = scores_of(
        (third, to_other(third_sent, 2)), (own, own_got), out_as=(F32, F32)
    )
    far_counts = selected(far_ids)
    first_edge, total, near_in, near_across, second, across, third, grads, far_counts = tied(
        first_edge, total, near_in, near_across, second, across, third, grads, far_counts
    )

    third = along((third + across.astype(F32)).astype(BF16), outward)
    second = along(second, [(0, 2), (3, 1)])
    last, last_sent = core_sum(*product(flags, [first_edge], fisher))
    last_got = to_other(last_sent, 2)
    ends = [(0, 3), (3, 0)]
    none = jnp.zeros((8, quarter), F32)
    pieces = [(*place, grad) for place, grad in zip(places, grads)]
    away, chosen = last_scores(last, last_got, far_counts, none, pieces[2:], 0)
    away = along(away, ends)
    away = [to_other(away[0], 2), to_other(away[1], 3)]
    here, _ = last_scores(last, last_got, far_counts, chosen, pieces[:2], EXTRA)
    here, second, third = tied(here, second, third)
    here = along(here, ends)
    here = [here[0], to_other(here[1], 1)]
    chosen = [part[own_rows:] for part in here]
    chosen += [to_other(chosen[0], 2), to_other(chosen[0], 3)]
    last = in_order([part[:own_rows] for part in here] + away)
    last_chosen = in_order(chosen)[0]

    total = total + sum(value.astype(F32) for value in (near_in, near_across, second, third))
    chosen = jnp.sum(total * counts, axis=(0, 1))
    total = [jnp.concatenate([part, jnp.broadcast_to(chosen, (8, quarter))]) for part in total]
    total = in_order([total[0]] + [to_other(total[r], r) for r in range(1, 4)])

    scores = total[:own_rows] + last.astype(F32)
    return scores, total[own_rows] + last_chosen.astype(F32)


def solution(mesh):
    sizes = (mesh.shape["train"], mesh.shape["test"])
    return jax.shard_map(
        four_by_four if sizes == (4, 4) else any_mesh,
        mesh=mesh,
        in_specs=(
            P(("groups", "train"), "test"),
            P(("groups", "test"), "train"),
            P("train", "test"),
            P(("groups", "test"), None),
        ),
        out_specs=(P(("groups", "train"), "test"), P(("groups", "test"))),
        check_vma=False,
    )
```

```python
import functools

import jax
import jax.numpy as jnp
from jax import lax
from jax.experimental import pallas as pl
from jax.experimental.pallas import tpu as pltpu
from jax.sharding import PartitionSpec as P

COLUMNS = 512
EXTRA = 16

F32 = jnp.float32
BF16 = jnp.bfloat16


def dot_t(a, b):
    return lax.dot_general(a, b, (((1,), (1,)), ((), ())), preferred_element_type=F32)


def selection_counts(chosen_ids, first_row, rows):
    row_ids = first_row + lax.broadcasted_iota(jnp.int32, (rows, chosen_ids.shape[0]), 0)
    ids = chosen_ids.T
    counts = jnp.zeros(row_ids.shape, F32)
    for k in range(ids.shape[0]):
        counts = counts + (row_ids == ids[k][None, :]).astype(F32)
    return counts


def any_mesh(train_grads, test_grads, fisher, chosen_ids):
    test_whole = lax.all_gather(test_grads, "test", axis=0, tiled=True)
    partial_value = jnp.dot(test_whole, fisher, preferred_element_type=F32)
    precond = lax.psum(partial_value, "train").astype(BF16)
    partial_scores = dot_t(train_grads, precond)
    scores = lax.psum_scatter(partial_scores, "test", scatter_dimension=1, tiled=True)
    rows = scores.shape[0]
    counts = selection_counts(chosen_ids, lax.axis_index("train") * rows, rows)
    return scores, lax.psum(jnp.sum(counts * scores, axis=0), "train")


SMALL = pl.CostEstimate(flops=1, bytes_accessed=1, transcendentals=0)
SOME = pl.CostEstimate(flops=2 * 10**9, bytes_accessed=2**20, transcendentals=0)
MORE = pl.CostEstimate(flops=7 * 10**9, bytes_accessed=2**20, transcendentals=0)
PARAMS = pltpu.CompilerParams(vmem_limit_bytes=12 * 2**20)


VMEM = pl.BlockSpec(memory_space=pltpu.VMEM)


def product_body(count, flags, *refs):
    blocks, fisher, outs = refs[:count], refs[count], refs[count + 1 :]
    quarter = blocks[0].shape[0] // 4
    mine = flags[0] == 0

    def multiply(block, kept, *sent):
        @pl.loop(0, fisher.shape[1] // COLUMNS)
        def _(n):
            columns = pl.ds(pl.multiple_of(n * COLUMNS, COLUMNS), COLUMNS)
            value = jnp.dot(block[...], fisher[:, columns], preferred_element_type=F32)
            for chip in range(2):
                low, high = (value[(2 * core + chip) * quarter :][:quarter] for core in range(2))
                kept[pl.ds(chip * quarter, quarter), columns] = jnp.where(mine, low, high)
                other = jnp.where(mine, high, low).astype(BF16)
                if len(sent) == 2:
                    sent[chip][:, columns] = other
                else:
                    sent[0][pl.ds(chip * quarter, quarter), columns] = other

    if len(blocks) == 1:
        multiply(blocks[0], *outs)
    else:
        pl.when(flags[2] == 1)(lambda: multiply(blocks[0], *outs))
        pl.when(flags[2] == 0)(lambda: multiply(blocks[1], *outs))


def product(flags, blocks, fisher, ways=2):
    half = blocks[0].shape[0] // 2
    columns = fisher.shape[1]
    sent = jax.ShapeDtypeStruct((half // ways, columns), BF16)
    return pl.pallas_call(
        functools.partial(product_body, len(blocks)),
        in_specs=[pl.BlockSpec(memory_space=pltpu.SMEM)] + [VMEM] * (len(blocks) + 1),
        out_specs=[VMEM] * (1 + ways),
        out_shape=[jax.ShapeDtypeStruct((half, columns), F32)] + [sent] * ways,
        compiler_params=PARAMS,
        cost_estimate=SMALL,
        name="product",
    )(flags, *blocks, fisher)


def fold_body(flags, kept, *refs):
    got, kept_out, sent_out = refs[:-2], refs[-2], refs[-1]
    half = kept_out.shape[0]
    first = flags[1] == 0

    @pl.loop(0, kept.shape[1] // COLUMNS)
    def _(n):
        columns = pl.ds(pl.multiple_of(n * COLUMNS, COLUMNS), COLUMNS)
        if len(got) == 2:
            low, high = got[0][:, columns], got[1][:, columns]
        else:
            low, high = got[0][:half, columns], got[0][half:, columns]
        low = kept[:half, columns] + low.astype(F32)
        high = kept[half:, columns] + high.astype(F32)
        kept_out[:, columns] = jnp.where(first, low, high)
        sent_out[:, columns] = jnp.where(first, high, low).astype(sent_out.dtype)


def fold(flags, kept, got, sent_as, cost):
    shape = (kept.shape[0] // 2, kept.shape[1])
    return pl.pallas_call(
        fold_body,
        in_specs=[pl.BlockSpec(memory_space=pltpu.SMEM)] + [VMEM] * (1 + len(got)),
        out_specs=[VMEM, VMEM],
        out_shape=[jax.ShapeDtypeStruct(shape, F32), jax.ShapeDtypeStruct(shape, sent_as)],
        compiler_params=PARAMS,
        cost_estimate=cost,
        name="fold",
    )(flags, kept, *got)


def split_sum(kept, got):
    value = kept[...] + got[...].astype(F32)
    high = value.astype(BF16)
    return high, (value - high.astype(F32)).astype(BF16)


def scores_body(places, units, *refs):
    sums, grads, outs = refs[: 2 * units], refs[2 * units :][: len(places)], refs[-units:]
    rows = sums[0].shape[0]
    precond = jnp.concatenate(
        [part for u in range(units) for part in split_sum(sums[2 * u], sums[2 * u + 1])]
    )
    for grad, (r, first) in zip(grads, places):
        both = dot_t(grad[...], precond)
        for u in range(units):
            value = both[:, 2 * u * rows :][:, :rows] + both[:, (2 * u + 1) * rows :][:, :rows]
            outs[u][r, first : first + grad.shape[0]] = value.astype(outs[u].dtype)


def partial_scores(units, grads, out_as, cost):
    rows = units[0][0].shape[0]
    train_rows = grads[0][2].shape[0]
    return pl.pallas_call(
        functools.partial(scores_body, [piece[:2] for piece in grads], len(units)),
        in_specs=[VMEM] * (2 * len(units) + len(grads)),
        out_specs=[VMEM] * len(units),
        out_shape=[jax.ShapeDtypeStruct((4, train_rows, rows), kind) for kind in out_as],
        compiler_params=PARAMS,
        cost_estimate=cost,
        name="scores",
    )(*[value for unit in units for value in unit], *[piece[2] for piece in grads])


def last_scores_body(places, kept, got, counts, before, *refs):
    grads, out, chosen_out = refs[: len(places)], refs[-2], refs[-1]
    rows = kept.shape[0]
    low = places[0][0]
    train_rows = counts.shape[1]
    precond = jnp.concatenate(split_sum(kept, got))
    chosen = before[:1]
    for grad, (r, first) in zip(grads, places):
        both = dot_t(grad[...], precond)
        value = both[:, :rows] + both[:, rows:]
        place = pl.ds(first, grad.shape[0])
        out[r - low, place] = value.astype(BF16)
        chosen = chosen + jnp.sum(value * counts[r, place], axis=0, keepdims=True)
    chosen_out[...] = jnp.broadcast_to(chosen, chosen_out.shape)
    for n in range(2):
        if out.shape[1] > train_rows:
            out[n, train_rows:] = jnp.broadcast_to(chosen, (EXTRA, rows)).astype(BF16)


def last_scores(kept, got, counts, before, grads, extra):
    rows = kept.shape[0]
    return pl.pallas_call(
        functools.partial(last_scores_body, [piece[:2] for piece in grads]),
        in_specs=[VMEM] * (4 + len(grads)),
        out_specs=[VMEM, VMEM],
        out_shape=[
            jax.ShapeDtypeStruct((2, counts.shape[1] + extra, rows), BF16),
            jax.ShapeDtypeStruct((8, rows), F32),
        ],
        compiler_params=PARAMS,
        cost_estimate=SMALL,
        name="last_scores",
    )(kept, got, counts, before, *[piece[2] for piece in grads])


def four_by_four(train_grads, test_grads, fisher, chosen_ids):
    z = lax.axis_index("test")
    i = lax.axis_index("train")
    chip, core = i // 2, i % 2
    inner = (z == 1) | (z == 2)
    flags = jnp.stack([core, chip, inner.astype(jnp.int32)])
    own_rows = train_grads.shape[0]
    quarter = test_grads.shape[0] // 4

    def along(value, pairs):
        return lax.ppermute(value, "test", pairs)

    def to_other(value, r):
        return lax.ppermute(value, "train", [(k, k ^ r) for k in range(4)])

    def tied(*values):
        return lax.optimization_barrier(values)

    pair = [(0, 1), (1, 0), (2, 3), (3, 2)]
    middle = [(1, 2), (2, 1)]
    outward = [(1, 0), (2, 3)]
    inward = [(0, 1), (3, 2)]

    def core_sum(kept, *sent, sent_as=BF16, cost=SMALL):
        return fold(flags, kept, [to_other(part, 1) for part in sent], sent_as, cost)

    def scores_of(*units, out_as=(BF16, BF16), cost=SMALL):
        pieces = [(*place, grad) for place, grad in zip(places, grads)]
        return partial_scores(units, pieces, out_as[: len(units)], cost)

    def in_order(parts):
        parts = [parts[0], parts[2], parts[1], parts[3]]
        parts = [jnp.where(chip == 0, parts[q], parts[q ^ 1]) for q in range(4)]
        parts = [jnp.where(core == 0, parts[q], parts[q ^ 2]) for q in range(4)]
        return jnp.concatenate(parts, axis=1)

    row_ids = jnp.stack([i, i ^ 1, i ^ 2, i ^ 3])[:, None] * own_rows + jnp.arange(own_rows)

    def selected(ids):
        ids = lax.dynamic_slice_in_dim(ids, (core * 2 + chip) * quarter, quarter).T
        return sum((ids[k] == row_ids[:, :, None]).astype(F32) for k in range(ids.shape[0]))

    pair_in = along(test_grads, pair)
    middle_in = along(test_grads, middle)
    other_core, other_chip = to_other(train_grads, 1), to_other(train_grads, 2)
    own, other_core = tied(test_grads, other_core)
    own, own_sent = core_sum(*product(flags, [own], fisher), sent_as=F32, cost=MORE)
    half = own_rows // 2
    other_both = [to_other(other_chip[:half], 1), to_other(other_chip[half:], 1)]
    grads = [train_grads, other_core, other_chip, *other_both]
    pair_in, middle_in, own, own_sent, chosen_ids, grads = tied(
        pair_in, middle_in, own, own_sent, chosen_ids, grads
    )
    places = ((0, 0), (1, 0), (2, 0), (3, 0), (3, half))

    second_edge = along(middle_in, outward)
    far_in = along(pair_in, middle)
    near, near_sent = core_sum(*product(flags, [middle_in, pair_in], fisher))
    own_got = to_other(own_sent, 2)
    near_sent, own_got, pair_in = tied(near_sent, own_got, pair_in)
    near_got = to_other(near_sent, 2)
    third, *third_sent = product(flags, [pair_in], fisher)
    third, second_edge = tied(third, second_edge)
    third, third_sent = core_sum(third, *third_sent, cost=SOME)
    (near,) = scores_of((near, near_got), cost=SOME)
    far_ids = along(chosen_ids, [(0, 3), (3, 0)])
    counts = selected(chosen_ids)
    far_in, second_edge, third, third_sent, own, own_got, near, far_ids, counts, grads = tied(
        far_in, second_edge, third, third_sent, own, own_got, near, far_ids, counts, grads
    )

    first_edge = along(far_in, outward)
    second, second_sent = core_sum(*product(flags, [far_in, second_edge], fisher))
    second, second_sent, near = tied(second, second_sent, near)
    second_got = to_other(second_sent, 2)
    near_in, near_across = along(near, inward), along(near, middle)
    second_got, near_in, near_across = tied(second_got, near_in, near_across)
    (second,) = scores_of((second, second_got))
    across = along(second, middle)
    third, total = scores_of(
        (third, to_other(third_sent, 2)), (own, own_got), out_as=(F32, F32)
    )
    far_counts = selected(far_ids)
    first_edge, total, near_in, near_across, second, across, third, grads, far_counts = tied(
        first_edge, total, near_in, near_across, second, across, third, grads, far_counts
    )

    third = along((third + across.astype(F32)).astype(BF16), outward)
    second = along(second, [(0, 2), (3, 1)])
    last, last_sent = core_sum(*product(flags, [first_edge], fisher))
    last_got = to_other(last_sent, 2)
    ends = [(0, 3), (3, 0)]
    none = jnp.zeros((8, quarter), F32)
    pieces = [(*place, grad) for place, grad in zip(places, grads)]
    away, chosen = last_scores(last, last_got, far_counts, none, pieces[2:], 0)
    away = along(away, ends)
    away = [to_other(away[0], 2), to_other(away[1], 3)]
    here, _ = last_scores(last, last_got, far_counts, chosen, pieces[:2], EXTRA)
    here, second, third = tied(here, second, third)
    here = along(here, ends)
    here = [here[0], to_other(here[1], 1)]
    chosen = [part[own_rows:] for part in here]
    chosen += [to_other(chosen[0], 2), to_other(chosen[0], 3)]
    last = in_order([part[:own_rows] for part in here] + away)
    last_chosen = in_order(chosen)[0]

    total = total + sum(value.astype(F32) for value in (near_in, near_across, second, third))
    chosen = jnp.sum(total * counts, axis=(0, 1))
    total = [jnp.concatenate([part, jnp.broadcast_to(chosen, (8, quarter))]) for part in total]
    total = in_order([total[0]] + [to_other(total[r], r) for r in range(1, 4)])

    scores = total[:own_rows] + last.astype(F32)
    return scores, total[own_rows] + last_chosen.astype(F32)


def solution(mesh):
    sizes = (mesh.shape["train"], mesh.shape["test"])
    return jax.shard_map(
        four_by_four if sizes == (4, 4) else any_mesh,
        mesh=mesh,
        in_specs=(
            P(("groups", "train"), "test"),
            P(("groups", "test"), "train"),
            P("train", "test"),
            P(("groups", "test"), None),
        ),
        out_specs=(P(("groups", "train"), "test"), P(("groups", "test"))),
        check_vma=False,
    )
```

```python
import functools

import jax
import jax.numpy as jnp
from jax import lax
from jax.experimental import pallas as pl
from jax.experimental.pallas import tpu as pltpu
from jax.sharding import PartitionSpec as P

COLUMNS = 512
EXTRA = 16

F32 = jnp.float32
BF16 = jnp.bfloat16


def dot_t(a, b):
    return lax.dot_general(a, b, (((1,), (1,)), ((), ())), preferred_element_type=F32)


def selection_counts(chosen_ids, first_row, rows):
    row_ids = first_row + lax.broadcasted_iota(jnp.int32, (rows, chosen_ids.shape[0]), 0)
    ids = chosen_ids.T
    counts = jnp.zeros(row_ids.shape, F32)
    for k in range(ids.shape[0]):
        counts = counts + (row_ids == ids[k][None, :]).astype(F32)
    return counts


def any_mesh(train_grads, test_grads, fisher, chosen_ids):
    test_whole = lax.all_gather(test_grads, "test", axis=0, tiled=True)
    partial_value = jnp.dot(test_whole, fisher, preferred_element_type=F32)
    precond = lax.psum(partial_value, "train").astype(BF16)
    partial_scores = dot_t(train_grads, precond)
    scores = lax.psum_scatter(partial_scores, "test", scatter_dimension=1, tiled=True)
    rows = scores.shape[0]
    counts = selection_counts(chosen_ids, lax.axis_index("train") * rows, rows)
    return scores, lax.psum(jnp.sum(counts * scores, axis=0), "train")


SMALL = pl.CostEstimate(flops=1, bytes_accessed=1, transcendentals=0)
SOME = pl.CostEstimate(flops=2 * 10**9, bytes_accessed=2**20, transcendentals=0)
MORE = pl.CostEstimate(flops=7 * 10**9, bytes_accessed=2**20, transcendentals=0)
PARAMS = pltpu.CompilerParams(vmem_limit_bytes=12 * 2**20)


VMEM = pl.BlockSpec(memory_space=pltpu.VMEM)


def product_body(count, flags, *refs):
    blocks, fisher, outs = refs[:count], refs[count], refs[count + 1 :]
    quarter = blocks[0].shape[0] // 4
    mine = flags[0] == 0

    def multiply(block, kept, *sent):
        @pl.loop(0, fisher.shape[1] // COLUMNS)
        def _(n):
            columns = pl.ds(pl.multiple_of(n * COLUMNS, COLUMNS), COLUMNS)
            value = jnp.dot(block[...], fisher[:, columns], preferred_element_type=F32)
            for chip in range(2):
                low, high = (value[(2 * core + chip) * quarter :][:quarter] for core in range(2))
                kept[pl.ds(chip * quarter, quarter), columns] = jnp.where(mine, low, high)
                other = jnp.where(mine, high, low).astype(BF16)
                if len(sent) == 2:
                    sent[chip][:, columns] = other
                else:
                    sent[0][pl.ds(chip * quarter, quarter), columns] = other

    if len(blocks) == 1:
        multiply(blocks[0], *outs)
    else:
        pl.when(flags[2] == 1)(lambda: multiply(blocks[0], *outs))
        pl.when(flags[2] == 0)(lambda: multiply(blocks[1], *outs))


def product(flags, blocks, fisher, ways=2):
    half = blocks[0].shape[0] // 2
    columns = fisher.shape[1]
    sent = jax.ShapeDtypeStruct((half // ways, columns), BF16)
    return pl.pallas_call(
        functools.partial(product_body, len(blocks)),
        in_specs=[pl.BlockSpec(memory_space=pltpu.SMEM)] + [VMEM] * (len(blocks) + 1),
        out_specs=[VMEM] * (1 + ways),
        out_shape=[jax.ShapeDtypeStruct((half, columns), F32)] + [sent] * ways,
        compiler_params=PARAMS,
        cost_estimate=SMALL,
        name="product",
    )(flags, *blocks, fisher)


def fold_body(flags, kept, *refs):
    got, kept_out, sent_out = refs[:-2], refs[-2], refs[-1]
    half = kept_out.shape[0]
    first = flags[1] == 0

    @pl.loop(0, kept.shape[1] // COLUMNS)
    def _(n):
        columns = pl.ds(pl.multiple_of(n * COLUMNS, COLUMNS), COLUMNS)
        if len(got) == 2:
            low, high = got[0][:, columns], got[1][:, columns]
        else:
            low, high = got[0][:half, columns], got[0][half:, columns]
        low = kept[:half, columns] + low.astype(F32)
        high = kept[half:, columns] + high.astype(F32)
        kept_out[:, columns] = jnp.where(first, low, high)
        sent_out[:, columns] = jnp.where(first, high, low).astype(sent_out.dtype)


def fold(flags, kept, got, sent_as, cost):
    shape = (kept.shape[0] // 2, kept.shape[1])
    return pl.pallas_call(
        fold_body,
        in_specs=[pl.BlockSpec(memory_space=pltpu.SMEM)] + [VMEM] * (1 + len(got)),
        out_specs=[VMEM, VMEM],
        out_shape=[jax.ShapeDtypeStruct(shape, F32), jax.ShapeDtypeStruct(shape, sent_as)],
        compiler_params=PARAMS,
        cost_estimate=cost,
        name="fold",
    )(flags, kept, *got)


def split_sum(kept, got):
    value = kept[...] + got[...].astype(F32)
    high = value.astype(BF16)
    return high, (value - high.astype(F32)).astype(BF16)


def scores_body(places, units, *refs):
    sums, grads, outs = refs[: 2 * units], refs[2 * units :][: len(places)], refs[-units:]
    rows = sums[0].shape[0]
    precond = jnp.concatenate(
        [part for u in range(units) for part in split_sum(sums[2 * u], sums[2 * u + 1])]
    )
    for grad, (r, first) in zip(grads, places):
        both = dot_t(grad[...], precond)
        for u in range(units):
            value = both[:, 2 * u * rows :][:, :rows] + both[:, (2 * u + 1) * rows :][:, :rows]
            outs[u][r, first : first + grad.shape[0]] = value.astype(outs[u].dtype)


def partial_scores(units, grads, out_as, cost):
    rows = units[0][0].shape[0]
    train_rows = grads[0][2].shape[0]
    return pl.pallas_call(
        functools.partial(scores_body, [piece[:2] for piece in grads], len(units)),
        in_specs=[VMEM] * (2 * len(units) + len(grads)),
        out_specs=[VMEM] * len(units),
        out_shape=[jax.ShapeDtypeStruct((4, train_rows, rows), kind) for kind in out_as],
        compiler_params=PARAMS,
        cost_estimate=cost,
        name="scores",
    )(*[value for unit in units for value in unit], *[piece[2] for piece in grads])


def last_scores_body(places, kept, got, counts, before, *refs):
    grads, out, chosen_out = refs[: len(places)], refs[-2], refs[-1]
    rows = kept.shape[0]
    low = places[0][0]
    train_rows = counts.shape[1]
    precond = jnp.concatenate(split_sum(kept, got))
    chosen = before[:1]
    for grad, (r, first) in zip(grads, places):
        both = dot_t(grad[...], precond)
        value = both[:, :rows] + both[:, rows:]
        place = pl.ds(first, grad.shape[0])
        out[r - low, place] = value.astype(BF16)
        chosen = chosen + jnp.sum(value * counts[r, place], axis=0, keepdims=True)
    chosen_out[...] = jnp.broadcast_to(chosen, chosen_out.shape)
    for n in range(2):
        if out.shape[1] > train_rows:
            out[n, train_rows:] = jnp.broadcast_to(chosen, (EXTRA, rows)).astype(BF16)


def last_scores(kept, got, counts, before, grads, extra):
    rows = kept.shape[0]
    return pl.pallas_call(
        functools.partial(last_scores_body, [piece[:2] for piece in grads]),
        in_specs=[VMEM] * (4 + len(grads)),
        out_specs=[VMEM, VMEM],
        out_shape=[
            jax.ShapeDtypeStruct((2, counts.shape[1] + extra, rows), BF16),
            jax.ShapeDtypeStruct((8, rows), F32),
        ],
        compiler_params=PARAMS,
        cost_estimate=SMALL,
        name="last_scores",
    )(kept, got, counts, before, *[piece[2] for piece in grads])


def four_by_four(train_grads, test_grads, fisher, chosen_ids):
    z = lax.axis_index("test")
    i = lax.axis_index("train")
    chip, core = i // 2, i % 2
    inner = (z == 1) | (z == 2)
    flags = jnp.stack([core, chip, inner.astype(jnp.int32)])
    own_rows = train_grads.shape[0]
    quarter = test_grads.shape[0] // 4

    def along(value, pairs):
        return lax.ppermute(value, "test", pairs)

    def to_other(value, r):
        return lax.ppermute(value, "train", [(k, k ^ r) for k in range(4)])

    def tied(*values):
        return lax.optimization_barrier(values)

    pair = [(0, 1), (1, 0), (2, 3), (3, 2)]
    middle = [(1, 2), (2, 1)]
    outward = [(1, 0), (2, 3)]
    inward = [(0, 1), (3, 2)]

    def core_sum(kept, *sent, sent_as=BF16, cost=SMALL):
        return fold(flags, kept, [to_other(part, 1) for part in sent], sent_as, cost)

    def scores_of(*units, out_as=(BF16, BF16), cost=SMALL):
        pieces = [(*place, grad) for place, grad in zip(places, grads)]
        return partial_scores(units, pieces, out_as[: len(units)], cost)

    def in_order(parts):
        parts = [parts[0], parts[2], parts[1], parts[3]]
        parts = [jnp.where(chip == 0, parts[q], parts[q ^ 1]) for q in range(4)]
        parts = [jnp.where(core == 0, parts[q], parts[q ^ 2]) for q in range(4)]
        return jnp.concatenate(parts, axis=1)

    row_ids = jnp.stack([i, i ^ 1, i ^ 2, i ^ 3])[:, None] * own_rows + jnp.arange(own_rows)

    def selected(ids):
        ids = lax.dynamic_slice_in_dim(ids, (core * 2 + chip) * quarter, quarter).T
        return sum((ids[k] == row_ids[:, :, None]).astype(F32) for k in range(ids.shape[0]))

    pair_in = along(test_grads, pair)
    middle_in = along(test_grads, middle)
    other_core, other_chip = to_other(train_grads, 1), to_other(train_grads, 2)
    own, other_core = tied(test_grads, other_core)
    own, own_sent = core_sum(*product(flags, [own], fisher), sent_as=F32, cost=MORE)
    half = own_rows // 2
    other_both = [to_other(other_chip[:half], 1), to_other(other_chip[half:], 1)]
    grads = [train_grads, other_core, other_chip, *other_both]
    pair_in, middle_in, own, own_sent, chosen_ids, grads = tied(
        pair_in, middle_in, own, own_sent, chosen_ids, grads
    )
    places = ((0, 0), (1, 0), (2, 0), (3, 0), (3, half))

    second_edge = along(middle_in, outward)
    far_in = along(pair_in, middle)
    near, near_sent = core_sum(*product(flags, [middle_in, pair_in], fisher))
    own_got = to_other(own_sent, 2)
    near_sent, own_got, pair_in = tied(near_sent, own_got, pair_in)
    near_got = to_other(near_sent, 2)
    third, *third_sent = product(flags, [pair_in], fisher)
    third, second_edge = tied(third, second_edge)
    third, third_sent = core_sum(third, *third_sent, cost=SOME)
    (near,) = scores_of((near, near_got), cost=SOME)
    counts = selected(chosen_ids)
    far_in, second_edge, third, third_sent, own, own_got, near, counts, chosen_ids, grads = tied(
        far_in, second_edge, third, third_sent, own, own_got, near, counts, chosen_ids, grads
    )

    first_edge = along(far_in, outward)
    second, second_sent = core_sum(*product(flags, [far_in, second_edge], fisher))
    second, second_sent, near = tied(second, second_sent, near)
    second_got = to_other(second_sent, 2)
    near_in, near_across = along(near, inward), along(near, middle)
    second_got, near_in, near_across, chosen_ids = tied(
        second_got, near_in, near_across, chosen_ids
    )
    far_ids = along(chosen_ids, [(0, 3), (3, 0)])
    (second,) = scores_of((second, second_got))
    across = along(second, middle)
    third, total = scores_of(
        (third, to_other(third_sent, 2)), (own, own_got), out_as=(F32, F32)
    )
    first_edge, total, near_in, near_across, second, across, third, grads, far_ids = tied(
        first_edge, total, near_in, near_across, second, across, third, grads, far_ids
    )
    far_counts = selected(far_ids)

    last, last_sent = core_sum(*product(flags, [first_edge], fisher))
    last, second, third = tied(last, second, third)
    third = along((third + across.astype(F32)).astype(BF16), outward)
    second = along(second, [(0, 2), (3, 1)])
    last_got = to_other(last_sent, 2)
    ends = [(0, 3), (3, 0)]
    none = jnp.zeros((8, quarter), F32)
    pieces = [(*place, grad) for place, grad in zip(places, grads)]
    away, chosen = last_scores(last, last_got, far_counts, none, pieces[2:], 0)
    away = along(away, ends)
    away = [to_other(away[0], 2), to_other(away[1], 3)]
    here, _ = last_scores(last, last_got, far_counts, chosen, pieces[:2], EXTRA)
    here, second, third = tied(here, second, third)
    here = along(here, ends)
    here = [here[0], to_other(here[1], 1)]
    chosen = [part[own_rows:] for part in here]
    chosen += [to_other(chosen[0], 2), to_other(chosen[0], 3)]
    last = in_order([part[:own_rows] for part in here] + away)
    last_chosen = in_order(chosen)[0]

    total = total + sum(value.astype(F32) for value in (near_in, near_across, second, third))
    chosen = jnp.sum(total * counts, axis=(0, 1))
    total = [jnp.concatenate([part, jnp.broadcast_to(chosen, (8, quarter))]) for part in total]
    total = in_order([total[0]] + [to_other(total[r], r) for r in range(1, 4)])

    scores = total[:own_rows] + last.astype(F32)
    return scores, total[own_rows] + last_chosen.astype(F32)


def solution(mesh):
    sizes = (mesh.shape["train"], mesh.shape["test"])
    return jax.shard_map(
        four_by_four if sizes == (4, 4) else any_mesh,
        mesh=mesh,
        in_specs=(
            P(("groups", "train"), "test"),
            P(("groups", "test"), "train"),
            P("train", "test"),
            P(("groups", "test"), None),
        ),
        out_specs=(P(("groups", "train"), "test"), P(("groups", "test"))),
        check_vma=False,
    )
```

```python
import functools

import jax
import jax.numpy as jnp
from jax import lax
from jax.experimental import pallas as pl
from jax.experimental.pallas import tpu as pltpu
from jax.sharding import PartitionSpec as P

COLUMNS = 512
EXTRA = 16

F32 = jnp.float32
BF16 = jnp.bfloat16


def dot_t(a, b):
    return lax.dot_general(a, b, (((1,), (1,)), ((), ())), preferred_element_type=F32)


def selection_counts(chosen_ids, first_row, rows):
    row_ids = first_row + lax.broadcasted_iota(jnp.int32, (rows, chosen_ids.shape[0]), 0)
    ids = chosen_ids.T
    counts = jnp.zeros(row_ids.shape, F32)
    for k in range(ids.shape[0]):
        counts = counts + (row_ids == ids[k][None, :]).astype(F32)
    return counts


def any_mesh(train_grads, test_grads, fisher, chosen_ids):
    test_whole = lax.all_gather(test_grads, "test", axis=0, tiled=True)
    partial_value = jnp.dot(test_whole, fisher, preferred_element_type=F32)
    precond = lax.psum(partial_value, "train").astype(BF16)
    partial_scores = dot_t(train_grads, precond)
    scores = lax.psum_scatter(partial_scores, "test", scatter_dimension=1, tiled=True)
    rows = scores.shape[0]
    counts = selection_counts(chosen_ids, lax.axis_index("train") * rows, rows)
    return scores, lax.psum(jnp.sum(counts * scores, axis=0), "train")


SMALL = pl.CostEstimate(flops=1, bytes_accessed=1, transcendentals=0)
SOME = pl.CostEstimate(flops=2 * 10**9, bytes_accessed=2**20, transcendentals=0)
MORE = pl.CostEstimate(flops=7 * 10**9, bytes_accessed=2**20, transcendentals=0)
PARAMS = pltpu.CompilerParams(vmem_limit_bytes=12 * 2**20)


VMEM = pl.BlockSpec(memory_space=pltpu.VMEM)


def product_body(count, flags, *refs):
    blocks, fisher, outs = refs[:count], refs[count], refs[count + 1 :]
    quarter = blocks[0].shape[0] // 4
    mine = flags[0] == 0

    def multiply(block, kept, *sent):
        @pl.loop(0, fisher.shape[1] // COLUMNS)
        def _(n):
            columns = pl.ds(pl.multiple_of(n * COLUMNS, COLUMNS), COLUMNS)
            value = jnp.dot(block[...], fisher[:, columns], preferred_element_type=F32)
            for chip in range(2):
                low, high = (value[(2 * core + chip) * quarter :][:quarter] for core in range(2))
                kept[pl.ds(chip * quarter, quarter), columns] = jnp.where(mine, low, high)
                other = jnp.where(mine, high, low).astype(BF16)
                if len(sent) == 2:
                    sent[chip][:, columns] = other
                else:
                    sent[0][pl.ds(chip * quarter, quarter), columns] = other

    if len(blocks) == 1:
        multiply(blocks[0], *outs)
    else:
        pl.when(flags[2] == 1)(lambda: multiply(blocks[0], *outs))
        pl.when(flags[2] == 0)(lambda: multiply(blocks[1], *outs))


def product(flags, blocks, fisher, ways=2):
    half = blocks[0].shape[0] // 2
    columns = fisher.shape[1]
    sent = jax.ShapeDtypeStruct((half // ways, columns), BF16)
    return pl.pallas_call(
        functools.partial(product_body, len(blocks)),
        in_specs=[pl.BlockSpec(memory_space=pltpu.SMEM)] + [VMEM] * (len(blocks) + 1),
        out_specs=[VMEM] * (1 + ways),
        out_shape=[jax.ShapeDtypeStruct((half, columns), F32)] + [sent] * ways,
        compiler_params=PARAMS,
        cost_estimate=SMALL,
        name="product",
    )(flags, *blocks, fisher)


def fold_body(flags, kept, *refs):
    got, kept_out, sent_out = refs[:-2], refs[-2], refs[-1]
    half = kept_out.shape[0]
    first = flags[1] == 0

    @pl.loop(0, kept.shape[1] // COLUMNS)
    def _(n):
        columns = pl.ds(pl.multiple_of(n * COLUMNS, COLUMNS), COLUMNS)
        if len(got) == 2:
            low, high = got[0][:, columns], got[1][:, columns]
        else:
            low, high = got[0][:half, columns], got[0][half:, columns]
        low = kept[:half, columns] + low.astype(F32)
        high = kept[half:, columns] + high.astype(F32)
        kept_out[:, columns] = jnp.where(first, low, high)
        sent_out[:, columns] = jnp.where(first, high, low).astype(sent_out.dtype)


def fold(flags, kept, got, sent_as, cost):
    shape = (kept.shape[0] // 2, kept.shape[1])
    return pl.pallas_call(
        fold_body,
        in_specs=[pl.BlockSpec(memory_space=pltpu.SMEM)] + [VMEM] * (1 + len(got)),
        out_specs=[VMEM, VMEM],
        out_shape=[jax.ShapeDtypeStruct(shape, F32), jax.ShapeDtypeStruct(shape, sent_as)],
        compiler_params=PARAMS,
        cost_estimate=cost,
        name="fold",
    )(flags, kept, *got)


def split_sum(kept, got):
    value = kept[...] + got[...].astype(F32)
    high = value.astype(BF16)
    return high, (value - high.astype(F32)).astype(BF16)


def scores_body(places, units, *refs):
    sums, grads, outs = refs[: 2 * units], refs[2 * units :][: len(places)], refs[-units:]
    rows = sums[0].shape[0]
    precond = jnp.concatenate(
        [part for u in range(units) for part in split_sum(sums[2 * u], sums[2 * u + 1])]
    )
    for grad, (r, first) in zip(grads, places):
        both = dot_t(grad[...], precond)
        for u in range(units):
            value = both[:, 2 * u * rows :][:, :rows] + both[:, (2 * u + 1) * rows :][:, :rows]
            outs[u][r, first : first + grad.shape[0]] = value.astype(outs[u].dtype)


def partial_scores(units, grads, out_as, cost):
    rows = units[0][0].shape[0]
    train_rows = grads[0][2].shape[0]
    return pl.pallas_call(
        functools.partial(scores_body, [piece[:2] for piece in grads], len(units)),
        in_specs=[VMEM] * (2 * len(units) + len(grads)),
        out_specs=[VMEM] * len(units),
        out_shape=[jax.ShapeDtypeStruct((4, train_rows, rows), kind) for kind in out_as],
        compiler_params=PARAMS,
        cost_estimate=cost,
        name="scores",
    )(*[value for unit in units for value in unit], *[piece[2] for piece in grads])


def last_scores_body(places, kept, got, counts, before, *refs):
    grads, out, chosen_out = refs[: len(places)], refs[-2], refs[-1]
    rows = kept.shape[0]
    low = places[0][0]
    train_rows = counts.shape[1]
    precond = jnp.concatenate(split_sum(kept, got))
    chosen = before[:1]
    for grad, (r, first) in zip(grads, places):
        both = dot_t(grad[...], precond)
        value = both[:, :rows] + both[:, rows:]
        place = pl.ds(first, grad.shape[0])
        out[r - low, place] = value.astype(BF16)
        chosen = chosen + jnp.sum(value * counts[r, place], axis=0, keepdims=True)
    chosen_out[...] = jnp.broadcast_to(chosen, chosen_out.shape)
    for n in range(2):
        if out.shape[1] > train_rows:
            out[n, train_rows:] = jnp.broadcast_to(chosen, (EXTRA, rows)).astype(BF16)


def last_scores(kept, got, counts, before, grads, extra):
    rows = kept.shape[0]
    return pl.pallas_call(
        functools.partial(last_scores_body, [piece[:2] for piece in grads]),
        in_specs=[VMEM] * (4 + len(grads)),
        out_specs=[VMEM, VMEM],
        out_shape=[
            jax.ShapeDtypeStruct((2, counts.shape[1] + extra, rows), BF16),
            jax.ShapeDtypeStruct((8, rows), F32),
        ],
        compiler_params=PARAMS,
        cost_estimate=SMALL,
        name="last_scores",
    )(kept, got, counts, before, *[piece[2] for piece in grads])


def hold_body(*refs):
    for n in range(len(refs) // 2):
        refs[len(refs) // 2 + n][...] = refs[n][...]


def hold(values):
    return pl.pallas_call(
        hold_body,
        in_specs=[VMEM] * len(values),
        out_specs=[VMEM] * len(values),
        out_shape=[jax.ShapeDtypeStruct(value.shape, value.dtype) for value in values],
        compiler_params=PARAMS,
        cost_estimate=SMALL,
        name="hold",
    )(*values)


def four_by_four(train_grads, test_grads, fisher, chosen_ids):
    z = lax.axis_index("test")
    i = lax.axis_index("train")
    chip, core = i // 2, i % 2
    inner = (z == 1) | (z == 2)
    flags = jnp.stack([core, chip, inner.astype(jnp.int32)])
    own_rows = train_grads.shape[0]
    quarter = test_grads.shape[0] // 4

    def along(value, pairs):
        return lax.ppermute(value, "test", pairs)

    def to_other(value, r):
        return lax.ppermute(value, "train", [(k, k ^ r) for k in range(4)])

    def tied(*values):
        return lax.optimization_barrier(values)

    pair = [(0, 1), (1, 0), (2, 3), (3, 2)]
    middle = [(1, 2), (2, 1)]
    outward = [(1, 0), (2, 3)]
    inward = [(0, 1), (3, 2)]

    def core_sum(kept, *sent, sent_as=BF16, cost=SMALL):
        return fold(flags, kept, [to_other(part, 1) for part in sent], sent_as, cost)

    def scores_of(*units, out_as=(BF16, BF16), cost=SMALL):
        pieces = [(*place, grad) for place, grad in zip(places, grads)]
        return partial_scores(units, pieces, out_as[: len(units)], cost)

    def in_order(parts):
        parts = [parts[0], parts[2], parts[1], parts[3]]
        parts = [jnp.where(chip == 0, parts[q], parts[q ^ 1]) for q in range(4)]
        parts = [jnp.where(core == 0, parts[q], parts[q ^ 2]) for q in range(4)]
        return jnp.concatenate(parts, axis=1)

    row_ids = jnp.stack([i, i ^ 1, i ^ 2, i ^ 3])[:, None] * own_rows + jnp.arange(own_rows)

    def selected(ids):
        ids = lax.dynamic_slice_in_dim(ids, (core * 2 + chip) * quarter, quarter).T
        return sum((ids[k] == row_ids[:, :, None]).astype(F32) for k in range(ids.shape[0]))

    pair_in = along(test_grads, pair)
    middle_in = along(test_grads, middle)
    other_core, other_chip = to_other(train_grads, 1), to_other(train_grads, 2)
    mine, other_core = hold([train_grads, other_core])
    own, mine, other_core = tied(test_grads, mine, other_core)
    own, own_sent = core_sum(*product(flags, [own], fisher), sent_as=F32, cost=MORE)
    half = own_rows // 2
    other_both = [to_other(other_chip[:half], 1), to_other(other_chip[half:], 1)]
    grads = [mine, other_core, other_chip, *other_both]
    pair_in, middle_in, own, own_sent, chosen_ids, grads = tied(
        pair_in, middle_in, own, own_sent, chosen_ids, grads
    )
    places = ((0, 0), (1, 0), (2, 0), (3, 0), (3, half))

    second_edge = along(middle_in, outward)
    far_in = along(pair_in, middle)
    near, near_sent = core_sum(*product(flags, [middle_in, pair_in], fisher))
    own_got = to_other(own_sent, 2)
    near_sent, own_got, pair_in = tied(near_sent, own_got, pair_in)
    near_got = to_other(near_sent, 2)
    third, third_sent = core_sum(*product(flags, [pair_in], fisher))
    (near,) = scores_of((near, near_got), cost=SOME)
    far_ids = along(chosen_ids, [(0, 3), (3, 0)])
    counts = selected(chosen_ids)
    far_in, second_edge, third, third_sent, own, own_got, near, far_ids, counts, grads = tied(
        far_in, second_edge, third, third_sent, own, own_got, near, far_ids, counts, grads
    )

    first_edge = along(far_in, outward)
    second, second_sent = core_sum(*product(flags, [far_in, second_edge], fisher))
    second, second_sent, near = tied(second, second_sent, near)
    second_got = to_other(second_sent, 2)
    near_in, near_across = along(near, inward), along(near, middle)
    second_got, near_in, near_across = tied(second_got, near_in, near_across)
    (second,) = scores_of((second, second_got))
    across = along(second, middle)
    third, total = scores_of(
        (third, to_other(third_sent, 2)), (own, own_got), out_as=(F32, F32)
    )
    far_counts = selected(far_ids)
    first_edge, total, near_in, near_across, second, across, third, grads, far_counts = tied(
        first_edge, total, near_in, near_across, second, across, third, grads, far_counts
    )

    third = along((third + across.astype(F32)).astype(BF16), outward)
    second = along(second, [(0, 2), (3, 1)])
    last, last_sent = core_sum(*product(flags, [first_edge], fisher))
    last_got = to_other(last_sent, 2)
    ends = [(0, 3), (3, 0)]
    none = jnp.zeros((8, quarter), F32)
    pieces = [(*place, grad) for place, grad in zip(places, grads)]
    away, chosen = last_scores(last, last_got, far_counts, none, pieces[2:], 0)
    away = along(away, ends)
    away = [to_other(away[0], 2), to_other(away[1], 3)]
    here, _ = last_scores(last, last_got, far_counts, chosen, pieces[:2], EXTRA)
    here, second, third = tied(here, second, third)
    here = along(here, ends)
    here = [here[0], to_other(here[1], 1)]
    chosen = [part[own_rows:] for part in here]
    chosen += [to_other(chosen[0], 2), to_other(chosen[0], 3)]
    last = in_order([part[:own_rows] for part in here] + away)
    last_chosen = in_order(chosen)[0]

    total = total + sum(value.astype(F32) for value in (near_in, near_across, second, third))
    chosen = jnp.sum(total * counts, axis=(0, 1))
    total = [jnp.concatenate([part, jnp.broadcast_to(chosen, (8, quarter))]) for part in total]
    total = in_order([total[0]] + [to_other(total[r], r) for r in range(1, 4)])

    scores = total[:own_rows] + last.astype(F32)
    return scores, total[own_rows] + last_chosen.astype(F32)


def solution(mesh):
    sizes = (mesh.shape["train"], mesh.shape["test"])
    return jax.shard_map(
        four_by_four if sizes == (4, 4) else any_mesh,
        mesh=mesh,
        in_specs=(
            P(("groups", "train"), "test"),
            P(("groups", "test"), "train"),
            P("train", "test"),
            P(("groups", "test"), None),
        ),
        out_specs=(P(("groups", "train"), "test"), P(("groups", "test"))),
        check_vma=False,
    )
```

```python
import functools

import jax
import jax.numpy as jnp
from jax import lax
from jax.experimental import pallas as pl
from jax.experimental.pallas import tpu as pltpu
from jax.sharding import PartitionSpec as P

COLUMNS = 512
EXTRA = 16

F32 = jnp.float32
BF16 = jnp.bfloat16


def dot_t(a, b):
    return lax.dot_general(a, b, (((1,), (1,)), ((), ())), preferred_element_type=F32)


def selection_counts(chosen_ids, first_row, rows):
    row_ids = first_row + lax.broadcasted_iota(jnp.int32, (rows, chosen_ids.shape[0]), 0)
    ids = chosen_ids.T
    counts = jnp.zeros(row_ids.shape, F32)
    for k in range(ids.shape[0]):
        counts = counts + (row_ids == ids[k][None, :]).astype(F32)
    return counts


def any_mesh(train_grads, test_grads, fisher, chosen_ids):
    test_whole = lax.all_gather(test_grads, "test", axis=0, tiled=True)
    partial_value = jnp.dot(test_whole, fisher, preferred_element_type=F32)
    precond = lax.psum(partial_value, "train").astype(BF16)
    partial_scores = dot_t(train_grads, precond)
    scores = lax.psum_scatter(partial_scores, "test", scatter_dimension=1, tiled=True)
    rows = scores.shape[0]
    counts = selection_counts(chosen_ids, lax.axis_index("train") * rows, rows)
    return scores, lax.psum(jnp.sum(counts * scores, axis=0), "train")


SMALL = pl.CostEstimate(flops=1, bytes_accessed=1, transcendentals=0)
SOME = pl.CostEstimate(flops=2 * 10**9, bytes_accessed=2**20, transcendentals=0)
MORE = pl.CostEstimate(flops=7 * 10**9, bytes_accessed=2**20, transcendentals=0)
PARAMS = pltpu.CompilerParams(vmem_limit_bytes=12 * 2**20)


VMEM = pl.BlockSpec(memory_space=pltpu.VMEM)


def product_body(count, flags, *refs):
    blocks, fisher, outs = refs[:count], refs[count], refs[count + 1 :]
    quarter = blocks[0].shape[0] // 4
    mine = flags[0] == 0

    def multiply(block, kept, *sent):
        @pl.loop(0, fisher.shape[1] // COLUMNS)
        def _(n):
            columns = pl.ds(pl.multiple_of(n * COLUMNS, COLUMNS), COLUMNS)
            value = jnp.dot(block[...], fisher[:, columns], preferred_element_type=F32)
            for chip in range(2):
                low, high = (value[(2 * core + chip) * quarter :][:quarter] for core in range(2))
                kept[pl.ds(chip * quarter, quarter), columns] = jnp.where(mine, low, high)
                other = jnp.where(mine, high, low).astype(BF16)
                if len(sent) == 2:
                    sent[chip][:, columns] = other
                else:
                    sent[0][pl.ds(chip * quarter, quarter), columns] = other

    if len(blocks) == 1:
        multiply(blocks[0], *outs)
    else:
        pl.when(flags[2] == 1)(lambda: multiply(blocks[0], *outs))
        pl.when(flags[2] == 0)(lambda: multiply(blocks[1], *outs))


def product(flags, blocks, fisher, ways=2):
    half = blocks[0].shape[0] // 2
    columns = fisher.shape[1]
    sent = jax.ShapeDtypeStruct((half // ways, columns), BF16)
    return pl.pallas_call(
        functools.partial(product_body, len(blocks)),
        in_specs=[pl.BlockSpec(memory_space=pltpu.SMEM)] + [VMEM] * (len(blocks) + 1),
        out_specs=[VMEM] * (1 + ways),
        out_shape=[jax.ShapeDtypeStruct((half, columns), F32)] + [sent] * ways,
        compiler_params=PARAMS,
        cost_estimate=SMALL,
        name="product",
    )(flags, *blocks, fisher)


def fold_body(flags, kept, *refs):
    got, kept_out, sent_out = refs[:-2], refs[-2], refs[-1]
    half = kept_out.shape[0]
    first = flags[1] == 0

    @pl.loop(0, kept.shape[1] // COLUMNS)
    def _(n):
        columns = pl.ds(pl.multiple_of(n * COLUMNS, COLUMNS), COLUMNS)
        if len(got) == 2:
            low, high = got[0][:, columns], got[1][:, columns]
        else:
            low, high = got[0][:half, columns], got[0][half:, columns]
        low = kept[:half, columns] + low.astype(F32)
        high = kept[half:, columns] + high.astype(F32)
        kept_out[:, columns] = jnp.where(first, low, high)
        sent_out[:, columns] = jnp.where(first, high, low).astype(sent_out.dtype)


def fold(flags, kept, got, sent_as, cost):
    shape = (kept.shape[0] // 2, kept.shape[1])
    return pl.pallas_call(
        fold_body,
        in_specs=[pl.BlockSpec(memory_space=pltpu.SMEM)] + [VMEM] * (1 + len(got)),
        out_specs=[VMEM, VMEM],
        out_shape=[jax.ShapeDtypeStruct(shape, F32), jax.ShapeDtypeStruct(shape, sent_as)],
        compiler_params=PARAMS,
        cost_estimate=cost,
        name="fold",
    )(flags, kept, *got)


def split_sum(kept, got):
    value = kept[...] + got[...].astype(F32)
    high = value.astype(BF16)
    return high, (value - high.astype(F32)).astype(BF16)


def scores_body(places, units, *refs):
    sums, grads, outs = refs[: 2 * units], refs[2 * units :][: len(places)], refs[-units:]
    rows = sums[0].shape[0]
    precond = jnp.concatenate(
        [part for u in range(units) for part in split_sum(sums[2 * u], sums[2 * u + 1])]
    )
    for grad, (r, first) in zip(grads, places):
        both = dot_t(grad[...], precond)
        for u in range(units):
            value = both[:, 2 * u * rows :][:, :rows] + both[:, (2 * u + 1) * rows :][:, :rows]
            outs[u][r, first : first + grad.shape[0]] = value.astype(outs[u].dtype)


def partial_scores(units, grads, out_as, cost):
    rows = units[0][0].shape[0]
    train_rows = grads[0][2].shape[0]
    return pl.pallas_call(
        functools.partial(scores_body, [piece[:2] for piece in grads], len(units)),
        in_specs=[VMEM] * (2 * len(units) + len(grads)),
        out_specs=[VMEM] * len(units),
        out_shape=[jax.ShapeDtypeStruct((4, train_rows, rows), kind) for kind in out_as],
        compiler_params=PARAMS,
        cost_estimate=cost,
        name="scores",
    )(*[value for unit in units for value in unit], *[piece[2] for piece in grads])


def last_scores_body(places, kept, got, counts, before, *refs):
    grads, out, chosen_out = refs[: len(places)], refs[-2], refs[-1]
    rows = kept.shape[0]
    low = places[0][0]
    train_rows = counts.shape[1]
    precond = jnp.concatenate(split_sum(kept, got))
    chosen = before[:1]
    for grad, (r, first) in zip(grads, places):
        both = dot_t(grad[...], precond)
        value = both[:, :rows] + both[:, rows:]
        place = pl.ds(first, grad.shape[0])
        out[r - low, place] = value.astype(BF16)
        chosen = chosen + jnp.sum(value * counts[r, place], axis=0, keepdims=True)
    chosen_out[...] = jnp.broadcast_to(chosen, chosen_out.shape)
    for n in range(2):
        if out.shape[1] > train_rows:
            out[n, train_rows:] = jnp.broadcast_to(chosen, (EXTRA, rows)).astype(BF16)


def last_scores(kept, got, counts, before, grads, extra):
    rows = kept.shape[0]
    return pl.pallas_call(
        functools.partial(last_scores_body, [piece[:2] for piece in grads]),
        in_specs=[VMEM] * (4 + len(grads)),
        out_specs=[VMEM, VMEM],
        out_shape=[
            jax.ShapeDtypeStruct((2, counts.shape[1] + extra, rows), BF16),
            jax.ShapeDtypeStruct((8, rows), F32),
        ],
        compiler_params=PARAMS,
        cost_estimate=SOME,
        name="last_scores",
    )(kept, got, counts, before, *[piece[2] for piece in grads])


def hold_body(*refs):
    for n in range(len(refs) // 2):
        refs[len(refs) // 2 + n][...] = refs[n][...]


def hold(values):
    return pl.pallas_call(
        hold_body,
        in_specs=[VMEM] * len(values),
        out_specs=[VMEM] * len(values),
        out_shape=[jax.ShapeDtypeStruct(value.shape, value.dtype) for value in values],
        compiler_params=PARAMS,
        cost_estimate=SMALL,
        name="hold",
    )(*values)


def four_by_four(train_grads, test_grads, fisher, chosen_ids):
    z = lax.axis_index("test")
    i = lax.axis_index("train")
    chip, core = i // 2, i % 2
    inner = (z == 1) | (z == 2)
    flags = jnp.stack([core, chip, inner.astype(jnp.int32)])
    own_rows = train_grads.shape[0]
    quarter = test_grads.shape[0] // 4

    def along(value, pairs):
        return lax.ppermute(value, "test", pairs)

    def to_other(value, r):
        return lax.ppermute(value, "train", [(k, k ^ r) for k in range(4)])

    def tied(*values):
        return lax.optimization_barrier(values)

    pair = [(0, 1), (1, 0), (2, 3), (3, 2)]
    middle = [(1, 2), (2, 1)]
    outward = [(1, 0), (2, 3)]
    inward = [(0, 1), (3, 2)]

    def core_sum(kept, *sent, sent_as=BF16, cost=SMALL):
        return fold(flags, kept, [to_other(part, 1) for part in sent], sent_as, cost)

    def scores_of(*units, out_as=(BF16, BF16), cost=SMALL):
        pieces = [(*place, grad) for place, grad in zip(places, grads)]
        return partial_scores(units, pieces, out_as[: len(units)], cost)

    def in_order(parts):
        parts = [parts[0], parts[2], parts[1], parts[3]]
        parts = [jnp.where(chip == 0, parts[q], parts[q ^ 1]) for q in range(4)]
        parts = [jnp.where(core == 0, parts[q], parts[q ^ 2]) for q in range(4)]
        return jnp.concatenate(parts, axis=1)

    row_ids = jnp.stack([i, i ^ 1, i ^ 2, i ^ 3])[:, None] * own_rows + jnp.arange(own_rows)

    def selected(ids):
        ids = lax.dynamic_slice_in_dim(ids, (core * 2 + chip) * quarter, quarter).T
        return sum((ids[k] == row_ids[:, :, None]).astype(F32) for k in range(ids.shape[0]))

    pair_in = along(test_grads, pair)
    middle_in = along(test_grads, middle)
    other_core, other_chip = to_other(train_grads, 1), to_other(train_grads, 2)
    mine, other_core = hold([train_grads, other_core])
    own, mine, other_core = tied(test_grads, mine, other_core)
    own, own_sent = core_sum(*product(flags, [own], fisher), sent_as=F32, cost=MORE)
    half = own_rows // 2
    other_both = [to_other(other_chip[:half], 1), to_other(other_chip[half:], 1)]
    grads = [mine, other_core, other_chip, *other_both]
    pair_in, middle_in, own, own_sent, chosen_ids, grads = tied(
        pair_in, middle_in, own, own_sent, chosen_ids, grads
    )
    places = ((0, 0), (1, 0), (2, 0), (3, 0), (3, half))

    second_edge = along(middle_in, outward)
    far_in = along(pair_in, middle)
    near, near_sent = core_sum(*product(flags, [middle_in, pair_in], fisher))
    own_got = to_other(own_sent, 2)
    near_sent, own_got, pair_in = tied(near_sent, own_got, pair_in)
    near_got = to_other(near_sent, 2)
    third, third_sent = core_sum(*product(flags, [pair_in], fisher))
    (near,) = scores_of((near, near_got), cost=SOME)
    counts = selected(chosen_ids)
    far_in, second_edge, third, third_sent, own, own_got, near, counts, chosen_ids, grads = tied(
        far_in, second_edge, third, third_sent, own, own_got, near, counts, chosen_ids, grads
    )

    first_edge = along(far_in, outward)
    second, second_sent = core_sum(*product(flags, [far_in, second_edge], fisher))
    second, second_sent, near = tied(second, second_sent, near)
    second_got = to_other(second_sent, 2)
    near_in, near_across = along(near, inward), along(near, middle)
    second_got, near_in, near_across, chosen_ids = tied(
        second_got, near_in, near_across, chosen_ids
    )
    far_ids = along(chosen_ids, [(0, 3), (3, 0)])
    (second,) = scores_of((second, second_got))
    across = along(second, middle)
    third, total = scores_of(
        (third, to_other(third_sent, 2)), (own, own_got), out_as=(F32, F32)
    )
    first_edge, total, near_in, near_across, second, across, third, grads, far_ids = tied(
        first_edge, total, near_in, near_across, second, across, third, grads, far_ids
    )
    far_counts = selected(far_ids)

    last, last_sent = core_sum(*product(flags, [first_edge], fisher))
    last, second, third = tied(last, second, third)
    third = along((third + across.astype(F32)).astype(BF16), outward)
    second = along(second, [(0, 2), (3, 1)])
    last_got = to_other(last_sent, 2)
    ends = [(0, 3), (3, 0)]
    none = jnp.zeros((8, quarter), F32)
    pieces = [(*place, grad) for place, grad in zip(places, grads)]
    away, chosen = last_scores(last, last_got, far_counts, none, pieces[2:], 0)
    away = along(away, ends)
    away = [to_other(away[0], 2), to_other(away[1], 3)]
    here, _ = last_scores(last, last_got, far_counts, chosen, pieces[:2], EXTRA)
    here, second, third = tied(here, second, third)
    here = along(here, ends)
    here = [here[0], to_other(here[1], 1)]
    chosen = [part[own_rows:] for part in here]
    chosen += [to_other(chosen[0], 2), to_other(chosen[0], 3)]
    last = in_order([part[:own_rows] for part in here] + away)
    last_chosen = in_order(chosen)[0]

    total = total + sum(value.astype(F32) for value in (near_in, near_across, second, third))
    chosen = jnp.sum(total * counts, axis=(0, 1))
    total = [jnp.concatenate([part, jnp.broadcast_to(chosen, (8, quarter))]) for part in total]
    total = in_order([total[0]] + [to_other(total[r], r) for r in range(1, 4)])

    scores = total[:own_rows] + last.astype(F32)
    return scores, total[own_rows] + last_chosen.astype(F32)


def solution(mesh):
    sizes = (mesh.shape["train"], mesh.shape["test"])
    return jax.shard_map(
        four_by_four if sizes == (4, 4) else any_mesh,
        mesh=mesh,
        in_specs=(
            P(("groups", "train"), "test"),
            P(("groups", "test"), "train"),
            P("train", "test"),
            P(("groups", "test"), None),
        ),
        out_specs=(P(("groups", "train"), "test"), P(("groups", "test"))),
        check_vma=False,
    )
```

```python
import functools

import jax
import jax.numpy as jnp
from jax import lax
from jax.experimental import pallas as pl
from jax.experimental.pallas import tpu as pltpu
from jax.sharding import PartitionSpec as P

COLUMNS = 512
EXTRA = 16

F32 = jnp.float32
BF16 = jnp.bfloat16


def dot_t(a, b):
    return lax.dot_general(a, b, (((1,), (1,)), ((), ())), preferred_element_type=F32)


def selection_counts(chosen_ids, first_row, rows):
    row_ids = first_row + lax.broadcasted_iota(jnp.int32, (rows, chosen_ids.shape[0]), 0)
    ids = chosen_ids.T
    counts = jnp.zeros(row_ids.shape, F32)
    for k in range(ids.shape[0]):
        counts = counts + (row_ids == ids[k][None, :]).astype(F32)
    return counts


def any_mesh(train_grads, test_grads, fisher, chosen_ids):
    test_whole = lax.all_gather(test_grads, "test", axis=0, tiled=True)
    partial_value = jnp.dot(test_whole, fisher, preferred_element_type=F32)
    precond = lax.psum(partial_value, "train").astype(BF16)
    partial_scores = dot_t(train_grads, precond)
    scores = lax.psum_scatter(partial_scores, "test", scatter_dimension=1, tiled=True)
    rows = scores.shape[0]
    counts = selection_counts(chosen_ids, lax.axis_index("train") * rows, rows)
    return scores, lax.psum(jnp.sum(counts * scores, axis=0), "train")


SMALL = pl.CostEstimate(flops=1, bytes_accessed=1, transcendentals=0)
SOME = pl.CostEstimate(flops=2 * 10**9, bytes_accessed=2**20, transcendentals=0)
MORE = pl.CostEstimate(flops=7 * 10**9, bytes_accessed=2**20, transcendentals=0)
PARAMS = pltpu.CompilerParams(vmem_limit_bytes=12 * 2**20)


VMEM = pl.BlockSpec(memory_space=pltpu.VMEM)


def product_body(count, flags, *refs):
    blocks, fisher, outs = refs[:count], refs[count], refs[count + 1 :]
    quarter = blocks[0].shape[0] // 4
    mine = flags[0] == 0

    def multiply(block, kept, *sent):
        @pl.loop(0, fisher.shape[1] // COLUMNS)
        def _(n):
            columns = pl.ds(pl.multiple_of(n * COLUMNS, COLUMNS), COLUMNS)
            value = jnp.dot(block[...], fisher[:, columns], preferred_element_type=F32)
            for chip in range(2):
                low, high = (value[(2 * core + chip) * quarter :][:quarter] for core in range(2))
                kept[pl.ds(chip * quarter, quarter), columns] = jnp.where(mine, low, high)
                other = jnp.where(mine, high, low).astype(BF16)
                if len(sent) == 2:
                    sent[chip][:, columns] = other
                else:
                    sent[0][pl.ds(chip * quarter, quarter), columns] = other

    if len(blocks) == 1:
        multiply(blocks[0], *outs)
    else:
        pl.when(flags[2] == 1)(lambda: multiply(blocks[0], *outs))
        pl.when(flags[2] == 0)(lambda: multiply(blocks[1], *outs))


def product(flags, blocks, fisher, ways=2):
    half = blocks[0].shape[0] // 2
    columns = fisher.shape[1]
    sent = jax.ShapeDtypeStruct((half // ways, columns), BF16)
    return pl.pallas_call(
        functools.partial(product_body, len(blocks)),
        in_specs=[pl.BlockSpec(memory_space=pltpu.SMEM)] + [VMEM] * (len(blocks) + 1),
        out_specs=[VMEM] * (1 + ways),
        out_shape=[jax.ShapeDtypeStruct((half, columns), F32)] + [sent] * ways,
        compiler_params=PARAMS,
        cost_estimate=SMALL,
        name="product",
    )(flags, *blocks, fisher)


def fold_body(flags, kept, *refs):
    got, kept_out, sent_out = refs[:-2], refs[-2], refs[-1]
    half = kept_out.shape[0]
    first = flags[1] == 0

    @pl.loop(0, kept.shape[1] // COLUMNS)
    def _(n):
        columns = pl.ds(pl.multiple_of(n * COLUMNS, COLUMNS), COLUMNS)
        if len(got) == 2:
            low, high = got[0][:, columns], got[1][:, columns]
        else:
            low, high = got[0][:half, columns], got[0][half:, columns]
        low = kept[:half, columns] + low.astype(F32)
        high = kept[half:, columns] + high.astype(F32)
        kept_out[:, columns] = jnp.where(first, low, high)
        sent_out[:, columns] = jnp.where(first, high, low).astype(sent_out.dtype)


def fold(flags, kept, got, sent_as, cost):
    shape = (kept.shape[0] // 2, kept.shape[1])
    return pl.pallas_call(
        fold_body,
        in_specs=[pl.BlockSpec(memory_space=pltpu.SMEM)] + [VMEM] * (1 + len(got)),
        out_specs=[VMEM, VMEM],
        out_shape=[jax.ShapeDtypeStruct(shape, F32), jax.ShapeDtypeStruct(shape, sent_as)],
        compiler_params=PARAMS,
        cost_estimate=cost,
        name="fold",
    )(flags, kept, *got)


def split_sum(kept, got):
    value = kept[...] + got[...].astype(F32)
    high = value.astype(BF16)
    return high, (value - high.astype(F32)).astype(BF16)


def scores_body(places, units, *refs):
    sums, grads, outs = refs[: 2 * units], refs[2 * units :][: len(places)], refs[-units:]
    rows = sums[0].shape[0]
    precond = jnp.concatenate(
        [part for u in range(units) for part in split_sum(sums[2 * u], sums[2 * u + 1])]
    )
    for grad, (r, first) in zip(grads, places):
        both = dot_t(grad[...], precond)
        for u in range(units):
            value = both[:, 2 * u * rows :][:, :rows] + both[:, (2 * u + 1) * rows :][:, :rows]
            outs[u][r, first : first + grad.shape[0]] = value.astype(outs[u].dtype)


def partial_scores(units, grads, out_as, cost):
    rows = units[0][0].shape[0]
    train_rows = grads[0][2].shape[0]
    return pl.pallas_call(
        functools.partial(scores_body, [piece[:2] for piece in grads], len(units)),
        in_specs=[VMEM] * (2 * len(units) + len(grads)),
        out_specs=[VMEM] * len(units),
        out_shape=[jax.ShapeDtypeStruct((4, train_rows, rows), kind) for kind in out_as],
        compiler_params=PARAMS,
        cost_estimate=cost,
        name="scores",
    )(*[value for unit in units for value in unit], *[piece[2] for piece in grads])


def last_scores_body(places, kept, got, counts, before, *refs):
    grads, out, chosen_out = refs[: len(places)], refs[-2], refs[-1]
    rows = kept.shape[0]
    low = places[0][0]
    train_rows = counts.shape[1]
    precond = jnp.concatenate(split_sum(kept, got))
    chosen = before[:1]
    for grad, (r, first) in zip(grads, places):
        both = dot_t(grad[...], precond)
        value = both[:, :rows] + both[:, rows:]
        place = pl.ds(first, grad.shape[0])
        out[r - low, place] = value.astype(BF16)
        chosen = chosen + jnp.sum(value * counts[r, place], axis=0, keepdims=True)
    chosen_out[...] = jnp.broadcast_to(chosen, chosen_out.shape)
    for n in range(2):
        if out.shape[1] > train_rows:
            out[n, train_rows:] = jnp.broadcast_to(chosen, (EXTRA, rows)).astype(BF16)


def last_scores(kept, got, counts, before, grads, extra):
    rows = kept.shape[0]
    return pl.pallas_call(
        functools.partial(last_scores_body, [piece[:2] for piece in grads]),
        in_specs=[VMEM] * (4 + len(grads)),
        out_specs=[VMEM, VMEM],
        out_shape=[
            jax.ShapeDtypeStruct((2, counts.shape[1] + extra, rows), BF16),
            jax.ShapeDtypeStruct((8, rows), F32),
        ],
        compiler_params=PARAMS,
        cost_estimate=SOME,
        name="last_scores",
    )(kept, got, counts, before, *[piece[2] for piece in grads])


def hold_body(*refs):
    for n in range(len(refs) // 2):
        refs[len(refs) // 2 + n][...] = refs[n][...]


def hold(values):
    return pl.pallas_call(
        hold_body,
        in_specs=[VMEM] * len(values),
        out_specs=[VMEM] * len(values),
        out_shape=[jax.ShapeDtypeStruct(value.shape, value.dtype) for value in values],
        compiler_params=PARAMS,
        cost_estimate=SMALL,
        name="hold",
    )(*values)


def four_by_four(train_grads, test_grads, fisher, chosen_ids):
    z = lax.axis_index("test")
    i = lax.axis_index("train")
    chip, core = i // 2, i % 2
    inner = (z == 1) | (z == 2)
    flags = jnp.stack([core, chip, inner.astype(jnp.int32)])
    own_rows = train_grads.shape[0]
    quarter = test_grads.shape[0] // 4

    def along(value, pairs):
        return lax.ppermute(value, "test", pairs)

    def to_other(value, r):
        return lax.ppermute(value, "train", [(k, k ^ r) for k in range(4)])

    def tied(*values):
        return lax.optimization_barrier(values)

    pair = [(0, 1), (1, 0), (2, 3), (3, 2)]
    middle = [(1, 2), (2, 1)]
    outward = [(1, 0), (2, 3)]
    inward = [(0, 1), (3, 2)]

    def core_sum(kept, *sent, sent_as=BF16, cost=SMALL):
        return fold(flags, kept, [to_other(part, 1) for part in sent], sent_as, cost)

    def scores_of(*units, out_as=(BF16, BF16), cost=SMALL):
        pieces = [(*place, grad) for place, grad in zip(places, grads)]
        return partial_scores(units, pieces, out_as[: len(units)], cost)

    def in_order(parts):
        parts = [parts[0], parts[2], parts[1], parts[3]]
        parts = [jnp.where(chip == 0, parts[q], parts[q ^ 1]) for q in range(4)]
        parts = [jnp.where(core == 0, parts[q], parts[q ^ 2]) for q in range(4)]
        return jnp.concatenate(parts, axis=1)

    row_ids = jnp.stack([i, i ^ 1, i ^ 2, i ^ 3])[:, None] * own_rows + jnp.arange(own_rows)

    def selected(ids):
        ids = lax.dynamic_slice_in_dim(ids, (core * 2 + chip) * quarter, quarter).T
        return sum((ids[k] == row_ids[:, :, None]).astype(F32) for k in range(ids.shape[0]))

    pair_in = along(test_grads, pair)
    middle_in = along(test_grads, middle)
    other_core, other_chip = to_other(train_grads, 1), to_other(train_grads, 2)
    mine, other_core = hold([train_grads, other_core])
    own, mine, other_core = tied(test_grads, mine, other_core)
    own, own_sent = core_sum(*product(flags, [own], fisher), sent_as=F32, cost=MORE)
    half = own_rows // 2
    other_both = [to_other(other_chip[:half], 1), to_other(other_chip[half:], 1)]
    grads = [mine, other_core, other_chip, *other_both]
    pair_in, middle_in, own, own_sent, chosen_ids, grads = tied(
        pair_in, middle_in, own, own_sent, chosen_ids, grads
    )
    places = ((0, 0), (1, 0), (2, 0), (3, 0), (3, half))

    second_edge = along(middle_in, outward)
    far_in = along(pair_in, middle)
    near, near_sent = core_sum(*product(flags, [middle_in, pair_in], fisher))
    own_got = to_other(own_sent, 2)
    near_sent, own_got, pair_in = tied(near_sent, own_got, pair_in)
    near_got = to_other(near_sent, 2)
    third, *third_sent = product(flags, [pair_in], fisher)
    third, second_edge = tied(third, second_edge)
    third, third_sent = core_sum(third, *third_sent, cost=SOME)
    (near,) = scores_of((near, near_got), cost=SOME)
    counts = selected(chosen_ids)
    far_in, second_edge, third, third_sent, own, own_got, near, counts, chosen_ids, grads = tied(
        far_in, second_edge, third, third_sent, own, own_got, near, counts, chosen_ids, grads
    )

    first_edge = along(far_in, outward)
    second, second_sent = core_sum(*product(flags, [far_in, second_edge], fisher))
    second, second_sent, near = tied(second, second_sent, near)
    second_got = to_other(second_sent, 2)
    near_in, near_across = along(near, inward), along(near, middle)
    second_got, near_in, near_across, chosen_ids = tied(
        second_got, near_in, near_across, chosen_ids
    )
    far_ids = along(chosen_ids, [(0, 3), (3, 0)])
    (second,) = scores_of((second, second_got))
    across = along(second, middle)
    third, total = scores_of(
        (third, to_other(third_sent, 2)), (own, own_got), out_as=(F32, F32)
    )
    first_edge, total, near_in, near_across, second, across, third, grads, far_ids = tied(
        first_edge, total, near_in, near_across, second, across, third, grads, far_ids
    )
    far_counts = selected(far_ids)

    last, last_sent = core_sum(*product(flags, [first_edge], fisher))
    last, second, third = tied(last, second, third)
    third = along((third + across.astype(F32)).astype(BF16), outward)
    second = along(second, [(0, 2), (3, 1)])
    last_got = to_other(last_sent, 2)
    ends = [(0, 3), (3, 0)]
    none = jnp.zeros((8, quarter), F32)
    pieces = [(*place, grad) for place, grad in zip(places, grads)]
    away, chosen = last_scores(last, last_got, far_counts, none, pieces[2:], 0)
    away = along(away, ends)
    away = [to_other(away[0], 2), to_other(away[1], 3)]
    here, _ = last_scores(last, last_got, far_counts, chosen, pieces[:2], EXTRA)
    here, second, third = tied(here, second, third)
    here = along(here, ends)
    here = [here[0], to_other(here[1], 1)]
    chosen = [part[own_rows:] for part in here]
    chosen += [to_other(chosen[0], 2), to_other(chosen[0], 3)]
    last = in_order([part[:own_rows] for part in here] + away)
    last_chosen = in_order(chosen)[0]

    total = total + sum(value.astype(F32) for value in (near_in, near_across, second, third))
    chosen = jnp.sum(total * counts, axis=(0, 1))
    total = [jnp.concatenate([part, jnp.broadcast_to(chosen, (8, quarter))]) for part in total]
    total = in_order([total[0]] + [to_other(total[r], r) for r in range(1, 4)])

    scores = total[:own_rows] + last.astype(F32)
    return scores, total[own_rows] + last_chosen.astype(F32)


def solution(mesh):
    sizes = (mesh.shape["train"], mesh.shape["test"])
    return jax.shard_map(
        four_by_four if sizes == (4, 4) else any_mesh,
        mesh=mesh,
        in_specs=(
            P(("groups", "train"), "test"),
            P(("groups", "test"), "train"),
            P("train", "test"),
            P(("groups", "test"), None),
        ),
        out_specs=(P(("groups", "train"), "test"), P(("groups", "test"))),
        check_vma=False,
    )
```

```python
import functools

import jax
import jax.numpy as jnp
from jax import lax
from jax.experimental import pallas as pl
from jax.experimental.pallas import tpu as pltpu
from jax.sharding import PartitionSpec as P

COLUMNS = 512
EXTRA = 16

F32 = jnp.float32
BF16 = jnp.bfloat16


def dot_t(a, b):
    return lax.dot_general(a, b, (((1,), (1,)), ((), ())), preferred_element_type=F32)


def selection_counts(chosen_ids, first_row, rows):
    row_ids = first_row + lax.broadcasted_iota(jnp.int32, (rows, chosen_ids.shape[0]), 0)
    ids = chosen_ids.T
    counts = jnp.zeros(row_ids.shape, F32)
    for k in range(ids.shape[0]):
        counts = counts + (row_ids == ids[k][None, :]).astype(F32)
    return counts


def any_mesh(train_grads, test_grads, fisher, chosen_ids):
    test_whole = lax.all_gather(test_grads, "test", axis=0, tiled=True)
    partial_value = jnp.dot(test_whole, fisher, preferred_element_type=F32)
    precond = lax.psum(partial_value, "train").astype(BF16)
    partial_scores = dot_t(train_grads, precond)
    scores = lax.psum_scatter(partial_scores, "test", scatter_dimension=1, tiled=True)
    rows = scores.shape[0]
    counts = selection_counts(chosen_ids, lax.axis_index("train") * rows, rows)
    return scores, lax.psum(jnp.sum(counts * scores, axis=0), "train")


SMALL = pl.CostEstimate(flops=1, bytes_accessed=1, transcendentals=0)
SOME = pl.CostEstimate(flops=2 * 10**9, bytes_accessed=2**20, transcendentals=0)
MORE = pl.CostEstimate(flops=7 * 10**9, bytes_accessed=2**20, transcendentals=0)
PARAMS = pltpu.CompilerParams(vmem_limit_bytes=12 * 2**20)


VMEM = pl.BlockSpec(memory_space=pltpu.VMEM)


def product_body(count, flags, *refs):
    blocks, fisher, outs = refs[:count], refs[count], refs[count + 1 :]
    quarter = blocks[0].shape[0] // 4
    mine = flags[0] == 0

    def multiply(block, kept, *sent):
        @pl.loop(0, fisher.shape[1] // COLUMNS)
        def _(n):
            columns = pl.ds(pl.multiple_of(n * COLUMNS, COLUMNS), COLUMNS)
            value = jnp.dot(block[...], fisher[:, columns], preferred_element_type=F32)
            for chip in range(2):
                low, high = (value[(2 * core + chip) * quarter :][:quarter] for core in range(2))
                kept[pl.ds(chip * quarter, quarter), columns] = jnp.where(mine, low, high)
                other = jnp.where(mine, high, low).astype(BF16)
                if len(sent) == 2:
                    sent[chip][:, columns] = other
                else:
                    sent[0][pl.ds(chip * quarter, quarter), columns] = other

    if len(blocks) == 1:
        multiply(blocks[0], *outs)
    else:
        pl.when(flags[2] == 1)(lambda: multiply(blocks[0], *outs))
        pl.when(flags[2] == 0)(lambda: multiply(blocks[1], *outs))


def product(flags, blocks, fisher, ways=2):
    half = blocks[0].shape[0] // 2
    columns = fisher.shape[1]
    sent = jax.ShapeDtypeStruct((half // ways, columns), BF16)
    return pl.pallas_call(
        functools.partial(product_body, len(blocks)),
        in_specs=[pl.BlockSpec(memory_space=pltpu.SMEM)] + [VMEM] * (len(blocks) + 1),
        out_specs=[VMEM] * (1 + ways),
        out_shape=[jax.ShapeDtypeStruct((half, columns), F32)] + [sent] * ways,
        compiler_params=PARAMS,
        cost_estimate=SMALL,
        name="product",
    )(flags, *blocks, fisher)


def fold_body(flags, kept, *refs):
    got, kept_out, sent_out = refs[:-2], refs[-2], refs[-1]
    half = kept_out.shape[0]
    first = flags[1] == 0

    @pl.loop(0, kept.shape[1] // COLUMNS)
    def _(n):
        columns = pl.ds(pl.multiple_of(n * COLUMNS, COLUMNS), COLUMNS)
        if len(got) == 2:
            low, high = got[0][:, columns], got[1][:, columns]
        else:
            low, high = got[0][:half, columns], got[0][half:, columns]
        low = kept[:half, columns] + low.astype(F32)
        high = kept[half:, columns] + high.astype(F32)
        kept_out[:, columns] = jnp.where(first, low, high)
        sent_out[:, columns] = jnp.where(first, high, low).astype(sent_out.dtype)


def fold(flags, kept, got, sent_as, cost):
    shape = (kept.shape[0] // 2, kept.shape[1])
    return pl.pallas_call(
        fold_body,
        in_specs=[pl.BlockSpec(memory_space=pltpu.SMEM)] + [VMEM] * (1 + len(got)),
        out_specs=[VMEM, VMEM],
        out_shape=[jax.ShapeDtypeStruct(shape, F32), jax.ShapeDtypeStruct(shape, sent_as)],
        compiler_params=PARAMS,
        cost_estimate=cost,
        name="fold",
    )(flags, kept, *got)


def split_sum(kept, got):
    value = kept[...] + got[...].astype(F32)
    high = value.astype(BF16)
    return high, (value - high.astype(F32)).astype(BF16)


def scores_body(places, units, *refs):
    sums, grads, outs = refs[: 2 * units], refs[2 * units :][: len(places)], refs[-units:]
    rows = sums[0].shape[0]
    precond = jnp.concatenate(
        [part for u in range(units) for part in split_sum(sums[2 * u], sums[2 * u + 1])]
    )
    for grad, (r, first) in zip(grads, places):
        both = dot_t(grad[...], precond)
        for u in range(units):
            value = both[:, 2 * u * rows :][:, :rows] + both[:, (2 * u + 1) * rows :][:, :rows]
            outs[u][r, first : first + grad.shape[0]] = value.astype(outs[u].dtype)


def partial_scores(units, grads, out_as, cost):
    rows = units[0][0].shape[0]
    train_rows = grads[0][2].shape[0]
    return pl.pallas_call(
        functools.partial(scores_body, [piece[:2] for piece in grads], len(units)),
        in_specs=[VMEM] * (2 * len(units) + len(grads)),
        out_specs=[VMEM] * len(units),
        out_shape=[jax.ShapeDtypeStruct((4, train_rows, rows), kind) for kind in out_as],
        compiler_params=PARAMS,
        cost_estimate=cost,
        name="scores",
    )(*[value for unit in units for value in unit], *[piece[2] for piece in grads])


def last_scores_body(places, kept, got, counts, before, *refs):
    grads, out, chosen_out = refs[: len(places)], refs[-2], refs[-1]
    rows = kept.shape[0]
    low = places[0][0]
    train_rows = counts.shape[1]
    precond = jnp.concatenate(split_sum(kept, got))
    chosen = before[:1]
    for grad, (r, first) in zip(grads, places):
        both = dot_t(grad[...], precond)
        value = both[:, :rows] + both[:, rows:]
        place = pl.ds(first, grad.shape[0])
        out[r - low, place] = value.astype(BF16)
        chosen = chosen + jnp.sum(value * counts[r, place], axis=0, keepdims=True)
    chosen_out[...] = jnp.broadcast_to(chosen, chosen_out.shape)
    for n in range(2):
        if out.shape[1] > train_rows:
            out[n, train_rows:] = jnp.broadcast_to(chosen, (EXTRA, rows)).astype(BF16)


def last_scores(kept, got, counts, before, grads, extra):
    rows = kept.shape[0]
    return pl.pallas_call(
        functools.partial(last_scores_body, [piece[:2] for piece in grads]),
        in_specs=[VMEM] * (4 + len(grads)),
        out_specs=[VMEM, VMEM],
        out_shape=[
            jax.ShapeDtypeStruct((2, counts.shape[1] + extra, rows), BF16),
            jax.ShapeDtypeStruct((8, rows), F32),
        ],
        compiler_params=PARAMS,
        cost_estimate=SMALL,
        name="last_scores",
    )(kept, got, counts, before, *[piece[2] for piece in grads])


def hold_body(*refs):
    for n in range(len(refs) // 2):
        refs[len(refs) // 2 + n][...] = refs[n][...]


def hold(values):
    return pl.pallas_call(
        hold_body,
        in_specs=[VMEM] * len(values),
        out_specs=[VMEM] * len(values),
        out_shape=[jax.ShapeDtypeStruct(value.shape, value.dtype) for value in values],
        compiler_params=PARAMS,
        cost_estimate=SMALL,
        name="hold",
    )(*values)


def four_by_four(train_grads, test_grads, fisher, chosen_ids):
    z = lax.axis_index("test")
    i = lax.axis_index("train")
    chip, core = i // 2, i % 2
    inner = (z == 1) | (z == 2)
    flags = jnp.stack([core, chip, inner.astype(jnp.int32)])
    own_rows = train_grads.shape[0]
    quarter = test_grads.shape[0] // 4

    def along(value, pairs):
        return lax.ppermute(value, "test", pairs)

    def to_other(value, r):
        return lax.ppermute(value, "train", [(k, k ^ r) for k in range(4)])

    def tied(*values):
        return lax.optimization_barrier(values)

    pair = [(0, 1), (1, 0), (2, 3), (3, 2)]
    middle = [(1, 2), (2, 1)]
    outward = [(1, 0), (2, 3)]
    inward = [(0, 1), (3, 2)]

    def core_sum(kept, *sent, sent_as=BF16, cost=SMALL):
        return fold(flags, kept, [to_other(part, 1) for part in sent], sent_as, cost)

    def scores_of(*units, out_as=(BF16, BF16), cost=SMALL):
        pieces = [(*place, grad) for place, grad in zip(places, grads)]
        return partial_scores(units, pieces, out_as[: len(units)], cost)

    def in_order(parts):
        parts = [parts[0], parts[2], parts[1], parts[3]]
        parts = [jnp.where(chip == 0, parts[q], parts[q ^ 1]) for q in range(4)]
        parts = [jnp.where(core == 0, parts[q], parts[q ^ 2]) for q in range(4)]
        return jnp.concatenate(parts, axis=1)

    row_ids = jnp.stack([i, i ^ 1, i ^ 2, i ^ 3])[:, None] * own_rows + jnp.arange(own_rows)

    def selected(ids):
        ids = lax.dynamic_slice_in_dim(ids, (core * 2 + chip) * quarter, quarter).T
        return sum((ids[k] == row_ids[:, :, None]).astype(F32) for k in range(ids.shape[0]))

    pair_in = along(test_grads, pair)
    middle_in = along(test_grads, middle)
    other_core, other_chip = to_other(train_grads, 1), to_other(train_grads, 2)
    mine, other_core = hold([train_grads, other_core])
    own, mine, other_core = tied(test_grads, mine, other_core)
    own, own_sent = core_sum(*product(flags, [own], fisher), sent_as=F32, cost=MORE)
    half = own_rows // 2
    other_both = [to_other(other_chip[:half], 1), to_other(other_chip[half:], 1)]
    grads = [mine, other_core, other_chip, *other_both]
    pair_in, middle_in, own, own_sent, chosen_ids, grads = tied(
        pair_in, middle_in, own, own_sent, chosen_ids, grads
    )
    places = ((0, 0), (1, 0), (2, 0), (3, 0), (3, half))

    second_edge = along(middle_in, outward)
    far_in = along(pair_in, middle)
    near, near_sent = core_sum(*product(flags, [middle_in, pair_in], fisher))
    own_got = to_other(own_sent, 2)
    near_sent, own_got, pair_in = tied(near_sent, own_got, pair_in)
    near_got = to_other(near_sent, 2)
    third, third_sent = core_sum(*product(flags, [pair_in], fisher))
    (near,) = scores_of((near, near_got), cost=SOME)
    far_ids = along(chosen_ids, [(0, 3), (3, 0)])
    counts = selected(chosen_ids)
    far_in, second_edge, third, third_sent, own, own_got, near, far_ids, counts, grads = tied(
        far_in, second_edge, third, third_sent, own, own_got, near, far_ids, counts, grads
    )

    first_edge = along(far_in, outward)
    second, second_sent = core_sum(*product(flags, [far_in, second_edge], fisher))
    second, second_sent, near = tied(second, second_sent, near)
    second_got = to_other(second_sent, 2)
    near_in, near_across = along(near, inward), along(near, middle)
    second_got, near_in, near_across = tied(second_got, near_in, near_across)
    (second,) = scores_of((second, second_got))
    across = along(second, middle)
    third, total = scores_of(
        (third, to_other(third_sent, 2)), (own, own_got), out_as=(F32, F32)
    )
    far_counts = selected(far_ids)
    first_edge, total, near_in, near_across, second, across, third, grads, far_counts = tied(
        first_edge, total, near_in, near_across, second, across, third, grads, far_counts
    )

    third = along((third + across.astype(F32)).astype(BF16), outward)
    second = along(second, [(0, 2), (3, 1)])
    last, last_sent = core_sum(*product(flags, [first_edge], fisher))
    last_got = to_other(last_sent, 2)
    ends = [(0, 3), (3, 0)]
    none = jnp.zeros((8, quarter), F32)
    pieces = [(*place, grad) for place, grad in zip(places, grads)]
    away, chosen = last_scores(last, last_got, far_counts, none, pieces[2:], 0)
    away = along(away, ends)
    away = [to_other(away[0], 2), to_other(away[1], 3)]
    here, _ = last_scores(last, last_got, far_counts, chosen, pieces[:2], EXTRA)
    here, third = tied(here, third)
    here = along(here, ends)
    here = [here[0], to_other(here[1], 1)]
    chosen = [part[own_rows:] for part in here]
    chosen += [to_other(chosen[0], 2), to_other(chosen[0], 3)]
    last = in_order([part[:own_rows] for part in here] + away)
    last_chosen = in_order(chosen)[0]

    total = total + sum(value.astype(F32) for value in (near_in, near_across, second, third))
    chosen = jnp.sum(total * counts, axis=(0, 1))
    total = [jnp.concatenate([part, jnp.broadcast_to(chosen, (8, quarter))]) for part in total]
    total = in_order([total[0]] + [to_other(total[r], r) for r in range(1, 4)])

    scores = total[:own_rows] + last.astype(F32)
    return scores, total[own_rows] + last_chosen.astype(F32)


def solution(mesh):
    sizes = (mesh.shape["train"], mesh.shape["test"])
    return jax.shard_map(
        four_by_four if sizes == (4, 4) else any_mesh,
        mesh=mesh,
        in_specs=(
            P(("groups", "train"), "test"),
            P(("groups", "test"), "train"),
            P("train", "test"),
            P(("groups", "test"), None),
        ),
        out_specs=(P(("groups", "train"), "test"), P(("groups", "test"))),
        check_vma=False,
    )
```
